32 devices in a mesh: dp: 8 (over y, x, core), tensor: 4 (over z).
Axes of the slice: x: 2, y: 2, z: 4, core: 2. Of those that a mesh axis runs over, the one named last changes fastest.
Arguments:
- inputs: bfloat16 [8, 1024, 2048], P('dp', 'tensor'), may hold values from -6 to 6
- cotangent: bfloat16 [8, 1024, 2048], P('dp', 'tensor'), may hold values from -6 to 6
- seg_ids: int32 [8, 1024], P('dp'), may hold values from 0 to 127, as said below
- norm_gains: bfloat16 [1, 2, 2048], P(None, None, ('dp', 'tensor')), may hold values from 0.5 to 1.5
- w_q: bfloat16 [1, 2048, 1024], P(None, 'dp', 'tensor'), may hold values from -0.125 to 0.125
- key_value_weight: bfloat16 [1, 2048, 512], P(None, ('dp', 'tensor')), may hold values from -0.125 to 0.125
- w_zx: bfloat16 [1, 2048, 2, 3072], P(None, 'dp', None, 'tensor'), may hold values from -0.125 to 0.125
- w_bc: bfloat16 [1, 2048, 512], P(None, ('dp', 'tensor')), may hold values from -0.125 to 0.125
- w_dt: bfloat16 [1, 2048, 48], P(None, 'dp', 'tensor'), may hold values from -0.125 to 0.125
- a_log: float32 [1, 48], P(None, 'tensor'), may hold values from 0 to 2.5
- dt_bias: float32 [1, 48], P(None, 'tensor'), may hold values from -9 to -3
- d_skip: float32 [1, 48], P(None, 'tensor'), may hold values from 0.5 to 1.5
- conv_x: float32 [1, 4, 3072], P(None, None, 'tensor'), may hold values from -3 to 3
- conv_bc: bfloat16 [1, 4, 512], P(None, None, ('dp', 'tensor')), may hold values from -3 to 3
- m_gain: float32 [1, 3072], P(None, 'tensor'), may hold values from 0.5 to 1.5
- w_ao: bfloat16 [1, 1024, 2048], P(None, 'tensor', 'dp'), may hold values from -0.75 to 0.75
- w_mo: bfloat16 [1, 3072, 2048], P(None, 'tensor', 'dp'), may hold values from -0.109375 to 0.109375
- w_gu: bfloat16 [1, 2048, 2, 4096], P(None, 'dp', None, 'tensor'), may hold values from -0.125 to 0.125
- w_down: bfloat16 [1, 4096, 2048], P(None, 'tensor', 'dp'), may hold values from -0.09375 to 0.09375
Outputs:
- hidden_out: bfloat16 [8, 1024, 2048], P('dp', 'tensor')
- input_grad: float32 [8, 1024, 2048], P('dp', 'tensor')
- grad_norm_gains: float32 [1, 2, 2048], P(None, None, ('dp', 'tensor'))
- grad_w_q: float32 [1, 2048, 1024], P(None, 'dp', 'tensor')
- grad_w_kv: float32 [1, 2048, 512], P(None, ('dp', 'tensor'))
- grad_w_zx: float32 [1, 2048, 2, 3072], P(None, 'dp', None, 'tensor')
- grad_w_bc: float32 [1, 2048, 512], P(None, ('dp', 'tensor'))
- grad_w_dt: float32 [1, 2048, 48], P(None, 'dp', 'tensor')
- grad_a_log: float32 [1, 48], P(None, 'tensor')
- grad_dt_bias: float32 [1, 48], P(None, 'tensor')
- grad_d_skip: float32 [1, 48], P(None, 'tensor')
- grad_conv_x: float32 [1, 4, 3072], P(None, None, 'tensor')
- grad_conv_bc: float32 [1, 4, 512], P(None, None, ('dp', 'tensor'))
- grad_m_gain: float32 [1, 3072], P(None, 'tensor')
- grad_w_ao: float32 [1, 1024, 2048], P(None, 'tensor', 'dp')
- grad_w_mo: float32 [1, 3072, 2048], P(None, 'tensor', 'dp')
- grad_w_gu: float32 [1, 2048, 2, 4096], P(None, 'dp', None, 'tensor')
- grad_w_down: float32 [1, 4096, 2048], P(None, 'tensor', 'dp')
The draws below stay inside these ranges and needn't reach their ends.
Inputs may be any that keep to these rules, and one draw needn't show every extreme that they name: `seg_ids`: in each sequence the ids start at 0, never fall and rise by at most one from a position to the next. One document of each sequence begins at position 64 or earlier and ends at position 960 or later.
All inputs are finite; a program needn't handle non-finite values.
Results may differ from the reference program's by a relative error of at most 0.017.
Values may be sent and summed in bfloat16 or wider, within the bound.
No kernel may reach another device: no remote copies, remote signals or barrier semaphores. Data moves between devices by JAX's collectives and lax.ppermute only.
A program may use at most 320 MiB of HBM per device.

```python
import jax
import jax.numpy as jnp
from jax import lax

MODEL_WIDTH = 2048
QUERY_HEADS = 8
KEY_VALUE_HEADS = 2
HEAD_SIZE = 128
HM = 48
P_SIZE = 64
NS = 256
FF = 4096
CONV = 4
LAYER_COUNT = 1
LEN = 1024
SEQS = 8


def draw_seg_ids(key, part):
    key = jax.random.fold_in(key, 11)
    key_start, key_stop, key_rate, key_bits, key_pick = jax.random.split(key, 5)
    margin = LEN // 16
    chosen = jax.random.randint(key_pick, (), 0, SEQS)
    is_chosen = (jnp.arange(SEQS) == chosen)[:, None]
    starts = jax.random.randint(key_start, (SEQS, 1), 1, margin + 1)
    stops_at = jax.random.randint(key_stop, (SEQS, 1), LEN - margin, LEN)
    break_rate = jax.random.randint(key_rate, (SEQS, 1), 1, 9)
    starts = jnp.where(is_chosen, margin, starts)
    stops_at = jnp.where(is_chosen, LEN - margin, stops_at)
    break_rate = jnp.where(is_chosen, 64, break_rate)
    coin_draw = jax.random.randint(key_bits, (SEQS, LEN), 0, 64)
    positions = jnp.arange(LEN)[None, :]
    outside = (positions < starts) | (positions > stops_at)
    breaks = outside & (coin_draw < break_rate) | (positions == starts) | (positions == stops_at + 1)
    breaks = breaks & (positions > 0)
    return jnp.cumsum(breaks.astype(jnp.int32), axis=1).astype(jnp.int32)


def levels(key, shape, cuts, low, high):
    level = 1.0
    for position, blocks in cuts:
        draws = jax.random.uniform(jax.random.fold_in(jax.random.fold_in(key, 6), position), (blocks,), jnp.float32, low / len(cuts), high / len(cuts))
        level = level * jnp.repeat(jnp.exp(draws), shape[position] // blocks).reshape((-1,) + (1,) * (len(shape) - 1 - position))
    return level


def bell_draw(key, dims, spread, bound, shards=(), held_as=jnp.bfloat16):
    drawn = jax.random.normal(key, dims, jnp.float32) * spread
    if len(shards) > 0:
        drawn = levels(key, dims, shards, -0.22, 0.18) * drawn
    return jnp.clip(drawn, min=-bound, max=bound).astype(held_as)


def setup_inputs(seed: int = 0) -> dict:
    splits = jax.random.split(jax.random.key(seed), 20)
    inputs = bell_draw(splits[0], (SEQS, LEN, MODEL_WIDTH), 1.0, 6.0, ((0, 8), (1, 4)))
    cotangent = bell_draw(splits[1], (SEQS, LEN, MODEL_WIDTH), 1.0, 6.0, ((0, 8), (1, 4)))
    seg_ids = draw_seg_ids(jax.random.fold_in(splits[19], 71), 0)
    norm_gains = jnp.clip(1.0 + 0.1 * jax.random.normal(splits[3], (LAYER_COUNT, 2, MODEL_WIDTH), jnp.float32), 0.5, 1.5).astype(jnp.bfloat16)
    w_q = bell_draw(splits[4], (LAYER_COUNT, MODEL_WIDTH, QUERY_HEADS * HEAD_SIZE), MODEL_WIDTH ** -0.5, 0.125, ((1, 8), (2, 4)))
    key_value_weight = bell_draw(splits[5], (LAYER_COUNT, MODEL_WIDTH, 2 * KEY_VALUE_HEADS * HEAD_SIZE), MODEL_WIDTH ** -0.5, 0.125, ((1, 32),))
    w_zx = bell_draw(splits[6], (LAYER_COUNT, MODEL_WIDTH, 2, HM * P_SIZE), MODEL_WIDTH ** -0.5, 0.125, ((1, 8), (3, 4)))
    w_bc = bell_draw(splits[7], (LAYER_COUNT, MODEL_WIDTH, 2 * NS), MODEL_WIDTH ** -0.5, 0.125, ((1, 32),))
    w_dt = bell_draw(splits[8], (LAYER_COUNT, MODEL_WIDTH, HM), MODEL_WIDTH ** -0.5, 0.125, ((1, 8), (2, 4)))
    a_log = jnp.clip(2.5 * jax.random.uniform(splits[9], (LAYER_COUNT, HM), jnp.float32) ** levels(splits[9], (LAYER_COUNT, HM), ((1, 4),), -0.2, 0.2), 0.0, 2.5)
    dt_bias = jnp.clip(-9.0 + 6.0 * jax.random.uniform(splits[10], (LAYER_COUNT, HM), jnp.float32) ** levels(splits[10], (LAYER_COUNT, HM), ((1, 4),), -0.2, 0.2), -9.0, -3.0)
    d_skip = jnp.clip(0.5 + 1.0 * jax.random.uniform(splits[11], (LAYER_COUNT, HM), jnp.float32) ** levels(splits[11], (LAYER_COUNT, HM), ((1, 4),), -0.2, 0.2), 0.5, 1.5)
    conv_x = bell_draw(splits[12], (LAYER_COUNT, CONV, HM * P_SIZE), CONV ** -0.5, 3.0, ((2, 4),), jnp.float32)
    conv_bc = bell_draw(splits[13], (LAYER_COUNT, CONV, 2 * NS), CONV ** -0.5, 3.0, ((2, 32),))
    m_gain = jnp.clip(1.0 + 0.1 * jax.random.normal(splits[14], (LAYER_COUNT, HM * P_SIZE), jnp.float32), 0.5, 1.5)
    w_ao = bell_draw(splits[15], (LAYER_COUNT, QUERY_HEADS * HEAD_SIZE, MODEL_WIDTH), (QUERY_HEADS * HEAD_SIZE // 16) ** -0.5, 0.75, ((1, 4), (2, 8)))
    w_mo = bell_draw(splits[16], (LAYER_COUNT, HM * P_SIZE, MODEL_WIDTH), (HM * P_SIZE) ** -0.5, 0.109375, ((1, 4), (2, 8)))
    w_gu = bell_draw(splits[17], (LAYER_COUNT, MODEL_WIDTH, 2, FF), MODEL_WIDTH ** -0.5, 0.125, ((1, 8), (3, 4)))
    w_down = bell_draw(splits[18], (LAYER_COUNT, FF, MODEL_WIDTH), FF ** -0.5, 0.09375, ((1, 4), (2, 8)))
    return dict(inputs=inputs, cotangent=cotangent, seg_ids=seg_ids, norm_gains=norm_gains, w_q=w_q, key_value_weight=key_value_weight, w_zx=w_zx, w_bc=w_bc, w_dt=w_dt, a_log=a_log, dt_bias=dt_bias, d_skip=d_skip, conv_x=conv_x, conv_bc=conv_bc, m_gain=m_gain, w_ao=w_ao, w_mo=w_mo, w_gu=w_gu, w_down=w_down)


NORM_EPS = 1e-05
ROPE_BASE = 100000000000.0
MASK_FILL = -1e+30
HIGHEST = lax.Precision.HIGHEST

@jax.custom_vjp
def lower_precision(v):
    return lax.optimization_barrier(v.astype(jnp.bfloat16)).astype(jnp.float32)

@jax.custom_vjp
def low_back(v):
    return v

def low_keep(v):
    return (lower_precision(v), None)

def low_pass(kept, grad):
    return (grad,)

def back_keep(v):
    return (v, None)

def back_low(kept, grad):
    return (lower_precision(grad),)
lower_precision.defvjp(low_keep, low_pass)
low_back.defvjp(back_keep, back_low)

def matmul_hi(left, right):
    return jnp.dot(left, right, precision=HIGHEST)

def rms_factor(hidden):
    return lax.rsqrt(lax.optimization_barrier(jnp.mean(hidden * hidden, axis=-1, keepdims=True)) + NORM_EPS)

def rotary_tables(length_total, head_dim):
    positions = jnp.arange(length_total).astype(jnp.float32)
    freqs = ROPE_BASE ** (-jnp.arange(0, head_dim // 2).astype(jnp.float32) * 2.0 / head_dim)
    angles = positions[:, None] * freqs[None, :]
    return (jnp.cos(angles)[:, None, :], jnp.sin(angles)[:, None, :])

def apply_rotation(values, cosine_table, sine_table):
    half_dim = values.shape[-1] // 2
    front_half = values[..., :half_dim]
    back_half = values[..., half_dim:]
    return jnp.concatenate([front_half * cosine_table - back_half * sine_table, back_half * cosine_table + front_half * sine_table], axis=-1)

def doc_conv(signal, kernel, segment):
    length_total = signal.shape[0]
    taps = kernel.shape[0]
    summed = jnp.zeros(signal.shape, jnp.float32)
    for tap_index in range(taps):
        offset = taps - 1 - tap_index
        shifted = jnp.pad(signal, ((offset, 0), (0, 0)))[:length_total]
        seg_shift = jnp.pad(segment, (offset, 0), constant_values=-1)[:length_total]
        summed = summed + kernel[tap_index] * shifted * (seg_shift == segment)[:, None]
    return jax.nn.silu(summed)

def ssd_block(carried, pieces):
    inputs_x, keys_b, query_c, log_decay, step_size, segment, prior_seg = pieces
    block_len = segment.shape[0]
    cumulative = jnp.cumsum(log_decay, axis=0)
    order_idx = jnp.arange(block_len)
    within = (segment[:, None] == segment[None, :]) & (order_idx[:, None] >= order_idx[None, :])
    mask_three = within[:, :, None]
    gap_logs = cumulative[:, None, :] - cumulative[None, :, :]
    decays = jnp.where(mask_three, jnp.exp(jnp.where(mask_three, gap_logs, 0.0)), 0.0)
    c_dot_b = jnp.dot(query_c, keys_b.T, precision=HIGHEST)
    scaled_x = inputs_x * step_size[:, :, None]
    local_y = jnp.einsum('ijh,jhp->ihp', decays * c_dot_b[:, :, None], scaled_x, precision=HIGHEST)
    entering = jnp.exp(cumulative) * (segment == prior_seg)[:, None]
    carried_y = jnp.einsum('in,hpn->ihp', query_c, carried, precision=HIGHEST) * entering[:, :, None]
    last_seg = segment[-1]
    leaving = jnp.exp(cumulative[-1][None, :] - cumulative) * (segment == last_seg)[:, None]
    keep_scale = jnp.exp(cumulative[-1]) * (last_seg == prior_seg)
    updated = carried * keep_scale[:, None, None] + jnp.einsum('jh,jhp,jn->hpn', leaving, scaled_x, keys_b, precision=HIGHEST)
    return (updated, local_y + carried_y)

def ssd_scan(x_conv, keys_b, query_c, log_decay, step_size, segment):
    length_total, head_count, head_dim = x_conv.shape
    block_len = min(128, length_total)
    blocks = length_total // block_len
    prior_seg = jnp.concatenate([jnp.full((1,), -1, jnp.int32), segment[block_len - 1:length_total - 1:block_len].astype(jnp.int32)])

    def by_blocks(array_in):
        return array_in.reshape((blocks, block_len) + array_in.shape[1:])
    initial = jnp.zeros((head_count, head_dim, keys_b.shape[1]), jnp.float32)
    _, outputs = lax.scan(jax.checkpoint(ssd_block), initial, (by_blocks(x_conv), by_blocks(keys_b), by_blocks(query_c), by_blocks(log_decay), by_blocks(step_size), by_blocks(segment.astype(jnp.int32)), prior_seg))
    return outputs.reshape(length_total, head_count, head_dim)

def mamba_core(x_raw, bc_raw, dt_raw, a_log, dt_bias, d_skip, conv_x, conv_bc, segment):
    length_total, head_count = dt_raw.shape
    x_conv = doc_conv(x_raw, conv_x, segment).reshape(length_total, head_count, -1)
    bc_conv = doc_conv(bc_raw, conv_bc, segment)
    states = bc_conv.shape[1] // 2
    step_size = jax.nn.softplus(dt_raw + dt_bias)
    log_decay = -step_size * jnp.exp(a_log)
    output = ssd_scan(x_conv, bc_conv[:, :states], bc_conv[:, states:], log_decay, step_size, segment)
    return (output + d_skip[None, :, None] * x_conv).reshape(length_total, -1)

def layer_forward(hidden, segment, weights, cosine_table, sine_table):
    gain_pair, query_w, keyval_w, zx_w, bc_w, dt_w, alog_v, dtbias_v, dskip_v, convx_w, convbc_w, mgain_v, attn_out_w, mamba_out_w, gateup_w, down_w = weights
    length_total = hidden.shape[0]
    normed = lower_precision(hidden * rms_factor(hidden) * gain_pair[0])
    q_proj = low_back(matmul_hi(normed, query_w)).reshape(length_total, QUERY_HEADS, HEAD_SIZE)
    queries = lower_precision(apply_rotation(q_proj, cosine_table, sine_table))
    key_value_projected = matmul_hi(normed, keyval_w)
    rotated_keys = lower_precision(apply_rotation(key_value_projected[:, :KEY_VALUE_HEADS * HEAD_SIZE].reshape(length_total, KEY_VALUE_HEADS, HEAD_SIZE), cosine_table, sine_table))
    value_rows = lower_precision(key_value_projected[:, KEY_VALUE_HEADS * HEAD_SIZE:].reshape(length_total, KEY_VALUE_HEADS, HEAD_SIZE))
    query_group_width = QUERY_HEADS // KEY_VALUE_HEADS
    rotated_keys = jnp.repeat(rotated_keys, query_group_width, axis=1)
    value_rows = jnp.repeat(value_rows, query_group_width, axis=1)
    scores = low_back(jnp.einsum('qhd,khd->hqk', queries, rotated_keys, precision=HIGHEST) * HEAD_SIZE ** (-0.5))
    order_idx = jnp.arange(length_total)
    allowed = (order_idx[:, None] >= order_idx[None, :]) & (segment[:, None] == segment[None, :])
    prob_low = lower_precision(jax.nn.softmax(jnp.where(allowed[None], scores, MASK_FILL), axis=-1))
    attended = low_back(lower_precision(jnp.einsum('hqk,khd->qhd', prob_low, value_rows, precision=HIGHEST)))
    attn_part = matmul_hi(attended.reshape(length_total, QUERY_HEADS * HEAD_SIZE), attn_out_w)
    zx_proj = low_back(jnp.einsum('td,dkc->tkc', normed, zx_w, precision=HIGHEST))
    bc_raw = matmul_hi(normed, bc_w)
    dt_raw = matmul_hi(normed, dt_w)
    y_out = mamba_core(zx_proj[:, 1], bc_raw, dt_raw, alog_v, dtbias_v, dskip_v, convx_w, convbc_w, segment)
    gated = y_out * jax.nn.silu(zx_proj[:, 0])
    rstd = lax.rsqrt(lax.optimization_barrier(jnp.mean(gated * gated, axis=-1, keepdims=True)) + NORM_EPS)
    mixed = lower_precision(gated * rstd * mgain_v)
    branch = low_back(attn_part + matmul_hi(mixed, mamba_out_w))
    hidden = hidden + branch
    normed2 = lower_precision(hidden * rms_factor(hidden) * gain_pair[1])
    gate_up = low_back(jnp.einsum('td,dkf->tkf', normed2, gateup_w, precision=HIGHEST))
    act = lower_precision(jax.nn.silu(gate_up[:, 0]) * gate_up[:, 1])
    return hidden + low_back(matmul_hi(act, down_w))

def reference(inputs, cotangent, seg_ids, norm_gains, w_q, key_value_weight, w_zx, w_bc, w_dt, a_log, dt_bias, d_skip, conv_x, conv_bc, m_gain, w_ao, w_mo, w_gu, w_down):
    params = tuple((member.astype(jnp.float32) for member in (norm_gains, w_q, key_value_weight, w_zx, w_bc, w_dt, a_log, dt_bias, d_skip, conv_x, conv_bc, m_gain, w_ao, w_mo, w_gu, w_down)))
    cosine_table, sine_table = rotary_tables(LEN, HEAD_SIZE)

    def one_sequence(running, pieces):
        tokens, grad_out, segment = pieces

        def forward(hidden, weights):
            for layer_index in range(LAYER_COUNT):
                hidden = layer_forward(hidden, segment, tuple((member[layer_index] for member in weights)), cosine_table, sine_table)
            return hidden
        result, pullback = jax.vjp(forward, tokens.astype(jnp.float32), params)
        d_tokens, d_params = pullback(grad_out.astype(jnp.float32))
        return (jax.tree.map(jnp.add, running, d_params), (result, d_tokens))
    zeros_init = jax.tree.map(jnp.zeros_like, params)
    grad_sums, (results, d_inputs) = lax.scan(one_sequence, zeros_init, (inputs, cotangent, seg_ids))
    return (results.astype(jnp.bfloat16), d_inputs, grad_sums[0], grad_sums[1], grad_sums[2], grad_sums[3], grad_sums[4], grad_sums[5], grad_sums[6], grad_sums[7], grad_sums[8], grad_sums[9], grad_sums[10], grad_sums[11], grad_sums[12], grad_sums[13], grad_sums[14], grad_sums[15])
```

```python
from functools import partial

import jax
import jax.numpy as jnp
import numpy as np
from jax import lax
from jax.experimental import pallas as pl
from jax.experimental.pallas import tpu as pltpu
from jax.sharding import PartitionSpec as P

QUERY_HEADS = 8
KEY_VALUE_HEADS = 2
HEAD_SIZE = 128
HM = 48
P_SIZE = 64
LANES = 128
CHUNK = 128
NORM_EPS = 1e-05
ROPE_BASE = 100000000000.0
MASK_FILL = -1e30
F32 = jnp.float32
BF16 = jnp.bfloat16
NN = (((1,), (0,)), ((), ()))
NT = (((1,), (1,)), ((), ()))
TN = (((0,), (0,)), ((), ()))
VMEM_LIMIT = 48 * 1024 * 1024


def dot(left, right, dims=NN):
    return lax.dot_general(left, right, dims, preferred_element_type=F32)


def dot_exact(left, right):
    return lax.dot_general(
        left, right, NN, precision=lax.Precision.HIGHEST, preferred_element_type=F32
    )


def sigmoid(v):
    return 1.0 / (1.0 + jnp.exp(-v))


def send_dp(value, mask):
    size = lax.axis_size("dp")
    return lax.ppermute(value, "dp", [(i, i ^ mask) for i in range(size)])


def dp_gather(rows, *earlier):
    chips = lax.axis_size("dp") // 2
    if earlier:
        rows = after(rows, *earlier)
    mine = [rows] + [send_dp(rows, 2 * k) for k in range(1, chips)]
    mine = jnp.concatenate(mine, axis=0)
    return jnp.concatenate([mine, send_dp(mine, 1)], axis=0), mine


def dp_scatter(grad):
    chips = lax.axis_size("dp") // 2
    half = grad.shape[0] // 2
    block = half // chips
    other = send_dp(grad[half:], 1)
    pair = (grad[:half].astype(F32) + other.astype(F32)).astype(grad.dtype)
    total = pair[:block].astype(F32)
    for k in range(1, chips):
        total = total + send_dp(pair[k * block : (k + 1) * block], 2 * k).astype(F32)
    return total


def dp_sum(value):
    chips = lax.axis_size("dp") // 2
    value = value + send_dp(value, 1)
    total = value
    for k in range(1, chips):
        total = total + send_dp(value, 2 * k)
    return total


def send_z(value, shift):
    size = lax.axis_size("tensor")
    return lax.ppermute(value, "tensor", [(i, (i + shift) % size) for i in range(size)])


def z_gather_direct(rows):
    size = lax.axis_size("tensor")
    me = lax.axis_index("tensor")
    count = rows.shape[0]
    out = jnp.zeros((size * count,) + rows.shape[1:], rows.dtype)
    pieces = [rows] + [send_z(rows, k) for k in range(1, size)]
    for k, piece in enumerate(pieces):
        out = lax.dynamic_update_slice_in_dim(out, piece, lax.rem(me - k + size, size) * count, 0)
    return out


def z_scatter_direct(total):
    size = lax.axis_size("tensor")
    me = lax.axis_index("tensor")
    count = total.shape[0] // size
    mine = lax.dynamic_slice_in_dim(total, me * count, count, 0).astype(F32)
    for k in range(1, size):
        piece = lax.dynamic_slice_in_dim(total, lax.rem(me + k, size) * count, count, 0)
        mine = mine + send_z(piece, k).astype(F32)
    return mine


def z_gather(rows):
    size = lax.axis_size("tensor")
    me = lax.axis_index("tensor")
    count = rows.shape[0]
    from_left, from_right = [], []
    right = left = rows
    for s in range(size - 1):
        right = lax.ppermute(right, "tensor", [(i, i + 1) for i in range(s, size - 1)])
        left = lax.ppermute(left, "tensor", [(i, i - 1) for i in range(1, size - s)])
        from_left.append(right)
        from_right.append(left)
    out = jnp.zeros((size * count,) + rows.shape[1:], rows.dtype)
    out = lax.dynamic_update_slice_in_dim(out, rows, me * count, 0)
    for d in range(1, size):
        piece = from_left[d - 1] + from_right[size - d - 1]
        out = lax.dynamic_update_slice_in_dim(out, piece, lax.rem(me - d + size, size) * count, 0)
    return out


def z_scatter(total):
    size = lax.axis_size("tensor")
    me = lax.axis_index("tensor")
    count = total.shape[0] // size

    def part(offset):
        index = jnp.clip(me + offset, 0, size - 1)
        return lax.dynamic_slice_in_dim(total, index * count, count, 0)

    right = left = None
    for s in range(size - 1):
        d = size - 1 - s
        to_right, to_left = part(d), part(-d)
        if s:
            to_right = (to_right.astype(F32) + right.astype(F32)).astype(total.dtype)
            to_left = (to_left.astype(F32) + left.astype(F32)).astype(total.dtype)
        right = lax.ppermute(to_right, "tensor", [(i, i + 1) for i in range(s + 1)])
        left = lax.ppermute(to_left, "tensor", [(i, i - 1) for i in range(size - 1 - s, size)])
    return part(0).astype(F32) + right.astype(F32) + left.astype(F32)


def z_sum(value):
    size = lax.axis_size("tensor")
    total = value
    for k in range(1, size):
        total = total + send_z(value, k)
    return total


def block_order(j, chips):
    return 2 * lax.rem(j, chips) + lax.div(j, chips)


def place_of(mask, chips):
    return (mask & 1) * chips + lax.shift_right_logical(mask, 1)


def permute_kernel(me_ref, in_ref, out_ref):
    out_ref[...] = in_ref[...]


def permute_blocks(value, me, count, forward):
    chips = count // 2
    rows, width = value.shape
    block = width // count

    def source(j, me_ref):
        if forward:
            return (0, me_ref[0] ^ block_order(j, chips))
        return (0, place_of(me_ref[0] ^ j, chips))

    return pl.pallas_call(
        permute_kernel,
        grid_spec=pltpu.PrefetchScalarGridSpec(
            num_scalar_prefetch=1,
            grid=(count,),
            in_specs=[pl.BlockSpec((rows, block), source)],
            out_specs=pl.BlockSpec((rows, block), lambda j, me_ref: (0, j)),
        ),
        out_shape=jax.ShapeDtypeStruct(value.shape, value.dtype),
        cost_estimate=pl.CostEstimate(
            flops=0, bytes_accessed=2 * value.size * value.dtype.itemsize, transcendentals=0
        ),
        name="permute_blocks",
    )(me, value)


def norm_kernel(count, me_ref, x_ref, gain_ref, out_ref):
    chips = count // 2
    width = x_ref.shape[1]
    block = width // count
    x = x_ref[...].astype(F32)
    factor = lax.rsqrt(jnp.sum(x * x, axis=1, keepdims=True) * (1.0 / width) + NORM_EPS)
    for j in range(count):
        source = me_ref[0] ^ (2 * (j % chips) + j // chips)
        columns = pl.ds(pl.multiple_of(source * block, block), block)
        here = slice(j * block, (j + 1) * block)
        out = x_ref[:, columns].astype(F32) * factor * gain_ref[:, here]
        out_ref[:, here] = out.astype(BF16)


def norm_permuted(value, gain, me, count):
    rows, width = value.shape
    block = min(256, rows)
    return pl.pallas_call(
        partial(norm_kernel, count),
        grid_spec=pltpu.PrefetchScalarGridSpec(
            num_scalar_prefetch=1,
            grid=(rows // block,),
            in_specs=[
                pl.BlockSpec((block, width), lambda i, me_ref: (i, 0)),
                pl.BlockSpec((1, width), lambda i, me_ref: (0, 0)),
            ],
            out_specs=pl.BlockSpec((block, width), lambda i, me_ref: (i, 0)),
        ),
        out_shape=jax.ShapeDtypeStruct(value.shape, BF16),
        compiler_params=pltpu.CompilerParams(vmem_limit_bytes=VMEM_LIMIT),
        cost_estimate=pl.CostEstimate(
            flops=4 * value.size, bytes_accessed=4 * value.size, transcendentals=rows
        ),
        name="norm_permuted",
    )(me, value, gain)


def rotary_rows(length):
    half = HEAD_SIZE // 2
    freqs = np.float32(ROPE_BASE) ** (
        -np.arange(half).astype(np.float32) * np.float32(2.0) / np.float32(HEAD_SIZE)
    )
    angles = np.arange(length).astype(np.float32)[:, None] * freqs.astype(np.float32)[None, :]
    cosine, sine = np.cos(angles), np.sin(angles)
    return (
        np.concatenate([cosine, cosine], axis=1).astype(np.float32),
        np.concatenate([-sine, sine], axis=1).astype(np.float32),
    )


def rotate(value, cosine, sine):
    return value * cosine + pltpu.roll(value, HEAD_SIZE // 2, 1) * sine


def attention_probs(q_ref, keys, cos_ref, sin_ref, allowed, start, stop):
    query = rotate(q_ref[start:stop, :], cos_ref[start:stop, :], sin_ref[start:stop, :])
    query = query.astype(BF16)
    scores = dot(query, keys, NT) * (HEAD_SIZE**-0.5)
    scores = jnp.where(allowed, scores, MASK_FILL)
    raised = jnp.exp(scores - jnp.max(scores, axis=1, keepdims=True))
    return query, raised * (1.0 / jnp.sum(raised, axis=1, keepdims=True))


def attention_mask(aux_ref, segr_ref, start, stop):
    rows = start + lax.broadcasted_iota(jnp.int32, (stop - start, stop), 0)
    cols = lax.broadcasted_iota(jnp.int32, (stop - start, stop), 1)
    return (aux_ref[start:stop, 0:1] == segr_ref[0:1, :stop]) & (rows >= cols)


def attention_forward_kernel(heads, block, *refs):
    q_refs = refs[:heads]
    k_ref, v_ref, cos_ref, sin_ref, aux_ref, segr_ref, out_ref = refs[heads:]
    length = k_ref.shape[0]
    keys = rotate(k_ref[...], cos_ref[...], sin_ref[...]).astype(BF16)
    vals = v_ref[...].astype(BF16)
    for start in range(0, length, block):
        stop = start + block
        allowed = attention_mask(aux_ref, segr_ref, start, stop)
        for h in range(heads):
            _, probs = attention_probs(
                q_refs[h], keys[:stop], cos_ref, sin_ref, allowed, start, stop
            )
            out = dot(probs.astype(BF16), vals[:stop])
            out_ref[start:stop, h * HEAD_SIZE : (h + 1) * HEAD_SIZE] = out.astype(BF16)


def attention_backward_kernel(heads, block, *refs):
    q_refs = refs[:heads]
    k_ref, v_ref, cos_ref, sin_ref, aux_ref, segr_ref, do_ref, out_ref, dk, dv = refs[heads:]
    length = k_ref.shape[0]
    scale = HEAD_SIZE**-0.5
    keys = rotate(k_ref[...], cos_ref[...], sin_ref[...]).astype(BF16)
    vals = v_ref[...].astype(BF16)
    dk[...] = jnp.zeros_like(dk)
    dv[...] = jnp.zeros_like(dv)
    for start in range(0, length, block):
        stop = start + block
        allowed = attention_mask(aux_ref, segr_ref, start, stop)
        for h in range(heads):
            query, probs = attention_probs(
                q_refs[h], keys[:stop], cos_ref, sin_ref, allowed, start, stop
            )
            given = do_ref[start:stop, h * HEAD_SIZE : (h + 1) * HEAD_SIZE].astype(BF16)
            d_probs = dot(given, vals[:stop], NT)
            delta = jnp.sum(probs * d_probs, axis=1, keepdims=True)
            d_scores = (probs * (d_probs - delta)).astype(BF16)
            d_query = dot(d_scores, keys[:stop]) * scale
            d_query = rotate(d_query, cos_ref[start:stop, :], -sin_ref[start:stop, :])
            out_ref[start:stop, h * HEAD_SIZE : (h + 1) * HEAD_SIZE] = d_query.astype(BF16)
            dk[:stop, :] += dot(d_scores, query, TN)
            dv[:stop, :] += dot(probs.astype(BF16), given, TN)
    d_keys = rotate(dk[...] * scale, cos_ref[...], -sin_ref[...])
    out_ref[:, heads * HEAD_SIZE : (heads + 1) * HEAD_SIZE] = d_keys.astype(BF16)
    out_ref[:, (heads + 1) * HEAD_SIZE :] = dv[...].astype(BF16)


def attention_call(kernel, name, panel, first, heads, tables, aux, segr, extra, width, scratch):
    length = panel.shape[0]

    def column(index):
        return pl.BlockSpec((length, HEAD_SIZE), lambda i: (0, index))

    def whole(array):
        return pl.BlockSpec(array.shape, lambda i: (0, 0))

    specs = [column(first // HEAD_SIZE + h) for h in range(heads + 2)]
    operands = [*tables, aux, segr]
    specs += [whole(a) for a in operands]
    if extra is not None:
        specs.append(pl.BlockSpec((length, heads * HEAD_SIZE), lambda i: (0, 0)))
        operands.append(extra)
    return pl.pallas_call(
        partial(kernel, heads, min(256, length)),
        grid=(1,),
        in_specs=specs,
        out_specs=pl.BlockSpec((length, width), lambda i: (0, 0)),
        out_shape=jax.ShapeDtypeStruct((length, width), BF16),
        scratch_shapes=scratch,
        compiler_params=pltpu.CompilerParams(vmem_limit_bytes=VMEM_LIMIT),
        cost_estimate=pl.CostEstimate(
            flops=(16 if extra is not None else 8) * heads * length * length * HEAD_SIZE,
            bytes_accessed=4 * length * 12 * HEAD_SIZE,
            transcendentals=heads * length * length,
        ),
        name=name,
    )(*([panel] * (heads + 2)), *operands)


def split_pair(value):
    high = value.astype(BF16)
    return high, (value - high.astype(F32)).astype(BF16)


def widen(value, expand_ref):
    high, rest = split_pair(value)
    return dot(jnp.concatenate([high, rest], axis=1), expand_ref[...])


def by_head(value, reduce_ref):
    high, rest = split_pair(value)
    return dot(high, reduce_ref[...]) + dot(rest, reduce_ref[...])


def conv_rows(current, halo, pad, taps_ref, aux):
    rows = current.shape[0]
    pad[0:8, :] = halo
    pad[8 : 8 + rows, :] = current
    out = taps_ref[3:4, :] * current
    for k in range(1, 4):
        out = out + taps_ref[3 - k : 4 - k, :] * (pad[8 - k : 8 - k + rows, :] * aux[:, k : k + 1])
    return out


def head_scalars(dt_raw, par_ref, lower):
    biased = dt_raw + par_ref[1:2, :]
    step = jnp.maximum(biased, 0.0) + jnp.log1p(jnp.exp(-jnp.abs(biased)))
    log_decay = -step * jnp.exp(par_ref[0:1, :])
    cumulative = dot_exact(lower, log_decay)
    return biased, step, log_decay, cumulative


def triangle(rows, flip):
    i = lax.broadcasted_iota(jnp.int32, (rows, rows), 0)
    j = lax.broadcasted_iota(jnp.int32, (rows, rows), 1)
    return (i <= j) if flip else (i >= j)


def mamba_forward_kernel(
    cols,
    p_ref,
    halo_ref,
    aux_ref,
    segr_ref,
    cx_ref,
    cbc_ref,
    par_ref,
    dskip_ref,
    mgain_ref,
    expand_ref,
    gm_ref,
    sq_ref,
    y_ref,
    st_ref,
    state,
    pad_x,
    pad_bc,
):
    width, states = cols["width"], cols["states"]
    rows = p_ref.shape[0]
    x0, bc0, dt0 = cols["x"], cols["bc"], cols["dt"]

    @pl.when(pl.program_id(0) == 0)
    def _():
        state[...] = jnp.zeros_like(state)

    aux = aux_ref[...]
    u_x = conv_rows(
        p_ref[:, x0 : x0 + width], halo_ref[:, x0 : x0 + width], pad_x, cx_ref, aux
    )
    x_conv = u_x * sigmoid(u_x)
    u_bc = conv_rows(
        p_ref[:, bc0 : bc0 + 2 * states], halo_ref[:, bc0 : bc0 + 2 * states], pad_bc, cbc_ref, aux
    )
    bc = (u_bc * sigmoid(u_bc)).astype(BF16)
    keys, query = bc[:, :states], bc[:, states:]
    lower = triangle(rows, False)
    _, step, _, cum = head_scalars(p_ref[:, dt0 : dt0 + LANES], par_ref, lower.astype(F32))
    cum_t = cum.T
    last = cum[rows - 1 : rows, :]
    entering = jnp.exp(cum) * aux[:, 7:8]
    leaving = jnp.exp(last - cum) * aux[:, 8:9]
    wide = widen(jnp.concatenate([step, entering, leaving], axis=0), expand_ref)
    step_w, enter_w, leave_w = wide[:rows], wide[rows : 2 * rows], wide[2 * rows :]
    xs = x_conv * step_w
    xs_low = xs.astype(BF16)
    mask = lower & (aux[:, 0:1] == segr_ref[0:1, :])
    c_dot_b = dot(query, keys, NT)
    held = state[...]
    held_low = held.astype(BF16)
    st_ref[0] = held_low
    carried = dot(query, held_low) * enter_w
    lane = lax.broadcasted_iota(jnp.int32, (rows, LANES), 1)
    parts = []
    for pair in range(width // LANES):
        pair_x = xs_low[:, pair * LANES : (pair + 1) * LANES]
        sides = []
        for e in range(2):
            h = 2 * pair + e
            gap = cum[:, h : h + 1] - cum_t[h : h + 1, :]
            decay = jnp.exp(jnp.where(mask, gap, MASK_FILL))
            sides.append(dot((decay * c_dot_b).astype(BF16), pair_x))
        parts.append(jnp.where(lane < P_SIZE, sides[0], sides[1]))
    y = jnp.concatenate(parts, axis=1) + carried + dskip_ref[0:1, :] * x_conv
    state[...] = held * enter_w[rows - 1 : rows, :] + dot(
        keys, (leave_w * xs).astype(BF16), TN
    )
    z = p_ref[:, :width]
    gated = y * (z * sigmoid(z))
    y_ref[...] = y
    gm_ref[...] = (gated * mgain_ref[0:1, :]).astype(BF16)
    sq_ref[...] = jnp.broadcast_to(jnp.sum(gated * gated, axis=1, keepdims=True), sq_ref.shape)


def mamba_backward_kernel(
    cols,
    p_ref,
    halo_ref,
    aux_ref,
    segr_ref,
    cx_ref,
    cbc_ref,
    par_ref,
    dskip_ref,
    mgain_ref,
    expand_ref,
    reduce_ref,
    y_ref,
    st_ref,
    db_ref,
    aux2_ref,
    dqkv_ref,
    dp_ref,
    gw_ref,
    gcx_ref,
    gcbc_ref,
    gh_ref,
    d_state,
    pad_x,
    pad_bc,
    fut_x,
    fut_bc,
):
    width, states = cols["width"], cols["states"]
    rows = p_ref.shape[0]
    x0, q0, bc0, dt0 = cols["x"], cols["q"], cols["bc"], cols["dt"]
    first_step = pl.program_id(0) == 0

    @pl.when(first_step)
    def _():
        d_state[...] = jnp.zeros_like(d_state)
        gw_ref[...] = jnp.zeros_like(gw_ref)
        gcx_ref[...] = jnp.zeros_like(gcx_ref)
        gcbc_ref[...] = jnp.zeros_like(gcbc_ref)
        gh_ref[...] = jnp.zeros_like(gh_ref)
        fut_x[...] = jnp.zeros_like(fut_x)
        fut_bc[...] = jnp.zeros_like(fut_bc)

    aux = aux_ref[...]
    u_x = conv_rows(
        p_ref[:, x0 : x0 + width], halo_ref[:, x0 : x0 + width], pad_x, cx_ref, aux
    )
    sig_x = sigmoid(u_x)
    x_conv = u_x * sig_x
    u_bc = conv_rows(
        p_ref[:, bc0 : bc0 + 2 * states], halo_ref[:, bc0 : bc0 + 2 * states], pad_bc, cbc_ref, aux
    )
    sig_bc = sigmoid(u_bc)
    bc = (u_bc * sig_bc).astype(BF16)
    keys, query = bc[:, :states], bc[:, states:]
    lower = triangle(rows, False).astype(F32)
    biased, step, log_decay, cum = head_scalars(p_ref[:, dt0 : dt0 + LANES], par_ref, lower)
    cum_t = cum.T
    last = cum[rows - 1 : rows, :]
    entering = jnp.exp(cum) * aux[:, 7:8]
    leaving = jnp.exp(last - cum) * aux[:, 8:9]
    wide = widen(jnp.concatenate([step, entering, leaving], axis=0), expand_ref)
    step_w, enter_w, leave_w = wide[:rows], wide[rows : 2 * rows], wide[2 * rows :]
    xs = x_conv * step_w
    xs_low = xs.astype(BF16)

    y = y_ref[...]
    z = p_ref[:, :width]
    sig_z = sigmoid(z)
    silu_z = z * sig_z
    gated = y * silu_z
    rstd = aux2_ref[:, 0:1]
    inner = aux2_ref[:, 1:2]
    d_mixed = db_ref[:, db_ref.shape[1] - width :]
    g_mgain = jnp.sum(d_mixed * (gated * rstd), axis=0, keepdims=True)
    d_gated = rstd * (d_mixed * mgain_ref[0:1, :]) - gated * inner
    d_y = d_gated * silu_z
    dp_ref[:, :width] = (d_gated * y * (sig_z * (1.0 + z * (1.0 - sig_z)))).astype(BF16)
    gw_ref[0:1, :] += g_mgain
    gw_ref[1:2, :] += jnp.sum(d_y * x_conv, axis=0, keepdims=True)

    dy_low = d_y.astype(BF16)
    held_low = st_ref[0]
    d_next = d_state[...]
    d_next_low = d_next.astype(BF16)
    entered_dy = (enter_w * d_y).astype(BF16)
    left_xs = (leave_w * xs).astype(BF16)
    from_next = leave_w * dot(keys, d_next_low)
    mask_t = triangle(rows, True) & (aux[:, 0:1] == segr_ref[0:1, :])
    b_dot_c = dot(keys, query, NT)
    lane = lax.broadcasted_iota(jnp.int32, (rows, LANES), 1)
    d_gram = jnp.zeros((rows, rows), F32)
    parts = []
    for pair in range(width // LANES):
        pair_dy = dy_low[:, pair * LANES : (pair + 1) * LANES]
        pair_x = xs_low[:, pair * LANES : (pair + 1) * LANES]
        sides = []
        for e in range(2):
            h = 2 * pair + e
            gap = cum_t[h : h + 1, :] - cum[:, h : h + 1]
            decay = jnp.exp(jnp.where(mask_t, gap, MASK_FILL))
            sides.append(dot((decay * b_dot_c).astype(BF16), pair_dy))
            inside = (lane < P_SIZE) if e == 0 else (lane >= P_SIZE)
            only = jnp.where(inside, pair_x, jnp.zeros_like(pair_x))
            d_gram = d_gram + decay * dot(only, pair_dy, NT)
        parts.append(jnp.where(lane < P_SIZE, sides[0], sides[1]))
    d_xs_inner = jnp.concatenate(parts, axis=1)
    d_xs = d_xs_inner + from_next
    d_gram = d_gram.astype(BF16)
    d_keys = dot(d_gram, query) + dot(left_xs, d_next_low, NT)
    d_query = dot(d_gram, keys, TN) + dot(entered_dy, held_low, NT)
    keep_w = enter_w[rows - 1 : rows, :]
    d_state[...] = dot(query, entered_dy, TN) + keep_w * d_next

    y_scan = y - dskip_ref[0:1, :] * x_conv
    pairs = dy_low.astype(F32) * y_scan - xs_low.astype(F32) * d_xs_inner
    d_cum = by_head(pairs - xs * from_next, reduce_ref)
    at_last = jnp.sum(xs * from_next, axis=0, keepdims=True) + keep_w * jnp.sum(
        held_low.astype(F32) * d_next, axis=0, keepdims=True
    )
    at_last = by_head(jnp.broadcast_to(at_last, (8, width)), reduce_ref)[0:1, :]
    d_log = dot_exact(triangle(rows, True).astype(F32), d_cum) + at_last
    d_step = by_head(x_conv * d_xs, reduce_ref) - d_log * jnp.exp(par_ref[0:1, :])
    d_dt = d_step * sigmoid(biased)
    dp_ref[:, dt0 : dt0 + LANES] = d_dt.astype(BF16)
    gh_ref[0:1, :] += jnp.sum(d_log * log_decay, axis=0, keepdims=True)
    gh_ref[1:2, :] += jnp.sum(d_dt, axis=0, keepdims=True)

    d_ux = (dskip_ref[0:1, :] * d_y + step_w * d_xs) * (sig_x * (1.0 + u_x * (1.0 - sig_x)))
    d_conv = jnp.concatenate([d_keys, d_query], axis=1)
    d_ubc = d_conv * (sig_bc * (1.0 + u_bc * (1.0 - sig_bc)))
    for grad, pad, fut, taps_ref, g_ref, c0 in (
        (d_ux, pad_x, fut_x, cx_ref, gcx_ref, x0),
        (d_ubc, pad_bc, fut_bc, cbc_ref, gcbc_ref, bc0),
    ):
        size = grad.shape[1]
        g_ref[3:4, :] += jnp.sum(grad * pad[8 : 8 + rows, :], axis=0, keepdims=True)
        for k in range(1, 4):
            shifted = pad[8 - k : 8 - k + rows, :] * aux[:, k : k + 1]
            g_ref[3 - k : 4 - k, :] += jnp.sum(grad * shifted, axis=0, keepdims=True)
        fut[0:rows, :] = grad
        d_in = taps_ref[3:4, :] * grad
        for k in range(1, 4):
            d_in = d_in + taps_ref[3 - k : 4 - k, :] * (
                fut[k : k + rows, :] * aux[:, 3 + k : 4 + k]
            )
        fut[rows : rows + 8, :] = grad[0:8, :]
        dp_ref[:, c0 : c0 + size] = d_in.astype(BF16)
    dp_ref[:, q0 : q0 + dqkv_ref.shape[1]] = dqkv_ref[...]


def head_maps(width):
    expand = (np.arange(width)[None, :] // P_SIZE == np.arange(LANES)[:, None]).astype(np.float32)
    return (
        jnp.asarray(np.concatenate([expand, expand], axis=0), BF16),
        jnp.asarray(expand.T, BF16),
    )


def mamba_specs(panel, chunk, chunk_of):
    length, total = panel.shape

    def rows(array):
        return pl.BlockSpec((chunk, array.shape[1]), lambda i: (chunk_of(i), 0))

    def fixed(array):
        return pl.BlockSpec(array.shape, lambda i: (0, 0))

    halo = pl.BlockSpec(
        (8, total), lambda i: (jnp.maximum(chunk_of(i) * (chunk // 8) - 1, 0), 0)
    )
    seg = pl.BlockSpec((8, chunk), lambda i: (0, chunk_of(i)))
    return rows, fixed, halo, seg


def mamba_forward(cols, panel, aux, segr, cx, cbc, par, dskip, mgain):
    length = panel.shape[0]
    width, states = cols["width"], cols["states"]
    chunk = min(CHUNK, length)
    chunks = length // chunk
    expand, _ = head_maps(width)
    rows, fixed, halo, seg = mamba_specs(panel, chunk, lambda i: i)
    small = [cx, cbc, par, dskip, mgain, expand]
    shapes = [
        jax.ShapeDtypeStruct((length, width), BF16),
        jax.ShapeDtypeStruct((length, LANES), F32),
        jax.ShapeDtypeStruct((length, width), F32),
        jax.ShapeDtypeStruct((chunks, states, width), BF16),
    ]
    return pl.pallas_call(
        partial(mamba_forward_kernel, cols),
        grid=(chunks,),
        in_specs=[rows(panel), halo, rows(aux), seg] + [fixed(a) for a in small],
        out_specs=[
            rows(shapes[0]),
            rows(shapes[1]),
            rows(shapes[2]),
            pl.BlockSpec((1, states, width), lambda i: (i, 0, 0)),
        ],
        out_shape=shapes,
        scratch_shapes=[
            pltpu.VMEM((states, width), F32),
            pltpu.VMEM((chunk + 8, width), F32),
            pltpu.VMEM((chunk + 8, 2 * states), F32),
        ],
        compiler_params=pltpu.CompilerParams(vmem_limit_bytes=VMEM_LIMIT),
        cost_estimate=pl.CostEstimate(
            flops=2 * length * width * (2 * states + 4 * chunk) * 4,
            bytes_accessed=4 * (panel.size + 3 * length * width),
            transcendentals=length * width * 4,
        ),
        name="mamba_forward",
    )(panel, panel, aux, segr, *small)


def mamba_backward(
    cols, panel, aux, segr, cx, cbc, par, dskip, mgain, y, held, d_branch_in, aux2, d_qkv
):
    length = panel.shape[0]
    width, states = cols["width"], cols["states"]
    chunk = min(CHUNK, length)
    chunks = length // chunk
    expand, reduce = head_maps(width)
    rows, fixed, halo, seg = mamba_specs(panel, chunk, lambda i: chunks - 1 - i)
    small = [cx, cbc, par, dskip, mgain, expand, reduce]
    sums = [(8, width), (8, width), (8, 2 * states), (8, LANES)]
    return pl.pallas_call(
        partial(mamba_backward_kernel, cols),
        grid=(chunks,),
        in_specs=[rows(panel), halo, rows(aux), seg]
        + [fixed(a) for a in small]
        + [
            rows(y),
            pl.BlockSpec((1, states, width), lambda i: (chunks - 1 - i, 0, 0)),
            rows(d_branch_in),
            rows(aux2),
            rows(d_qkv),
        ],
        out_specs=[rows(panel)] + [pl.BlockSpec(s, lambda i: (0, 0)) for s in sums],
        out_shape=[jax.ShapeDtypeStruct(panel.shape, BF16)]
        + [jax.ShapeDtypeStruct(s, F32) for s in sums],
        scratch_shapes=[
            pltpu.VMEM((states, width), F32),
            pltpu.VMEM((chunk + 8, width), F32),
            pltpu.VMEM((chunk + 8, 2 * states), F32),
            pltpu.VMEM((chunk + 8, width), F32),
            pltpu.VMEM((chunk + 8, 2 * states), F32),
        ],
        compiler_params=pltpu.CompilerParams(vmem_limit_bytes=VMEM_LIMIT),
        cost_estimate=pl.CostEstimate(
            flops=2 * length * width * (4 * states + 8 * chunk) * 4,
            bytes_accessed=4 * (panel.size + 3 * length * width),
            transcendentals=length * width * 4,
        ),
        name="mamba_backward",
    )(panel, panel, aux, segr, *small, y, held, d_branch_in, aux2, d_qkv)


def pad_rows(value, rows):
    return jnp.pad(value, ((0, rows - value.shape[0]), (0, 0)))


def segment_tables(segment, chunk):
    length = segment.shape[0]
    seg = segment.astype(F32)
    columns = [seg]
    for k in range(1, 4):
        before = jnp.concatenate([jnp.full((k,), -1.0, F32), seg[:-k]])
        columns.append((before == seg).astype(F32))
    for k in range(1, 4):
        after = jnp.concatenate([seg[k:], jnp.full((k,), -1.0, F32)])
        columns.append((after == seg).astype(F32))
    blocks = seg.reshape(-1, chunk)
    ends = blocks[:, -1:]
    prior = jnp.concatenate([jnp.full((1, 1), -1.0, F32), ends[:-1]], axis=0)
    columns.append((blocks == prior).astype(F32).reshape(-1))
    columns.append((blocks == ends).astype(F32).reshape(-1))
    stacked = jnp.stack(columns + [jnp.zeros_like(seg)] * (16 - len(columns)), axis=0)
    return jnp.pad(stacked.T, ((0, 0), (0, LANES - 16))), jnp.broadcast_to(seg, (8, length))


def rms_factor(hidden):
    return lax.rsqrt(jnp.mean(hidden * hidden, axis=-1, keepdims=True) + NORM_EPS)


def norm_backward(hidden, gain, d_normed, grad_h):
    factor = rms_factor(hidden)
    weighted = gain * d_normed
    inner_mean = jnp.mean(weighted * hidden, axis=-1, keepdims=True)
    return grad_h + factor * weighted - hidden * factor**3 * inner_mean, factor


def after(value, *earlier):
    return lax.optimization_barrier((value, *earlier))[0]


def local(
    inputs,
    cotangent,
    seg_ids,
    norm_gains,
    w_q,
    key_value_weight,
    w_zx,
    w_bc,
    w_dt,
    a_log,
    dt_bias,
    d_skip,
    conv_x,
    conv_bc,
    m_gain,
    w_ao,
    w_mo,
    w_gu,
    w_down,
):
    members = lax.axis_size("dp")
    size_z = lax.axis_size("tensor")
    me_z = lax.axis_index("tensor")
    me = lax.axis_index("dp").astype(jnp.int32).reshape(1)
    length = seg_ids.shape[1]
    model = inputs.shape[2]
    block = model // members
    owned = key_value_weight.shape[1]
    heads = w_q.shape[2] // HEAD_SIZE
    kv_head = me_z * heads // (QUERY_HEADS // KEY_VALUE_HEADS)
    width = w_zx.shape[3]
    m_heads = w_dt.shape[2]
    states2 = w_bc.shape[2]
    hidden_units = w_gu.shape[3]
    cols = {"width": width, "states": states2 // 2, "x": width, "q": 2 * width}
    cols["k"] = cols["q"] + heads * HEAD_SIZE
    cols["v"] = cols["k"] + HEAD_SIZE
    cols["bc"] = cols["v"] + HEAD_SIZE
    cols["dt"] = cols["bc"] + states2
    att_width = heads * HEAD_SIZE

    taps = conv_bc.shape[2]
    lane_rows = 2 * KEY_VALUE_HEADS * HEAD_SIZE + states2
    shares = [norm_gains.shape[2], taps]
    tiny = jnp.concatenate(
        [
            jnp.pad(norm_gains[0], ((0, 0), (0, lane_rows - shares[0]))),
            jnp.pad(conv_bc[0], ((0, 10), (0, lane_rows - shares[1]))),
        ],
        axis=0,
    )
    shared = jnp.concatenate([key_value_weight[0], w_bc[0]], axis=1)
    shared = jnp.concatenate([tiny, shared], axis=0)
    shared = z_gather_direct(shared).reshape(size_z, 16 + owned, lane_rows)
    x_all = z_gather(after(inputs[0], shared))
    tiny = shared[:, :16]
    shared = shared[:, 16:].reshape(block, lane_rows)
    gain_blocks = jnp.swapaxes(tiny[:, :2, : shares[0]], 0, 1).reshape(2, block)
    tap_blocks = jnp.swapaxes(tiny[:, 2:6, :taps], 0, 1).reshape(4, size_z * taps)
    tiny = jnp.concatenate(
        [
            jnp.pad(gain_blocks, ((0, 0), (0, max(block, LANES) - block))),
            jnp.pad(tap_blocks, ((0, 10), (0, max(block, LANES) - size_z * taps))),
        ],
        axis=0,
    )
    kv_cols = [
        lax.dynamic_slice_in_dim(shared, (base + kv_head) * HEAD_SIZE, HEAD_SIZE, 1)
        for base in (0, KEY_VALUE_HEADS)
    ]
    panel_rest = jnp.concatenate(
        [w_q[0]]
        + kv_cols
        + [
            shared[:, 2 * KEY_VALUE_HEADS * HEAD_SIZE :],
            jnp.pad(w_dt[0], ((0, 0), (0, LANES - m_heads))),
        ],
        axis=1,
    )
    w_zx_all, sent = dp_gather(w_zx[0].reshape(block, 2 * width))
    w_rest, sent = dp_gather(panel_rest, sent)
    w_a = jnp.concatenate([w_zx_all, w_rest], axis=1)
    tiny, _ = dp_gather(tiny)
    tiny = tiny.astype(F32).reshape(members, 16, -1)
    gains = jnp.swapaxes(tiny[:, :2, :block], 0, 1).reshape(2, model)
    tap_blocks = tiny[:, 2:6, : size_z * taps]
    order = np.array([2 * (j % (members // 2)) + j // (members // 2) for j in range(members)])
    owner = jnp.asarray(order, jnp.int32) ^ me[0]
    hit = (jnp.arange(members)[:, None] == owner[None, :]).astype(F32)
    convbc_all = jnp.sum(hit[:, :, None, None] * tap_blocks[None], axis=1)
    convbc_all = jnp.swapaxes(convbc_all, 0, 1).reshape(4, states2)
    w_b, sent = dp_gather(jnp.concatenate([w_ao[0], w_mo[0]], axis=0).T, sent)
    w_c, sent = dp_gather(w_gu[0].reshape(block, 2 * hidden_units), sent)
    w_d, sent = dp_gather(w_down[0].T, sent)

    x_local = permute_blocks(inputs[0], me, members, True).astype(F32)
    cot_low = permute_blocks(cotangent[0], me, members, True)
    cot = cot_low.astype(F32)
    gain1, gain2 = gains[0:1], gains[1:2]

    chunk = min(CHUNK, length)
    aux, segr = segment_tables(seg_ids[0], chunk)
    tables = [jnp.asarray(t) for t in rotary_rows(length)]
    cx = pad_rows(conv_x[0], 8)
    cbc = pad_rows(convbc_all, 8)
    par = jnp.pad(
        jnp.stack([a_log[0], dt_bias[0]]), ((0, 6), (0, LANES - m_heads))
    )
    dskip = jnp.broadcast_to(jnp.repeat(d_skip[0], P_SIZE)[None, :], (8, width))
    mgain = jnp.broadcast_to(m_gain[0][None, :], (8, width))

    normed1 = norm_permuted(x_all, gain1, me, members)
    panel = dot(normed1, w_a)
    d_out = lax.all_gather(after(cot_low, x_all), "tensor", axis=0, tiled=True)
    attended = attention_call(
        attention_forward_kernel,
        "attention_forward",
        panel,
        cols["q"],
        heads,
        tables,
        aux,
        segr,
        None,
        att_width,
        [],
    )
    gm, squares, y_out, held = mamba_forward(
        cols, panel, aux, segr, cx, cbc, par, dskip, mgain
    )
    squares = z_sum(squares[:, 0].reshape(-1, LANES)).reshape(length, 1)
    rstd = lax.rsqrt(squares / (HM * P_SIZE) + NORM_EPS)
    branch = dot(attended, w_b[:, :att_width], NT) + rstd * dot(gm, w_b[:, att_width:], NT)
    h_mid = x_local + z_scatter(branch.astype(BF16))

    normed2 = z_gather((h_mid * rms_factor(h_mid) * gain2).astype(BF16))
    gate_up = dot(normed2, w_c)
    gate, up = gate_up[:, :hidden_units], gate_up[:, hidden_units:]
    sig_gate = sigmoid(gate)
    silu_gate = gate * sig_gate
    act = (silu_gate * up).astype(BF16)
    d_act = dot(d_out, w_d)
    d_gu = jnp.concatenate(
        [d_act * up * (sig_gate * (1.0 + gate * (1.0 - sig_gate))), d_act * silu_gate], axis=1
    ).astype(BF16)
    d_norm2 = z_scatter(dot(d_gu, w_c, NT).astype(BF16))
    grad_mid, factor2 = norm_backward(h_mid, gain2, d_norm2, cot)
    g_gain2 = jnp.sum(d_norm2 * h_mid * factor2, axis=0)
    d_branch = z_gather(grad_mid.astype(BF16))
    ffn = lax.psum_scatter(
        after(dot(act, w_d, NT).astype(BF16), d_branch), "tensor", scatter_dimension=0, tiled=True
    ).astype(F32)
    hidden_out = permute_blocks((h_mid + ffn).astype(BF16), me, members, False)
    g_c = dp_scatter(dot(normed2, d_gu, TN).astype(BF16))
    g_d = dp_scatter(dot(d_out, act, TN).astype(BF16))

    d_branch = after(d_branch, g_c, g_d)
    d_b = dot(d_branch, w_b)
    mixed = (gm.astype(F32) * rstd).astype(BF16)
    g_b = dp_scatter(
        dot(d_branch, jnp.concatenate([attended, mixed], axis=1), TN).astype(BF16)
    )
    inner = jnp.sum(d_b[:, att_width:] * gm.astype(F32), axis=1)
    inner = z_sum(inner.reshape(-1, LANES)).reshape(length, 1)
    aux2 = jnp.pad(
        jnp.concatenate([rstd, rstd**3 * inner / (HM * P_SIZE)], axis=1),
        ((0, 0), (0, LANES - 2)),
    )
    d_qkv = attention_call(
        attention_backward_kernel,
        "attention_backward",
        panel,
        cols["q"],
        heads,
        tables,
        aux,
        segr,
        d_b,
        att_width + 2 * HEAD_SIZE,
        [pltpu.VMEM((length, HEAD_SIZE), F32), pltpu.VMEM((length, HEAD_SIZE), F32)],
    )
    d_panel, g_wide, g_cx, g_cbc, g_heads = mamba_backward(
        cols, panel, aux, segr, cx, cbc, par, dskip, mgain, y_out, held, d_b, aux2, d_qkv
    )
    d_norm1_part = dot(d_panel, w_a, NT)
    d_norm1 = z_scatter(d_norm1_part.astype(BF16))
    g_gain1 = jnp.sum(d_norm1_part * (normed1.astype(F32) / gain1), axis=0)
    grad_in, _ = norm_backward(x_local, gain1, d_norm1, grad_mid)
    input_grad = permute_blocks(grad_in, me, members, False)

    by_dp = [
        g_heads[0:2],
        jnp.pad(g_wide[1].reshape(m_heads, P_SIZE).sum(axis=1), (0, LANES - m_heads))[None],
        g_cx[:4].reshape(-1, LANES),
        g_wide[0].reshape(-1, LANES),
    ]
    counts = [v.shape[0] for v in by_dp]
    by_dp = jnp.concatenate(by_dp, axis=0)
    g_convbc = z_sum(g_cbc)[:4].reshape(-1, LANES)
    by_dp = jnp.concatenate([by_dp, g_convbc], axis=0)
    by_dp = dp_sum(pad_rows(by_dp, -(-by_dp.shape[0] // 8) * 8))
    ends = np.cumsum(counts)
    g_alog, g_dtbias = by_dp[0:1, :m_heads], by_dp[1:2, :m_heads]
    g_dskip = by_dp[2:3, :m_heads]
    g_convx = by_dp[ends[1] : ends[2]].reshape(1, 4, width)
    g_mgain = by_dp[ends[2] : ends[3]].reshape(1, width)
    g_convbc = by_dp[ends[3] : ends[3] + 4 * states2 // LANES].reshape(4, states2)
    slot = lax.axis_index("dp") * size_z + me_z
    g_convbc = lax.dynamic_slice_in_dim(g_convbc, slot * taps, taps, 1)[None]

    g_a = dp_scatter(dot(normed1, d_panel, TN).astype(BF16))
    g_gain = dp_scatter(jnp.pad(jnp.stack([g_gain1, g_gain2], axis=1), ((0, 0), (0, 6))))
    g_q = g_a[:, cols["q"] : cols["k"]]
    g_zx = g_a[:, : 2 * width].reshape(1, block, 2, width)
    g_dt = g_a[:, cols["dt"] : cols["dt"] + m_heads]
    kv_part = jnp.zeros((block, 2 * KEY_VALUE_HEADS * HEAD_SIZE), F32)
    for base, name in ((0, "k"), (KEY_VALUE_HEADS, "v")):
        kv_part = lax.dynamic_update_slice_in_dim(
            kv_part,
            g_a[:, cols[name] : cols[name] + HEAD_SIZE],
            (base + kv_head) * HEAD_SIZE,
            1,
        )
    shared_grad = z_scatter_direct(
        jnp.concatenate(
            [kv_part, g_a[:, cols["bc"] : cols["dt"]], jnp.pad(g_gain, ((0, 0), (0, LANES - 8)))],
            axis=1,
        )
    )
    kv_total = 2 * KEY_VALUE_HEADS * HEAD_SIZE
    g_kv = shared_grad[:, :kv_total]
    g_bc = shared_grad[:, kv_total : kv_total + states2]
    g_gains = shared_grad[:, kv_total + states2 : kv_total + states2 + 2].T

    return (
        hidden_out[None],
        input_grad[None],
        g_gains[None],
        g_q[None],
        g_kv[None],
        g_zx,
        g_bc[None],
        g_dt[None],
        g_alog,
        g_dtbias,
        g_dskip,
        g_convx,
        g_convbc,
        g_mgain,
        g_b[:, :att_width].T[None],
        g_b[:, att_width:].T[None],
        g_c.reshape(1, block, 2, hidden_units),
        g_d.T[None],
    )


def solution(mesh):
    return jax.shard_map(
        local,
        mesh=mesh,
        in_specs=(
            P("dp", "tensor", None),
            P("dp", "tensor", None),
            P("dp", None),
            P(None, None, ("dp", "tensor")),
            P(None, "dp", "tensor"),
            P(None, ("dp", "tensor"), None),
            P(None, "dp", None, "tensor"),
            P(None, ("dp", "tensor"), None),
            P(None, "dp", "tensor"),
            P(None, "tensor"),
            P(None, "tensor"),
            P(None, "tensor"),
            P(None, None, "tensor"),
            P(None, None, ("dp", "tensor")),
            P(None, "tensor"),
            P(None, "tensor", "dp"),
            P(None, "tensor", "dp"),
            P(None, "dp", None, "tensor"),
            P(None, "tensor", "dp"),
        ),
        out_specs=(
            P("dp", "tensor", None),
            P("dp", "tensor", None),
            P(None, None, ("dp", "tensor")),
            P(None, "dp", "tensor"),
            P(None, ("dp", "tensor"), None),
            P(None, "dp", None, "tensor"),
            P(None, ("dp", "tensor"), None),
            P(None, "dp", "tensor"),
            P(None, "tensor"),
            P(None, "tensor"),
            P(None, "tensor"),
            P(None, None, "tensor"),
            P(None, None, ("dp", "tensor")),
            P(None, "tensor"),
            P(None, "tensor", "dp"),
            P(None, "tensor", "dp"),
            P(None, "dp", None, "tensor"),
            P(None, "tensor", "dp"),
        ),
        check_vma=False,
    )
```

```python
from functools import partial

import jax
import jax.numpy as jnp
import numpy as np
from jax import lax
from jax.experimental import pallas as pl
from jax.experimental.pallas import tpu as pltpu
from jax.sharding import PartitionSpec as P

QUERY_HEADS = 8
KEY_VALUE_HEADS = 2
HEAD_SIZE = 128
HM = 48
P_SIZE = 64
LANES = 128
NORM_EPS = 1e-05
ROPE_BASE = 100000000000.0
MASK_FILL = -1e30
F32 = jnp.float32
BF16 = jnp.bfloat16
NN = (((1,), (0,)), ((), ()))
NT = (((1,), (1,)), ((), ()))
TN = (((0,), (0,)), ((), ()))
VMEM_LIMIT = 48 * 1024 * 1024


def dot(left, right, dims=NN):
    return lax.dot_general(left, right, dims, preferred_element_type=F32)


def sums_of(zero_one, value):
    high = value.astype(BF16)
    value = value - high.astype(F32)
    middle = value.astype(BF16)
    low = (value - middle.astype(F32)).astype(BF16)
    width = value.shape[1]
    out = dot(zero_one, jnp.concatenate([high, middle, low], axis=1))
    return out[:, :width] + out[:, width : 2 * width] + out[:, 2 * width :]


def sigmoid(v):
    return 0.5 * jnp.tanh(0.5 * v) + 0.5


def send_dp(value, mask):
    size = lax.axis_size("dp")
    return lax.ppermute(value, "dp", [(i, i ^ mask) for i in range(size)])


def chip_gather(rows, *earlier):
    chips = lax.axis_size("dp") // 2
    if earlier:
        rows = after(rows, *earlier)
    return [rows] + [send_dp(rows, 2 * k) for k in range(1, chips)]


def core_gather(pieces, *earlier):
    if earlier:
        pieces = ordered(pieces, *earlier)
    chips = len(pieces)
    me = lax.axis_index("dp")
    chip, core = lax.div(me, 2), lax.rem(me, 2)
    rows, width = pieces[0].shape
    mine = jnp.zeros((chips, rows, width), pieces[0].dtype)
    for k, piece in enumerate(pieces):
        mine = lax.dynamic_update_slice(mine, piece[None], (chip ^ k, 0, 0))
    other = send_dp(mine, 1)
    out = jnp.zeros((chips, 2, rows, width), mine.dtype)
    out = lax.dynamic_update_slice(out, mine[:, None], (0, core, 0, 0))
    out = lax.dynamic_update_slice(out, other[:, None], (0, 1 - core, 0, 0))
    return out.reshape(2 * chips * rows, width)


def core_scatter(grad, *earlier):
    chips = lax.axis_size("dp") // 2
    core = lax.rem(lax.axis_index("dp"), 2)
    blocks = grad.reshape(chips, 2, -1, grad.shape[1])
    other = send_dp(lax.dynamic_index_in_dim(blocks, 1 - core, 1, keepdims=False), 1)
    if earlier:
        other = after(other, *earlier)
    mine = lax.dynamic_index_in_dim(blocks, core, 1, keepdims=False)
    return (mine.astype(F32) + other.astype(F32)).astype(grad.dtype)


def chip_scatter(pair):
    chips = pair.shape[0]
    chip = lax.div(lax.axis_index("dp"), 2)
    pieces = [lax.dynamic_index_in_dim(pair, chip, 0, keepdims=False)]
    for k in range(1, chips):
        piece = lax.dynamic_index_in_dim(pair, chip ^ k, 0, keepdims=False)
        pieces.append(send_dp(piece, 2 * k))
    return pieces


def add_up(pieces, *earlier):
    if earlier:
        pieces = ordered(pieces, *earlier)
    total = pieces[0].astype(F32)
    for piece in pieces[1:]:
        total = total + piece.astype(F32)
    return total


def dp_sum(value):
    chips = lax.axis_size("dp") // 2
    value = value + send_dp(value, 1)
    total = value
    for k in range(1, chips):
        total = total + send_dp(value, 2 * k)
    return total


def send_z(value, shift):
    size = lax.axis_size("tensor")
    return lax.ppermute(value, "tensor", [(i, (i + shift) % size) for i in range(size)])


def z_gather_direct(rows):
    size = lax.axis_size("tensor")
    me = lax.axis_index("tensor")
    count = rows.shape[0]
    out = jnp.zeros((size * count,) + rows.shape[1:], rows.dtype)
    pieces = [rows] + [send_z(rows, k) for k in range(1, size)]
    for k, piece in enumerate(pieces):
        out = lax.dynamic_update_slice_in_dim(out, piece, lax.rem(me - k + size, size) * count, 0)
    return out


def z_scatter_direct(total):
    size = lax.axis_size("tensor")
    me = lax.axis_index("tensor")
    count = total.shape[0] // size
    mine = lax.dynamic_slice_in_dim(total, me * count, count, 0).astype(F32)
    for k in range(1, size):
        piece = lax.dynamic_slice_in_dim(total, lax.rem(me + k, size) * count, count, 0)
        mine = mine + send_z(piece, k).astype(F32)
    return mine


def ordered(values, *earlier):
    return lax.optimization_barrier((tuple(values), earlier))[0]


def z_gather_first(rows):
    size = lax.axis_size("tensor")
    right = lax.ppermute(rows, "tensor", [(i, i + 1) for i in range(size - 1)])
    left = lax.ppermute(rows, "tensor", [(i, i - 1) for i in range(1, size)])
    return [right, left]


def z_gather_parts(parts, hooks=None, first=None):
    size = lax.axis_size("tensor")
    hooks = hooks or {}
    moved = [[] for _ in parts]
    for h, rows in enumerate(parts):
        right = left = rows
        for s in range(size - 1):
            if s == 0 and h == 0 and first is not None:
                right, left = first
                moved[h].append(first)
                continue
            earlier = list(hooks.get((h, s), []))
            if s or earlier:
                right, left = ordered((right, left), *earlier)
            right = lax.ppermute(right, "tensor", [(i, i + 1) for i in range(s, size - 1)])
            left = lax.ppermute(left, "tensor", [(i, i - 1) for i in range(1, size - s)])
            moved[h].append([right, left])
    return moved


def line_gather(parts, *earlier):
    out = []
    for part in parts:
        if earlier:
            part = after(part, *earlier)
        out.append(lax.all_gather(part, "tensor", axis=0, tiled=True))
    return out


def line_scatter(parts, *earlier):
    out = []
    for part in parts:
        if earlier:
            part = after(part, *earlier)
        out.append(
            lax.psum_scatter(part, "tensor", scatter_dimension=0, tiled=True).astype(F32)
        )
    return out


def line_sends(parts, *earlier):
    size = lax.axis_size("tensor")
    me = lax.axis_index("tensor")
    count = parts[0].shape[0] // size
    pieces = []
    for k in range(size):
        index = lax.rem(me + k, size) * count
        piece = [lax.dynamic_slice_in_dim(part, index, count, 0) for part in parts]
        piece = jnp.concatenate(piece, axis=0)
        if k:
            if earlier:
                piece = after(piece, *earlier)
            piece = send_z(piece, k)
        pieces.append(piece)
    return pieces


def place_kernel(place_ref, in_ref, out_ref):
    out_ref[...] = in_ref[...]


def z_place(rows, moved):
    size = lax.axis_size("tensor")
    me = lax.axis_index("tensor")
    count, width = rows.shape
    out = pl.pallas_call(
        place_kernel,
        grid_spec=pltpu.PrefetchScalarGridSpec(
            num_scalar_prefetch=1,
            grid=(1,),
            in_specs=[pl.BlockSpec((count, width), lambda i, place_ref: (0, 0))],
            out_specs=pl.BlockSpec((count, width), lambda i, place_ref: (place_ref[0], 0)),
        ),
        out_shape=jax.ShapeDtypeStruct((size * count, width), rows.dtype),
        cost_estimate=pl.CostEstimate(
            flops=0, bytes_accessed=4 * rows.size, transcendentals=0
        ),
        name="place",
    )(me.astype(jnp.int32).reshape(1), rows)
    for d in range(1, size):
        piece = moved[d - 1][0] + moved[size - d - 1][1]
        at = lax.rem(me - d + size, size) * count
        out = lax.dynamic_update_slice_in_dim(out, piece, at, 0)
    return out


def block_of(total, index, size):
    if isinstance(total, list):
        return jnp.concatenate([block_of(t, index, size) for t in total], axis=0)
    count = total.shape[0] // size
    return lax.dynamic_slice_in_dim(total, index * count, count, 0)


def z_scatter_first(parts):
    size = lax.axis_size("tensor")
    right = lax.ppermute(block_of(parts[0], size - 1, size), "tensor", [(0, 1)])
    left = lax.ppermute(block_of(parts[0], 0, size), "tensor", [(size - 1, size - 2)])
    return [right, left]


def z_scatter_parts(parts, hooks=None, first=None):
    size = lax.axis_size("tensor")
    me = lax.axis_index("tensor")
    hooks = hooks or {}
    sums, moved = [], [[] for _ in parts]
    for h, total in enumerate(parts):

        def part(offset, total=total):
            return block_of(total, jnp.clip(me + offset, 0, size - 1), size)

        right = left = None
        for s in range(size - 1):
            if s == 0 and h == 0 and first is not None:
                right, left = first
                moved[h].append(first)
                continue
            d = size - 1 - s
            to_right, to_left = part(d), part(-d)
            if s:
                to_right = (to_right.astype(F32) + right.astype(F32)).astype(BF16)
                to_left = (to_left.astype(F32) + left.astype(F32)).astype(BF16)
            earlier = list(hooks.get((h, s), []))
            if h:
                earlier += moved[h - 1][s]
            to_right, to_left = ordered((to_right, to_left), *earlier)
            right = lax.ppermute(to_right, "tensor", [(i, i + 1) for i in range(s + 1)])
            left = lax.ppermute(to_left, "tensor", [(i, i - 1) for i in range(size - 1 - s, size)])
            moved[h].append([right, left])
        sums.append(part(0).astype(F32) + right.astype(F32) + left.astype(F32))
    return sums, moved


def z_sum(value):
    size = lax.axis_size("tensor")
    total = value
    for k in range(1, size):
        total = total + send_z(value, k)
    return total


def tile_of(width):
    return max(t for t in range(LANES, 513, LANES) if width % t == 0)


def norm_project_kernel(members, x_ref, gain_ref, w_ref, *refs):
    normed_ref, out_ref = refs[-2:]
    block, rows = x_ref.shape[1] // members, w_ref.shape[0] // members

    @pl.when(pl.program_id(0) == 0)
    def _():
        x = x_ref[...].astype(F32)
        mean = jnp.sum(x * x, axis=1, keepdims=True) * (1.0 / x.shape[1])
        normed_ref[...] = (x * lax.rsqrt(mean + NORM_EPS) * gain_ref[...]).astype(BF16)

    out = None
    for j in range(members):
        part = dot(
            normed_ref[:, j * block : (j + 1) * block], w_ref[j * rows : j * rows + block, :]
        )
        out = part if out is None else out + part
    out_ref[...] = out


def norm_project(x, gain, weights, held, index, parts, members):
    rows, model = x.shape
    total, width = rows * parts, weights.shape[1]
    tile = tile_of(width)
    return pl.pallas_call(
        partial(norm_project_kernel, members),
        grid=(width // tile,),
        in_specs=[
            pl.BlockSpec((rows, model), lambda j: (0, 0)),
            pl.BlockSpec((1, model), lambda j: (0, 0)),
            pl.BlockSpec((weights.shape[0], tile), lambda j: (0, j)),
        ]
        + [pl.BlockSpec(memory_space=pl.ANY)] * len(held),
        out_specs=[
            pl.BlockSpec((rows, model), lambda j: (index, 0)),
            pl.BlockSpec((rows, tile), lambda j: (index, j)),
        ],
        out_shape=[
            jax.ShapeDtypeStruct((total, model), BF16),
            jax.ShapeDtypeStruct((total, width), F32),
        ],
        input_output_aliases={3: 0, 4: 1} if held else {},
        compiler_params=pltpu.CompilerParams(vmem_limit_bytes=VMEM_LIMIT),
        cost_estimate=pl.CostEstimate(
            flops=2 * rows * model * width,
            bytes_accessed=2 * (rows + width) * model + 4 * rows * width,
            transcendentals=0,
        ),
        name="norm_project",
    )(x, gain, weights, *held)


def gradient_kernel(parts, *refs):
    out_ref = refs[-1]
    count = len(parts)
    lefts, rights = list(refs[: sum(parts)]), refs[sum(parts) : sum(parts) + count]
    at = 0
    for number, right in zip(parts, rights):
        width = right.shape[1]
        rows = right.shape[0] // number
        total = None
        for h in range(number):
            part = dot(lefts.pop(0)[...], right[h * rows : (h + 1) * rows, :], TN)
            total = part if total is None else total + part
        out_ref[:, at : at + width] = total.astype(BF16)
        at += width


def gradient(lefts, rights, held, piece, pieces):
    model = lefts[0][0].shape[1]
    width = sum(right.shape[1] for right in rights)
    tile = min(256, model // pieces)
    steps = model // pieces // tile
    parts = [len(left) for left in lefts]
    flat = [part for left in lefts for part in left]
    held = [] if held is None else [held]
    return pl.pallas_call(
        partial(gradient_kernel, parts),
        grid=(steps,),
        in_specs=[
            pl.BlockSpec((part.shape[0], tile), lambda j: (0, piece * steps + j)) for part in flat
        ]
        + [pl.BlockSpec(right.shape, lambda j: (0, 0)) for right in rights]
        + [pl.BlockSpec(memory_space=pl.ANY)] * len(held),
        out_specs=pl.BlockSpec((tile, width), lambda j: (piece * steps + j, 0)),
        out_shape=jax.ShapeDtypeStruct((model, width), BF16),
        input_output_aliases={len(flat) + len(rights): 0} if held else {},
        compiler_params=pltpu.CompilerParams(vmem_limit_bytes=VMEM_LIMIT),
        cost_estimate=pl.CostEstimate(
            flops=2 * rights[0].shape[0] * (model // pieces) * width,
            bytes_accessed=2 * (rights[0].shape[0] * (model + width) + model * width) // pieces,
            transcendentals=0,
        ),
        name="gradient",
    )(*flat, *rights, *held)


def feed_forward_kernel(parts, *refs):
    xs, ds = refs[:parts], refs[parts : 2 * parts]
    gate_ref, up_ref, down_ref, act_ref, d_gate_ref, d_up_ref = refs[2 * parts :]
    for h in range(parts):
        rows = xs[h].shape[0]
        here = slice(h * rows, (h + 1) * rows)
        gate = dot(xs[h][...], gate_ref[...])
        up = dot(xs[h][...], up_ref[...])
        sig_gate = sigmoid(gate)
        silu_gate = gate * sig_gate
        act_ref[here, :] = (silu_gate * up).astype(BF16)
        d_act = dot(ds[h][...], down_ref[...])
        d_gate = d_act * up * (sig_gate * (1.0 + gate * (1.0 - sig_gate)))
        d_gate_ref[here, :] = d_gate.astype(BF16)
        d_up_ref[here, :] = (d_act * silu_gate).astype(BF16)


def feed_forward(normed, d_out, weights, hidden_units):
    parts, (rows, model) = len(normed), normed[0].shape
    tile = min(256, hidden_units)
    steps = hidden_units // tile

    def columns(first):
        return pl.BlockSpec((model, tile), lambda j: (0, first * steps + j))

    whole = pl.BlockSpec((rows, model), lambda j: (0, 0))
    out = jax.ShapeDtypeStruct((rows * parts, hidden_units), BF16)
    return pl.pallas_call(
        partial(feed_forward_kernel, parts),
        grid=(steps,),
        in_specs=[whole] * (2 * parts) + [columns(0), columns(1), columns(2)],
        out_specs=[pl.BlockSpec((rows * parts, tile), lambda j: (0, j))] * 3,
        out_shape=[out] * 3,
        compiler_params=pltpu.CompilerParams(vmem_limit_bytes=VMEM_LIMIT),
        cost_estimate=pl.CostEstimate(
            flops=6 * rows * parts * model * hidden_units,
            bytes_accessed=2 * (2 * rows * parts + 3 * hidden_units) * model,
            transcendentals=rows * parts * hidden_units,
        ),
        name="feed_forward",
    )(*normed, *d_out, weights, weights, weights)


def branch_back_kernel(parts, *refs):
    w_ref, gm_ref, out_ref, inner_ref = refs[parts:]
    first = pl.program_id(0) == 0

    @pl.when(first)
    def _():
        inner_ref[...] = jnp.zeros_like(inner_ref)

    for h in range(parts):
        rows = refs[h].shape[0]
        here = slice(h * rows, (h + 1) * rows)
        out = dot(refs[h][...], w_ref[...])
        out_ref[here, :] = out
        inner = jnp.sum(out * gm_ref[here, :].astype(F32), axis=1, keepdims=True)
        inner_ref[here, :] += jnp.where(first, 0.0, inner)


def branch_back(d_branch, weights, gm):
    parts, (rows, model) = len(d_branch), d_branch[0].shape
    tile = weights.shape[1] - gm.shape[1]
    steps = weights.shape[1] // tile
    total = rows * parts
    return pl.pallas_call(
        partial(branch_back_kernel, parts),
        grid=(steps,),
        in_specs=[pl.BlockSpec((rows, model), lambda j: (0, 0))] * parts
        + [
            pl.BlockSpec((model, tile), lambda j: (0, j)),
            pl.BlockSpec((total, tile), lambda j: (0, jnp.maximum(j - 1, 0))),
        ],
        out_specs=[
            pl.BlockSpec((total, tile), lambda j: (0, j)),
            pl.BlockSpec((total, LANES), lambda j: (0, 0)),
        ],
        out_shape=[
            jax.ShapeDtypeStruct((total, weights.shape[1]), F32),
            jax.ShapeDtypeStruct((total, LANES), F32),
        ],
        compiler_params=pltpu.CompilerParams(vmem_limit_bytes=VMEM_LIMIT),
        cost_estimate=pl.CostEstimate(
            flops=2 * total * model * weights.shape[1],
            bytes_accessed=2 * (total + weights.shape[1]) * model,
            transcendentals=0,
        ),
        name="branch_back",
    )(*d_branch, weights, gm)


def transposed_kernel(count, *refs):
    out = None
    for left, right in zip(refs[:count], refs[count : 2 * count]):
        part = dot(left[...], right[...], NT)
        out = part if out is None else out + part
    refs[-1][...] = out.astype(BF16)


def transposed_product(lefts, weights, first):
    rows, width = lefts[0].shape
    model = weights.shape[0]
    tile = min(512, model)
    count = len(lefts)

    def columns(k):
        return pl.BlockSpec((tile, width), lambda j: (j, first + k))

    return pl.pallas_call(
        partial(transposed_kernel, count),
        grid=(model // tile,),
        in_specs=[pl.BlockSpec((rows, width), lambda j: (0, 0))] * count
        + [columns(k) for k in range(count)],
        out_specs=pl.BlockSpec((rows, tile), lambda j: (0, j)),
        out_shape=jax.ShapeDtypeStruct((rows, model), BF16),
        compiler_params=pltpu.CompilerParams(vmem_limit_bytes=VMEM_LIMIT),
        cost_estimate=pl.CostEstimate(
            flops=2 * rows * model * width * count,
            bytes_accessed=2 * ((rows + model) * width * count + rows * model),
            transcendentals=0,
        ),
        name="transposed_product",
    )(*lefts, *([weights] * count))


def branch_kernel(att_ref, gm_ref, rstd_ref, w_ref, out_ref):
    split = att_ref.shape[1]
    out = dot(att_ref[...], w_ref[:, :split], NT)
    out = out + rstd_ref[...] * dot(gm_ref[...], w_ref[:, split:], NT)
    out_ref[...] = out.astype(BF16)


def branch_product(attended, gm, rstd, weights):
    rows = attended.shape[0]
    model, width = weights.shape
    tile = min(512, model)

    def whole(array):
        return pl.BlockSpec(array.shape, lambda j: (0, 0))

    return pl.pallas_call(
        branch_kernel,
        grid=(model // tile,),
        in_specs=[
            whole(attended),
            whole(gm),
            whole(rstd),
            pl.BlockSpec((tile, width), lambda j: (j, 0)),
        ],
        out_specs=pl.BlockSpec((rows, tile), lambda j: (0, j)),
        out_shape=jax.ShapeDtypeStruct((rows, model), BF16),
        compiler_params=pltpu.CompilerParams(vmem_limit_bytes=VMEM_LIMIT),
        cost_estimate=pl.CostEstimate(
            flops=2 * rows * model * width,
            bytes_accessed=2 * ((rows + model) * width + rows * model),
            transcendentals=0,
        ),
        name="branch",
    )(attended, gm, rstd, weights)


def back_kernel(block, d_ref, w_ref, out_ref):
    count = out_ref.shape[1] // block
    rows = w_ref.shape[0] // count
    for k in range(count):
        out = dot(d_ref[...], w_ref[k * rows : k * rows + block, :], NT)
        out_ref[:, k * block : (k + 1) * block] = out.astype(BF16)


def back_product(d_all, weights, index, parts, members, model):
    rows, block = d_all.shape[0] // parts, model // members
    each = 2
    return pl.pallas_call(
        partial(back_kernel, block),
        grid=(members // each,),
        in_specs=[
            pl.BlockSpec((rows, d_all.shape[1]), lambda j: (index, 0)),
            pl.BlockSpec((each * weights.shape[0] // members, weights.shape[1]), lambda j: (j, 0)),
        ],
        out_specs=pl.BlockSpec((rows, each * block), lambda j: (0, j)),
        out_shape=jax.ShapeDtypeStruct((rows, model), BF16),
        compiler_params=pltpu.CompilerParams(vmem_limit_bytes=VMEM_LIMIT),
        cost_estimate=pl.CostEstimate(
            flops=2 * rows * model * d_all.shape[1],
            bytes_accessed=2 * (rows * d_all.shape[1] + weights.size + rows * model),
            transcendentals=0,
        ),
        name="back_product",
    )(d_all, weights)


def rotary_rows(length):
    half = HEAD_SIZE // 2
    freqs = np.float32(ROPE_BASE) ** (
        -np.arange(half).astype(np.float32) * np.float32(2.0) / np.float32(HEAD_SIZE)
    )
    angles = np.arange(length).astype(np.float32)[:, None] * freqs.astype(np.float32)[None, :]
    cosine, sine = np.cos(angles), np.sin(angles)
    return (
        np.concatenate([cosine, cosine], axis=1).astype(np.float32),
        np.concatenate([-sine, sine], axis=1).astype(np.float32),
    )


def rotate(value, cosine, sine):
    return value * cosine + pltpu.roll(value, HEAD_SIZE // 2, 1) * sine


def chunk_place(index, parts, members):
    return lax.rem(index, parts) * members + lax.div(index, parts)


def in_sequence(ref, places, rows, columns=slice(None)):
    return jnp.concatenate([ref[p * rows : (p + 1) * rows, columns] for p in places], axis=0)


def attention_probs(q_ref, keys, cos_ref, sin_ref, allowed, start, stop, places, rows):
    here = places[start // rows : stop // rows]
    query = in_sequence(q_ref, here, rows)
    query = rotate(query, cos_ref[start:stop, :], sin_ref[start:stop, :]).astype(BF16)
    scores = dot(query, keys, NT) * (HEAD_SIZE**-0.5)
    scores = jnp.where(allowed, scores, MASK_FILL)
    raised = jnp.exp(scores - jnp.max(scores, axis=1, keepdims=True))
    return query, raised * (1.0 / jnp.sum(raised, axis=1, keepdims=True))


def attention_mask(aux_ref, segr_ref, start, stop):
    rows = start + lax.broadcasted_iota(jnp.int32, (stop - start, stop), 0)
    cols = lax.broadcasted_iota(jnp.int32, (stop - start, stop), 1)
    return (aux_ref[start:stop, 0:1] == segr_ref[0:1, :stop]) & (rows >= cols)


def attention_forward_kernel(heads, block, places, *refs):
    q_refs = refs[:heads]
    k_ref, v_ref, cos_ref, sin_ref, aux_ref, segr_ref, out_ref = refs[heads:]
    length = k_ref.shape[0]
    rows = length // len(places)
    keys = rotate(in_sequence(k_ref, places, rows), cos_ref[...], sin_ref[...]).astype(BF16)
    vals = in_sequence(v_ref, places, rows).astype(BF16)
    for start in range(0, length, block):
        stop = start + block
        allowed = attention_mask(aux_ref, segr_ref, start, stop)
        for h in range(heads):
            _, probs = attention_probs(
                q_refs[h], keys[:stop], cos_ref, sin_ref, allowed, start, stop, places, rows
            )
            out = dot(probs.astype(BF16), vals[:stop]).astype(BF16)
            columns = slice(h * HEAD_SIZE, (h + 1) * HEAD_SIZE)
            for c in range(block // rows):
                p = places[start // rows + c]
                out_ref[p * rows : (p + 1) * rows, columns] = out[c * rows : (c + 1) * rows]


def attention_backward_kernel(heads, block, places, *refs):
    q_refs = refs[:heads]
    k_ref, v_ref, cos_ref, sin_ref, aux_ref, segr_ref, do_ref, out_ref, dk, dv = refs[heads:]
    length = k_ref.shape[0]
    rows = length // len(places)
    scale = HEAD_SIZE**-0.5
    keys = rotate(in_sequence(k_ref, places, rows), cos_ref[...], sin_ref[...]).astype(BF16)
    vals = in_sequence(v_ref, places, rows).astype(BF16)
    dk[...] = jnp.zeros_like(dk)
    dv[...] = jnp.zeros_like(dv)
    for start in range(0, length, block):
        stop = start + block
        allowed = attention_mask(aux_ref, segr_ref, start, stop)
        here = places[start // rows : stop // rows]
        for h in range(heads):
            columns = slice(h * HEAD_SIZE, (h + 1) * HEAD_SIZE)
            query, probs = attention_probs(
                q_refs[h], keys[:stop], cos_ref, sin_ref, allowed, start, stop, places, rows
            )
            given = in_sequence(do_ref, here, rows, columns).astype(BF16)
            d_probs = dot(given, vals[:stop], NT)
            delta = jnp.sum(probs * d_probs, axis=1, keepdims=True)
            d_scores = (probs * (d_probs - delta)).astype(BF16)
            d_query = dot(d_scores, keys[:stop]) * scale
            d_query = rotate(d_query, cos_ref[start:stop, :], -sin_ref[start:stop, :]).astype(BF16)
            for c, p in enumerate(here):
                out_ref[p * rows : (p + 1) * rows, columns] = d_query[c * rows : (c + 1) * rows]
            dk[:stop, :] += dot(d_scores, query, TN)
            dv[:stop, :] += dot(probs.astype(BF16), given, TN)
    d_keys = rotate(dk[...] * scale, cos_ref[...], -sin_ref[...]).astype(BF16)
    d_vals = dv[...].astype(BF16)
    for c, p in enumerate(places):
        there = slice(p * rows, (p + 1) * rows)
        out_ref[there, heads * HEAD_SIZE : (heads + 1) * HEAD_SIZE] = d_keys[
            c * rows : (c + 1) * rows
        ]
        out_ref[there, (heads + 1) * HEAD_SIZE :] = d_vals[c * rows : (c + 1) * rows]


def attention_call(
    kernel, name, panel, first, heads, tables, aux, segr, extra, width, scratch, places
):
    length = panel.shape[0]

    def column(index):
        return pl.BlockSpec((length, HEAD_SIZE), lambda i: (0, index))

    def whole(array):
        return pl.BlockSpec(array.shape, lambda i: (0, 0))

    specs = [column(first // HEAD_SIZE + h) for h in range(heads + 2)]
    operands = [*tables, aux, segr]
    specs += [whole(a) for a in operands]
    if extra is not None:
        specs.append(pl.BlockSpec((length, heads * HEAD_SIZE), lambda i: (0, 0)))
        operands.append(extra)
    return pl.pallas_call(
        partial(kernel, heads, min(256, length), places),
        grid=(1,),
        in_specs=specs,
        out_specs=pl.BlockSpec((length, width), lambda i: (0, 0)),
        out_shape=jax.ShapeDtypeStruct((length, width), BF16),
        scratch_shapes=scratch,
        compiler_params=pltpu.CompilerParams(vmem_limit_bytes=VMEM_LIMIT),
        cost_estimate=pl.CostEstimate(
            flops=(5000 if extra is not None else 3300) * heads * length * length,
            bytes_accessed=4 * length * 12 * HEAD_SIZE,
            transcendentals=heads * length * length,
        ),
        name=name,
    )(*([panel] * (heads + 2)), *operands)


def split_pair(value):
    high = value.astype(BF16)
    return high, (value - high.astype(F32)).astype(BF16)


def widen(value, expand_ref):
    high, rest = split_pair(value)
    return dot(jnp.concatenate([high, rest], axis=1), expand_ref[...])


def by_head(value, reduce_ref):
    high, rest = split_pair(value)
    return dot(high, reduce_ref[...]) + dot(rest, reduce_ref[...])


def conv_rows(current, halo, pad, taps_ref, aux):
    rows = current.shape[0]
    pad[0:8, :] = halo
    pad[8 : 8 + rows, :] = current
    out = taps_ref[3:4, :] * current
    for k in range(1, 4):
        out = out + taps_ref[3 - k : 4 - k, :] * (pad[8 - k : 8 - k + rows, :] * aux[:, k : k + 1])
    return out


def head_scalars(dt_raw, par_ref, lower):
    biased = dt_raw + par_ref[1:2, :]
    step = jnp.maximum(biased, 0.0) + jnp.log1p(jnp.exp(-jnp.abs(biased)))
    log_decay = -step * jnp.exp(par_ref[0:1, :])
    cumulative = sums_of(lower, log_decay)
    return biased, step, log_decay, cumulative


def triangle(rows, flip):
    i = lax.broadcasted_iota(jnp.int32, (rows, rows), 0)
    j = lax.broadcasted_iota(jnp.int32, (rows, rows), 1)
    return (i <= j) if flip else (i >= j)


def mamba_forward_kernel(
    cols,
    p_ref,
    halo_ref,
    aux_ref,
    segr_ref,
    cx_ref,
    cbc_ref,
    par_ref,
    dskip_ref,
    mgain_ref,
    expand_ref,
    gm_ref,
    sq_ref,
    y_ref,
    st_ref,
    state,
    pad_x,
    pad_bc,
):
    width, states = cols["width"], cols["states"]
    rows = p_ref.shape[0]
    r_ref, halo_r_ref = p_ref.at[:, 2 * width :], halo_ref.at[:, 2 * width :]
    x0, bc0, dt0 = cols["x"], cols["bc"], cols["dt"]

    @pl.when(pl.program_id(0) == 0)
    def _():
        state[...] = jnp.zeros_like(state)

    aux = aux_ref[...]
    u_x = conv_rows(
        p_ref[:, x0 : x0 + width], halo_ref[:, x0 : x0 + width], pad_x, cx_ref, aux
    )
    x_conv = u_x * sigmoid(u_x)
    u_bc = conv_rows(
        r_ref[:, bc0 : bc0 + 2 * states], halo_r_ref[:, bc0 : bc0 + 2 * states], pad_bc, cbc_ref, aux
    )
    bc = (u_bc * sigmoid(u_bc)).astype(BF16)
    keys, query = bc[:, :states], bc[:, states:]
    lower = triangle(rows, False)
    _, step, _, cum = head_scalars(
        r_ref[:, dt0 : dt0 + LANES], par_ref, lower.astype(F32).astype(BF16)
    )
    cum_t = cum.T
    last = cum[rows - 1 : rows, :]
    entering = jnp.exp(cum) * aux[:, 7:8]
    leaving = jnp.exp(last - cum) * aux[:, 8:9]
    wide = widen(jnp.concatenate([step, entering, leaving], axis=0), expand_ref)
    step_w, enter_w, leave_w = wide[:rows], wide[rows : 2 * rows], wide[2 * rows :]
    xs = x_conv * step_w
    xs_low = xs.astype(BF16)
    mask = lower & (aux[:, 0:1] == segr_ref[0:1, :])
    c_dot_b = dot(query, keys, NT)
    held = state[...]
    held_low = held.astype(BF16)
    st_ref[0] = held_low
    carried = dot(query, held_low) * enter_w
    lane = lax.broadcasted_iota(jnp.int32, (rows, LANES), 1)
    parts = []
    for pair in range(width // LANES):
        pair_x = xs_low[:, pair * LANES : (pair + 1) * LANES]
        sides = []
        for e in range(2):
            h = 2 * pair + e
            gap = cum[:, h : h + 1] - cum_t[h : h + 1, :]
            decay = jnp.exp(jnp.where(mask, gap, MASK_FILL))
            sides.append(dot((decay * c_dot_b).astype(BF16), pair_x))
        parts.append(jnp.where(lane < P_SIZE, sides[0], sides[1]))
    y = jnp.concatenate(parts, axis=1) + carried + dskip_ref[0:1, :] * x_conv
    state[...] = held * enter_w[rows - 1 : rows, :] + dot(
        keys, (leave_w * xs).astype(BF16), TN
    )
    z = p_ref[:, :width]
    gated = y * (z * sigmoid(z))
    y_ref[...] = y
    gm_ref[...] = (gated * mgain_ref[0:1, :]).astype(BF16)
    sq_ref[...] = jnp.broadcast_to(jnp.sum(gated * gated, axis=1, keepdims=True), sq_ref.shape)


def mamba_backward_kernel(
    cols,
    p_ref,
    halo_ref,
    aux_ref,
    segr_ref,
    cx_ref,
    cbc_ref,
    par_ref,
    dskip_ref,
    mgain_ref,
    expand_ref,
    reduce_ref,
    y_ref,
    st_ref,
    db_ref,
    aux2_ref,
    dqkv_ref,
    da_ref,
    gw_ref,
    gcx_ref,
    gcbc_ref,
    gh_ref,
    d_state,
    pad_x,
    pad_bc,
    fut_x,
    fut_bc,
):
    width, states = cols["width"], cols["states"]
    rows = p_ref.shape[0]
    r_ref, halo_r_ref = p_ref.at[:, 2 * width :], halo_ref.at[:, 2 * width :]
    x0, q0, bc0, dt0 = cols["x"], cols["q"], cols["bc"], cols["dt"]
    dp_ref = da_ref.at[:, : 2 * width]
    dr_ref = da_ref.at[:, 2 * width :]
    first_step = pl.program_id(0) == 0

    @pl.when(first_step)
    def _():
        d_state[...] = jnp.zeros_like(d_state)
        gw_ref[...] = jnp.zeros_like(gw_ref)
        gcx_ref[...] = jnp.zeros_like(gcx_ref)
        gcbc_ref[...] = jnp.zeros_like(gcbc_ref)
        gh_ref[...] = jnp.zeros_like(gh_ref)
        fut_x[...] = jnp.zeros_like(fut_x)
        fut_bc[...] = jnp.zeros_like(fut_bc)

    aux = aux_ref[...]
    u_x = conv_rows(
        p_ref[:, x0 : x0 + width], halo_ref[:, x0 : x0 + width], pad_x, cx_ref, aux
    )
    sig_x = sigmoid(u_x)
    x_conv = u_x * sig_x
    u_bc = conv_rows(
        r_ref[:, bc0 : bc0 + 2 * states], halo_r_ref[:, bc0 : bc0 + 2 * states], pad_bc, cbc_ref, aux
    )
    sig_bc = sigmoid(u_bc)
    bc = (u_bc * sig_bc).astype(BF16)
    keys, query = bc[:, :states], bc[:, states:]
    lower = triangle(rows, False).astype(F32).astype(BF16)
    biased, step, log_decay, cum = head_scalars(r_ref[:, dt0 : dt0 + LANES], par_ref, lower)
    cum_t = cum.T
    last = cum[rows - 1 : rows, :]
    entering = jnp.exp(cum) * aux[:, 7:8]
    leaving = jnp.exp(last - cum) * aux[:, 8:9]
    wide = widen(jnp.concatenate([step, entering, leaving], axis=0), expand_ref)
    step_w, enter_w, leave_w = wide[:rows], wide[rows : 2 * rows], wide[2 * rows :]
    xs = x_conv * step_w
    xs_low = xs.astype(BF16)

    y = y_ref[...]
    z = p_ref[:, :width]
    sig_z = sigmoid(z)
    silu_z = z * sig_z
    gated = y * silu_z
    rstd = aux2_ref[:, 0:1]
    inner = aux2_ref[:, 1:2]
    d_mixed = db_ref[:, db_ref.shape[1] - width :]
    g_mgain = jnp.sum(d_mixed * (gated * rstd), axis=0, keepdims=True)
    d_gated = rstd * (d_mixed * mgain_ref[0:1, :]) - gated * inner
    d_y = d_gated * silu_z
    dp_ref[:, :width] = (d_gated * y * (sig_z * (1.0 + z * (1.0 - sig_z)))).astype(BF16)
    gw_ref[0:1, :] += g_mgain
    gw_ref[1:2, :] += jnp.sum(d_y * x_conv, axis=0, keepdims=True)

    dy_low = d_y.astype(BF16)
    held_low = st_ref[0]
    d_next = d_state[...]
    d_next_low = d_next.astype(BF16)
    entered_dy = (enter_w * d_y).astype(BF16)
    left_xs = (leave_w * xs).astype(BF16)
    from_next = leave_w * dot(keys, d_next_low)
    mask_t = triangle(rows, True) & (aux[:, 0:1] == segr_ref[0:1, :])
    b_dot_c = dot(keys, query, NT)
    lane = lax.broadcasted_iota(jnp.int32, (rows, LANES), 1)
    d_gram = jnp.zeros((rows, rows), F32)
    parts = []
    for pair in range(width // LANES):
        pair_dy = dy_low[:, pair * LANES : (pair + 1) * LANES]
        pair_x = xs_low[:, pair * LANES : (pair + 1) * LANES]
        sides = []
        for e in range(2):
            h = 2 * pair + e
            gap = cum_t[h : h + 1, :] - cum[:, h : h + 1]
            decay = jnp.exp(jnp.where(mask_t, gap, MASK_FILL))
            sides.append(dot((decay * b_dot_c).astype(BF16), pair_dy))
            inside = (lane < P_SIZE) if e == 0 else (lane >= P_SIZE)
            only = jnp.where(inside, pair_x, jnp.zeros_like(pair_x))
            d_gram = d_gram + decay * dot(only, pair_dy, NT)
        parts.append(jnp.where(lane < P_SIZE, sides[0], sides[1]))
    d_xs_inner = jnp.concatenate(parts, axis=1)
    d_xs = d_xs_inner + from_next
    d_gram = d_gram.astype(BF16)
    d_keys = dot(d_gram, query) + dot(left_xs, d_next_low, NT)
    d_query = dot(d_gram, keys, TN) + dot(entered_dy, held_low, NT)
    keep_w = enter_w[rows - 1 : rows, :]
    d_state[...] = dot(query, entered_dy, TN) + keep_w * d_next

    y_scan = y - dskip_ref[0:1, :] * x_conv
    pairs = dy_low.astype(F32) * y_scan - xs_low.astype(F32) * d_xs_inner
    d_cum = by_head(pairs - xs * from_next, reduce_ref)
    at_last = jnp.sum(xs * from_next, axis=0, keepdims=True) + keep_w * jnp.sum(
        held_low.astype(F32) * d_next, axis=0, keepdims=True
    )
    at_last = by_head(jnp.broadcast_to(at_last, (8, width)), reduce_ref)[0:1, :]
    d_log = sums_of(triangle(rows, True).astype(F32).astype(BF16), d_cum) + at_last
    d_step = by_head(x_conv * d_xs, reduce_ref) - d_log * jnp.exp(par_ref[0:1, :])
    d_dt = d_step * sigmoid(biased)
    dr_ref[:, dt0 : dt0 + LANES] = d_dt.astype(BF16)
    gh_ref[0:1, :] += jnp.sum(d_log * log_decay, axis=0, keepdims=True)
    gh_ref[1:2, :] += jnp.sum(d_dt, axis=0, keepdims=True)

    d_ux = (dskip_ref[0:1, :] * d_y + step_w * d_xs) * (sig_x * (1.0 + u_x * (1.0 - sig_x)))
    d_conv = jnp.concatenate([d_keys, d_query], axis=1)
    d_ubc = d_conv * (sig_bc * (1.0 + u_bc * (1.0 - sig_bc)))
    for grad, pad, fut, taps_ref, g_ref, d_ref, c0 in (
        (d_ux, pad_x, fut_x, cx_ref, gcx_ref, dp_ref, x0),
        (d_ubc, pad_bc, fut_bc, cbc_ref, gcbc_ref, dr_ref, bc0),
    ):
        size = grad.shape[1]
        g_ref[3:4, :] += jnp.sum(grad * pad[8 : 8 + rows, :], axis=0, keepdims=True)
        for k in range(1, 4):
            shifted = pad[8 - k : 8 - k + rows, :] * aux[:, k : k + 1]
            g_ref[3 - k : 4 - k, :] += jnp.sum(grad * shifted, axis=0, keepdims=True)
        fut[0:rows, :] = grad
        d_in = taps_ref[3:4, :] * grad
        for k in range(1, 4):
            d_in = d_in + taps_ref[3 - k : 4 - k, :] * (
                fut[k : k + rows, :] * aux[:, 3 + k : 4 + k]
            )
        fut[rows : rows + 8, :] = grad[0:8, :]
        d_ref[:, c0 : c0 + size] = d_in.astype(BF16)
    dr_ref[:, q0 : q0 + dqkv_ref.shape[1]] = dqkv_ref[...]


def head_maps(width):
    expand = (np.arange(width)[None, :] // P_SIZE == np.arange(LANES)[:, None]).astype(np.float32)
    return (
        jnp.asarray(np.concatenate([expand, expand], axis=0), BF16),
        jnp.asarray(expand.T, BF16),
    )


def mamba_specs(chunk, chunk_of, parts, members):
    def place(i):
        return chunk_place(chunk_of(i), parts, members)

    def rows(array):
        return pl.BlockSpec((chunk, array.shape[1]), lambda i: (place(i), 0))

    def fixed(array):
        return pl.BlockSpec(array.shape, lambda i: (0, 0))

    def before(i):
        earlier = chunk_place(jnp.maximum(chunk_of(i) - 1, 0), parts, members)
        return ((earlier + 1) * (chunk // 8) - 1, 0)

    def halo(array):
        return pl.BlockSpec((8, array.shape[1]), before)

    aux = pl.BlockSpec((chunk, LANES), lambda i: (chunk_of(i), 0))
    seg = pl.BlockSpec((8, chunk), lambda i: (0, chunk_of(i)))
    return rows, fixed, halo, aux, seg


def mamba_forward(cols, panel, aux, segr, cx, cbc, par, dskip, mgain, chunk, parts, members):
    length = panel.shape[0]
    width, states = cols["width"], cols["states"]
    chunks = length // chunk
    expand, _ = head_maps(width)
    rows, fixed, halo, by_aux, seg = mamba_specs(chunk, lambda i: i, parts, members)
    small = [cx, cbc, par, dskip, mgain, expand]
    shapes = [
        jax.ShapeDtypeStruct((length, width), BF16),
        jax.ShapeDtypeStruct((length, LANES), F32),
        jax.ShapeDtypeStruct((length, width), F32),
        jax.ShapeDtypeStruct((chunks, states, width), BF16),
    ]
    return pl.pallas_call(
        partial(mamba_forward_kernel, cols),
        grid=(chunks,),
        in_specs=[rows(panel), halo(panel), by_aux, seg] + [fixed(a) for a in small],
        out_specs=[
            rows(shapes[0]),
            rows(shapes[1]),
            rows(shapes[2]),
            pl.BlockSpec((1, states, width), lambda i: (i, 0, 0)),
        ],
        out_shape=shapes,
        scratch_shapes=[
            pltpu.VMEM((states, width), F32),
            pltpu.VMEM((chunk + 8, width), F32),
            pltpu.VMEM((chunk + 8, 2 * states), F32),
        ],
        compiler_params=pltpu.CompilerParams(vmem_limit_bytes=VMEM_LIMIT),
        cost_estimate=pl.CostEstimate(
            flops=20000 * length * width,
            bytes_accessed=4 * (panel.size + 3 * length * width),
            transcendentals=length * width * 4,
        ),
        name="mamba_forward",
    )(panel, panel, aux, segr, *small)


def mamba_backward(
    cols,
    panel,
    aux,
    segr,
    cx,
    cbc,
    par,
    dskip,
    mgain,
    y,
    held,
    d_branch_in,
    aux2,
    d_qkv,
    chunk,
    parts,
    members,
):
    length = panel.shape[0]
    width, states = cols["width"], cols["states"]
    chunks = length // chunk
    expand, reduce = head_maps(width)
    rows, fixed, halo, by_aux, seg = mamba_specs(
        chunk, lambda i: chunks - 1 - i, parts, members
    )
    small = [cx, cbc, par, dskip, mgain, expand, reduce]
    sums = [(8, width), (8, width), (8, 2 * states), (8, LANES)]
    whole = jax.ShapeDtypeStruct(panel.shape, BF16)
    return pl.pallas_call(
        partial(mamba_backward_kernel, cols),
        grid=(chunks,),
        in_specs=[rows(panel), halo(panel), by_aux, seg]
        + [fixed(a) for a in small]
        + [
            rows(y),
            pl.BlockSpec((1, states, width), lambda i: (chunks - 1 - i, 0, 0)),
            rows(d_branch_in),
            rows(aux2),
            rows(d_qkv),
        ],
        out_specs=[rows(whole)] + [pl.BlockSpec(s, lambda i: (0, 0)) for s in sums],
        out_shape=[whole]
        + [jax.ShapeDtypeStruct(s, F32) for s in sums],
        scratch_shapes=[
            pltpu.VMEM((states, width), F32),
            pltpu.VMEM((chunk + 8, width), F32),
            pltpu.VMEM((chunk + 8, 2 * states), F32),
            pltpu.VMEM((chunk + 8, width), F32),
            pltpu.VMEM((chunk + 8, 2 * states), F32),
        ],
        compiler_params=pltpu.CompilerParams(vmem_limit_bytes=VMEM_LIMIT),
        cost_estimate=pl.CostEstimate(
            flops=47000 * length * width,
            bytes_accessed=4 * (panel.size + 3 * length * width),
            transcendentals=length * width * 4,
        ),
        name="mamba_backward",
    )(panel, panel, aux, segr, *small, y, held, d_branch_in, aux2, d_qkv)


def pad_rows(value, rows):
    return jnp.pad(value, ((0, rows - value.shape[0]), (0, 0)))


def segment_tables(segment, chunk):
    length = segment.shape[0]
    seg = segment.astype(F32)
    columns = [seg]
    for k in range(1, 4):
        before = jnp.concatenate([jnp.full((k,), -1.0, F32), seg[:-k]])
        columns.append((before == seg).astype(F32))
    for k in range(1, 4):
        after = jnp.concatenate([seg[k:], jnp.full((k,), -1.0, F32)])
        columns.append((after == seg).astype(F32))
    blocks = seg.reshape(-1, chunk)
    ends = blocks[:, -1:]
    prior = jnp.concatenate([jnp.full((1, 1), -1.0, F32), ends[:-1]], axis=0)
    columns.append((blocks == prior).astype(F32).reshape(-1))
    columns.append((blocks == ends).astype(F32).reshape(-1))
    stacked = jnp.stack(columns + [jnp.zeros_like(seg)] * (16 - len(columns)), axis=0)
    return jnp.pad(stacked.T, ((0, 0), (0, LANES - 16))), jnp.broadcast_to(seg, (8, length))


def rms_factor(hidden):
    return lax.rsqrt(jnp.mean(hidden * hidden, axis=-1, keepdims=True) + NORM_EPS)


def norm_backward(hidden, gain, d_normed, grad_h):
    factor = rms_factor(hidden)
    weighted = gain * d_normed
    inner_mean = jnp.mean(weighted * hidden, axis=-1, keepdims=True)
    return grad_h + factor * weighted - hidden * factor**3 * inner_mean, factor


def after(value, *earlier):
    return lax.optimization_barrier((value, *earlier))[0]


def local(
    inputs,
    cotangent,
    seg_ids,
    norm_gains,
    w_q,
    key_value_weight,
    w_zx,
    w_bc,
    w_dt,
    a_log,
    dt_bias,
    d_skip,
    conv_x,
    conv_bc,
    m_gain,
    w_ao,
    w_mo,
    w_gu,
    w_down,
):
    members = lax.axis_size("dp")
    size_z = lax.axis_size("tensor")
    me_z = lax.axis_index("tensor")
    length = seg_ids.shape[1]
    count, model = inputs.shape[1:]
    block = model // members
    owned = key_value_weight.shape[1]
    heads = w_q.shape[2] // HEAD_SIZE
    kv_head = me_z * heads // (QUERY_HEADS // KEY_VALUE_HEADS)
    width = w_zx.shape[3]
    m_heads = w_dt.shape[2]
    states2 = w_bc.shape[2]
    hidden_units = w_gu.shape[3]
    taps = conv_bc.shape[2]
    gains_own = norm_gains.shape[2]
    cols = {"width": width, "states": states2 // 2, "x": width, "q": 0}
    cols["k"] = cols["q"] + heads * HEAD_SIZE
    cols["v"] = cols["k"] + HEAD_SIZE
    cols["bc"] = cols["v"] + HEAD_SIZE
    cols["dt"] = cols["bc"] + states2
    att_width = heads * HEAD_SIZE
    parts = 2 if count % 256 == 0 else 1
    sub = count // parts
    chunk = sub
    chunks = length // chunk
    late = parts - 1
    places = [(c % parts) * size_z + c // parts for c in range(chunks)]

    def split(value):
        return [value[h * sub : (h + 1) * sub] for h in range(parts)]

    def by_part(value):
        rows = size_z * sub
        return [value[h * rows : (h + 1) * rows] for h in range(parts)]

    lane_rows = 2 * KEY_VALUE_HEADS * HEAD_SIZE + states2
    shared = jnp.concatenate(
        [
            jnp.pad(norm_gains[0], ((0, 0), (0, lane_rows - gains_own))),
            jnp.pad(conv_bc[0], ((0, 10), (0, lane_rows - taps))),
            jnp.concatenate([key_value_weight[0], w_bc[0]], axis=1),
        ],
        axis=0,
    )
    def scatter_dp(value):
        return lax.psum_scatter(value, "dp", scatter_dimension=0, tiled=True)

    def gather_dp(value, *earlier):
        if earlier:
            value = after(value, *earlier)
        return lax.all_gather(value, "dp", axis=0, tiled=True)

    x_parts = split(inputs[0])
    x_first = z_gather_first(x_parts[0])
    shared = z_gather_direct(shared).reshape(size_z, 16 + owned, lane_rows)
    tiny = shared[:, :16]
    shared = shared[:, 16:].reshape(block, lane_rows)
    kv_cols = [
        lax.dynamic_slice_in_dim(shared, (base + kv_head) * HEAD_SIZE, HEAD_SIZE, 1)
        for base in (0, KEY_VALUE_HEADS)
    ]
    panel_rest = jnp.concatenate(
        [w_q[0]]
        + kv_cols
        + [
            shared[:, 2 * KEY_VALUE_HEADS * HEAD_SIZE :],
            jnp.pad(w_dt[0], ((0, 0), (0, LANES - m_heads))),
        ],
        axis=1,
    )
    rest_width = panel_rest.shape[1]
    tiny = jnp.concatenate(
        [
            jnp.swapaxes(tiny[:, :2, :gains_own], 0, 1).reshape(2, block),
            jnp.pad(
                jnp.swapaxes(tiny[:, 2:6, :taps], 0, 1).reshape(4, size_z * taps),
                ((0, 10), (0, block - size_z * taps)),
            ),
        ],
        axis=0,
    )
    panel_rows = jnp.concatenate([w_zx[0].reshape(block, 2 * width), panel_rest], axis=1)
    all_width = panel_rows.shape[1]
    tiny = jnp.pad(tiny, ((0, 0), (0, all_width - block)))
    panel_rows, tiny = ordered((panel_rows, tiny), *x_first)
    panel_rows = jnp.concatenate([panel_rows, tiny], axis=0)
    w_all = gather_dp(panel_rows)
    x_moved = z_gather_parts(x_parts, None, x_first)
    tiny = w_all.reshape(members, block + 16, all_width)[:, block:, :block].astype(F32)
    gains = jnp.swapaxes(tiny[:, :2], 0, 1).reshape(2, model)
    convbc_all = jnp.swapaxes(tiny[:, 2:6, : size_z * taps], 0, 1).reshape(4, states2)
    gain1, gain2 = gains[0:1], gains[1:2]
    w_b = gather_dp(jnp.concatenate([w_ao[0], w_mo[0]], axis=0).T, panel_rows)
    w_cd = jnp.concatenate([w_gu[0].reshape(block, 2 * hidden_units), w_down[0].T], axis=1)
    w_cd = gather_dp(w_cd, panel_rows)

    seg_own, a_own, dtb_own, dskip_own, cx_own, mgain_own = ordered(
        [seg_ids[0], a_log[0], dt_bias[0], d_skip[0], conv_x[0], m_gain[0]], panel_rows
    )
    aux, segr = segment_tables(seg_own, chunk)
    tables = [jnp.asarray(t) for t in rotary_rows(length)]
    cx = pad_rows(cx_own, 8)
    cbc = pad_rows(convbc_all, 8)
    par = jnp.pad(jnp.stack([a_own, dtb_own]), ((0, 6), (0, LANES - m_heads)))
    dskip = jnp.broadcast_to(jnp.repeat(dskip_own, P_SIZE)[None, :], (8, width))
    mgain = jnp.broadcast_to(mgain_own[None, :], (8, width))
    setup = (aux, segr, cx, cbc, par, dskip, mgain)

    held = ()
    d_moved = None
    for h in range(parts):
        x_all = z_place(x_parts[h], x_moved[h])
        held = norm_project(x_all, gain1, w_all, held, h, parts, members)
        if d_moved is None:
            d_moved = z_gather_parts([after(cotangent[0], held[0])])[0]
    normed1, panel = held
    panel = after(panel, *d_moved[0])
    gm, squares, y_out, held = mamba_forward(cols, panel, *setup, chunk, parts, size_z)
    squares = z_sum(squares[:, 0].reshape(-1, LANES)).reshape(length, 1)
    attended = attention_call(
        attention_forward_kernel,
        "attention_forward",
        after(panel, y_out, *d_moved[min(1, size_z - 2)]),
        2 * width + cols["q"],
        heads,
        tables,
        aux,
        segr,
        None,
        att_width,
        [],
        places,
    )
    rstd = lax.rsqrt(squares / (HM * P_SIZE) + NORM_EPS)
    branch = branch_product(attended, gm, rstd, w_b)
    sums, moved = z_scatter_parts(by_part(branch), {(0, size_z - 2): d_moved[-1]})
    x_own = after(inputs[0], branch).astype(F32)
    h_mid, normed2_own = [], []
    for h, x in enumerate(split(x_own)):
        total = sums[h]
        if h:
            total = after(total, normed2_own[h - 1])
        h_mid.append(x + total)
        normed2_own.append((h_mid[h] * rms_factor(h_mid[h]) * gain2).astype(BF16))
    moved = z_gather_parts(normed2_own)
    d_out = [
        z_place(own, [[split(right)[h], split(left)[h]] for right, left in d_moved])
        for h, own in enumerate(split(cotangent[0]))
    ]
    normed2 = [z_place(own, m) for own, m in zip(normed2_own, moved)]
    act, d_gate, d_up = feed_forward(normed2, d_out, w_cd, hidden_units)
    d_norm2 = transposed_product([d_gate, d_up], w_cd, 0)
    first = z_scatter_first(by_part(d_norm2))
    sums, moved = z_scatter_parts(by_part(d_norm2), None, first)
    g_cd, pieces = None, 4
    steps = [first, moved[late][0], moved[0][-1], moved[late][-1]]
    for piece in range(pieces):
        left, right = ordered((normed2, d_out), *steps[piece])
        g_cd = gradient([left, left, right], [d_gate, d_up, act], g_cd, piece, pieces)
    g_cd = scatter_dp(g_cd)
    grad_mid, grad_low = [], []
    for h, part in enumerate(split(cotangent[0])):
        total = sums[h]
        if h:
            total = after(total, grad_low[h - 1])
        grad, _ = norm_backward(h_mid[h], gain2, total, part.astype(F32))
        grad_mid.append(grad)
        grad_low.append(grad.astype(BF16))
    h_mid_all = jnp.concatenate(h_mid, axis=0)
    ffn = transposed_product([after(act, *moved[0][-1])], w_cd, 2)
    if parts > 1:
        ffn = jnp.swapaxes(ffn.reshape(parts, size_z, sub, model), 0, 1).reshape(length, model)
    moved = z_gather_parts(grad_low, {(late, 1): [ffn]})
    d_branch = [z_place(own, m) for own, m in zip(grad_low, moved)]
    ffn = line_scatter([ffn], *moved[late][-1])[0]
    g_c, g_d = g_cd[:, : 2 * hidden_units], g_cd[:, 2 * hidden_units :]

    d_b, inner = branch_back(d_branch, w_b, gm)
    inner = z_sum(inner[:, 0].reshape(-1, LANES)).reshape(length, 1)
    d_qkv = attention_call(
        attention_backward_kernel,
        "attention_backward",
        after(panel, g_cd),
        2 * width + cols["q"],
        heads,
        tables,
        aux,
        segr,
        d_b,
        att_width + 2 * HEAD_SIZE,
        [pltpu.VMEM((length, HEAD_SIZE), F32), pltpu.VMEM((length, HEAD_SIZE), F32)],
        places,
    )
    aux2 = jnp.pad(
        jnp.concatenate([rstd, rstd**3 * inner / (HM * P_SIZE)], axis=1),
        ((0, 0), (0, LANES - 2)),
    )
    d_all, g_wide, g_cx, g_cbc, g_heads = mamba_backward(
        cols, panel, *setup, y_out, held, d_b, aux2, d_qkv, chunk, parts, size_z
    )
    mixed = (after(gm, aux2).astype(F32) * rstd).astype(BF16)
    mixed = jnp.concatenate([attended, mixed], axis=1)
    g_all = gradient([[normed1], d_branch], [d_all, mixed], None, 0, 1)
    d_norm1, low = [], g_all
    for h in range(parts):
        low = back_product(after(d_all, low), w_all, h, parts, members, model)
        d_norm1.append(low)
    low = d_norm1[-1:]
    g_all = scatter_dp(g_all)
    g_zx = g_all[:, : 2 * width].astype(F32)
    g_rest = g_all[:, 2 * width : all_width]
    g_b = g_all[:, all_width:].astype(F32)
    by_dp = [
        g_cbc[:4].reshape(-1, LANES),
        g_heads[0:2],
        jnp.pad(g_wide[1].reshape(m_heads, P_SIZE).sum(axis=1), (0, LANES - m_heads))[None],
        g_cx[:4].reshape(-1, LANES),
        g_wide[0].reshape(-1, LANES),
    ]
    ends = np.cumsum([v.shape[0] for v in by_dp])
    by_dp = jnp.concatenate(by_dp, axis=0)
    by_dp = pad_rows(by_dp, -(-by_dp.shape[0] // 8) * 8)
    by_dp = dp_sum(after(by_dp, *low))
    dp_taps = size_z * taps
    g_convbc = lax.dynamic_slice_in_dim(
        by_dp[: ends[0]].reshape(4, states2), lax.axis_index("dp") * dp_taps, dp_taps, 1
    )
    g_convbc = jnp.pad(
        g_convbc.T.reshape(size_z, taps, 4), ((0, 0), (0, owned - taps), (0, 0))
    ).reshape(block, 4)
    g_alog = by_dp[ends[0] : ends[0] + 1, :m_heads]
    g_dtbias = by_dp[ends[0] + 1 : ends[1], :m_heads]
    g_dskip = by_dp[ends[1] : ends[2], :m_heads]
    g_convx = by_dp[ends[2] : ends[3]].reshape(1, 4, width)
    g_mgain = by_dp[ends[3] : ends[4]].reshape(1, width)

    g_rest = g_rest.astype(F32)
    first = cols["q"]
    gain1_own = jnp.sum(panel_rest.astype(F32) * g_rest, axis=1) + jnp.sum(
        w_zx[0].reshape(block, 2 * width).astype(F32) * g_zx, axis=1
    )
    gain2_own = jnp.sum(
        w_gu[0].reshape(block, 2 * hidden_units).astype(F32) * g_c.astype(F32),
        axis=1,
    )
    mine = lax.axis_index("dp") * block
    gain1_own = gain1_own / lax.dynamic_slice_in_dim(gain1[0], mine, block, 0)
    gain2_own = gain2_own / lax.dynamic_slice_in_dim(gain2[0], mine, block, 0)
    small = jnp.concatenate([gain1_own[:, None], gain2_own[:, None], g_convbc], axis=1)
    g_q = g_rest[:, : cols["k"] - first]
    g_dt = g_rest[:, cols["dt"] - first : cols["dt"] - first + m_heads]
    kv_part = jnp.zeros((block, 2 * KEY_VALUE_HEADS * HEAD_SIZE), F32)
    for base, name in ((0, "k"), (KEY_VALUE_HEADS, "v")):
        at = cols[name] - first
        kv_part = lax.dynamic_update_slice_in_dim(
            kv_part, g_rest[:, at : at + HEAD_SIZE], (base + kv_head) * HEAD_SIZE, 1
        )
    kv_total = 2 * KEY_VALUE_HEADS * HEAD_SIZE
    shared_grad = jnp.concatenate(
        [
            kv_part,
            g_rest[:, cols["bc"] - first : cols["dt"] - first],
            jnp.pad(small, ((0, 0), (0, LANES - small.shape[1]))),
        ],
        axis=1,
    )
    sums, moved = z_scatter_parts(d_norm1, {(late, 1): [ffn]})
    hidden_out = (h_mid_all + ffn).astype(BF16)
    shared_grad = z_scatter_direct(shared_grad.astype(BF16))
    small = shared_grad[:, kv_total + states2 :]
    shared_grad = shared_grad[:, : kv_total + states2]
    g_gains = small[:, :2].T[None]
    g_convbc = small[:taps, 2:6].T[None]
    norm_sum = jnp.concatenate(sums, axis=0)
    grad_in, _ = norm_backward(x_own, gain1, norm_sum, jnp.concatenate(grad_mid, axis=0))
    input_grad = grad_in

    return (
        hidden_out[None],
        input_grad[None],
        g_gains,
        g_q[None],
        shared_grad[None, :, :kv_total],
        g_zx.reshape(1, block, 2, width),
        shared_grad[None, :, kv_total:],
        g_dt[None],
        g_alog,
        g_dtbias,
        g_dskip,
        g_convx,
        g_convbc,
        g_mgain,
        g_b[:, :att_width].T[None],
        g_b[:, att_width:].T[None],
        g_c.astype(F32).reshape(1, block, 2, hidden_units),
        g_d.astype(F32).T[None],
    )


def solution(mesh):
    return jax.shard_map(
        local,
        mesh=mesh,
        in_specs=(
            P("dp", "tensor", None),
            P("dp", "tensor", None),
            P("dp", None),
            P(None, None, ("dp", "tensor")),
            P(None, "dp", "tensor"),
            P(None, ("dp", "tensor"), None),
            P(None, "dp", None, "tensor"),
            P(None, ("dp", "tensor"), None),
            P(None, "dp", "tensor"),
            P(None, "tensor"),
            P(None, "tensor"),
            P(None, "tensor"),
            P(None, None, "tensor"),
            P(None, None, ("dp", "tensor")),
            P(None, "tensor"),
            P(None, "tensor", "dp"),
            P(None, "tensor", "dp"),
            P(None, "dp", None, "tensor"),
            P(None, "tensor", "dp"),
        ),
        out_specs=(
            P("dp", "tensor", None),
            P("dp", "tensor", None),
            P(None, None, ("dp", "tensor")),
            P(None, "dp", "tensor"),
            P(None, ("dp", "tensor"), None),
            P(None, "dp", None, "tensor"),
            P(None, ("dp", "tensor"), None),
            P(None, "dp", "tensor"),
            P(None, "tensor"),
            P(None, "tensor"),
            P(None, "tensor"),
            P(None, None, "tensor"),
            P(None, None, ("dp", "tensor")),
            P(None, "tensor"),
            P(None, "tensor", "dp"),
            P(None, "tensor", "dp"),
            P(None, "dp", None, "tensor"),
            P(None, "tensor", "dp"),
        ),
        check_vma=False,
    )
```

```python
from functools import partial

import jax
import jax.numpy as jnp
import numpy as np
from jax import lax
from jax.experimental import pallas as pl
from jax.experimental.pallas import tpu as pltpu
from jax.sharding import PartitionSpec as P

QUERY_HEADS = 8
KEY_VALUE_HEADS = 2
HEAD_SIZE = 128
HM = 48
P_SIZE = 64
LANES = 128
NORM_EPS = 1e-05
ROPE_BASE = 100000000000.0
MASK_FILL = -1e30
F32 = jnp.float32
BF16 = jnp.bfloat16
NN = (((1,), (0,)), ((), ()))
NT = (((1,), (1,)), ((), ()))
TN = (((0,), (0,)), ((), ()))
VMEM_LIMIT = 48 * 1024 * 1024


def dot(left, right, dims=NN):
    return lax.dot_general(left, right, dims, preferred_element_type=F32)


def sums_of(zero_one, value):
    high = value.astype(BF16)
    value = value - high.astype(F32)
    middle = value.astype(BF16)
    low = (value - middle.astype(F32)).astype(BF16)
    width = value.shape[1]
    out = dot(zero_one, jnp.concatenate([high, middle, low], axis=1))
    return out[:, :width] + out[:, width : 2 * width] + out[:, 2 * width :]


def sigmoid(v):
    return 0.5 * jnp.tanh(0.5 * v) + 0.5


def send_dp(value, mask):
    size = lax.axis_size("dp")
    return lax.ppermute(value, "dp", [(i, i ^ mask) for i in range(size)])


def chip_gather(rows, *earlier):
    chips = lax.axis_size("dp") // 2
    if earlier:
        rows = after(rows, *earlier)
    return [rows] + [send_dp(rows, 2 * k) for k in range(1, chips)]


def core_gather(pieces, *earlier):
    if earlier:
        pieces = ordered(pieces, *earlier)
    chips = len(pieces)
    me = lax.axis_index("dp")
    chip, core = lax.div(me, 2), lax.rem(me, 2)
    rows, width = pieces[0].shape
    mine = jnp.zeros((chips, rows, width), pieces[0].dtype)
    for k, piece in enumerate(pieces):
        mine = lax.dynamic_update_slice(mine, piece[None], (chip ^ k, 0, 0))
    other = send_dp(mine, 1)
    out = jnp.zeros((chips, 2, rows, width), mine.dtype)
    out = lax.dynamic_update_slice(out, mine[:, None], (0, core, 0, 0))
    out = lax.dynamic_update_slice(out, other[:, None], (0, 1 - core, 0, 0))
    return out.reshape(2 * chips * rows, width)


def core_scatter(grad, *earlier):
    chips = lax.axis_size("dp") // 2
    core = lax.rem(lax.axis_index("dp"), 2)
    blocks = grad.reshape(chips, 2, -1, grad.shape[1])
    other = send_dp(lax.dynamic_index_in_dim(blocks, 1 - core, 1, keepdims=False), 1)
    if earlier:
        other = after(other, *earlier)
    mine = lax.dynamic_index_in_dim(blocks, core, 1, keepdims=False)
    return (mine.astype(F32) + other.astype(F32)).astype(grad.dtype)


def chip_scatter(pair):
    chips = pair.shape[0]
    chip = lax.div(lax.axis_index("dp"), 2)
    pieces = [lax.dynamic_index_in_dim(pair, chip, 0, keepdims=False)]
    for k in range(1, chips):
        piece = lax.dynamic_index_in_dim(pair, chip ^ k, 0, keepdims=False)
        pieces.append(send_dp(piece, 2 * k))
    return pieces


def add_up(pieces, *earlier):
    if earlier:
        pieces = ordered(pieces, *earlier)
    total = pieces[0].astype(F32)
    for piece in pieces[1:]:
        total = total + piece.astype(F32)
    return total


def dp_sum(value):
    chips = lax.axis_size("dp") // 2
    value = value + send_dp(value, 1)
    total = value
    for k in range(1, chips):
        total = total + send_dp(value, 2 * k)
    return total


def send_z(value, shift):
    size = lax.axis_size("tensor")
    return lax.ppermute(value, "tensor", [(i, (i + shift) % size) for i in range(size)])


def z_gather_direct(rows):
    size = lax.axis_size("tensor")
    me = lax.axis_index("tensor")
    count = rows.shape[0]
    out = jnp.zeros((size * count,) + rows.shape[1:], rows.dtype)
    pieces = [rows] + [send_z(rows, k) for k in range(1, size)]
    for k, piece in enumerate(pieces):
        out = lax.dynamic_update_slice_in_dim(out, piece, lax.rem(me - k + size, size) * count, 0)
    return out


def z_scatter_direct(total):
    size = lax.axis_size("tensor")
    me = lax.axis_index("tensor")
    count = total.shape[0] // size
    mine = lax.dynamic_slice_in_dim(total, me * count, count, 0).astype(F32)
    for k in range(1, size):
        piece = lax.dynamic_slice_in_dim(total, lax.rem(me + k, size) * count, count, 0)
        mine = mine + send_z(piece, k).astype(F32)
    return mine


def ordered(values, *earlier):
    return lax.optimization_barrier((tuple(values), earlier))[0]


def z_gather_first(rows):
    size = lax.axis_size("tensor")
    right = lax.ppermute(rows, "tensor", [(i, i + 1) for i in range(size - 1)])
    left = lax.ppermute(rows, "tensor", [(i, i - 1) for i in range(1, size)])
    return [right, left]


def z_gather_parts(parts, hooks=None, first=None, in_turn=False):
    size = lax.axis_size("tensor")
    hooks = hooks or {}
    moved = [[] for _ in parts]
    for h, rows in enumerate(parts):
        right = left = rows
        for s in range(size - 1):
            if s == 0 and h == 0 and first is not None:
                right, left = first
                moved[h].append(first)
                continue
            earlier = list(hooks.get((h, s), []))
            if h and in_turn:
                earlier += moved[h - 1][s]
            if s or earlier:
                right, left = ordered((right, left), *earlier)
            right = lax.ppermute(right, "tensor", [(i, i + 1) for i in range(s, size - 1)])
            left = lax.ppermute(left, "tensor", [(i, i - 1) for i in range(1, size - s)])
            moved[h].append([right, left])
    return moved


def line_gather(parts, *earlier):
    out = []
    for part in parts:
        if earlier:
            part = after(part, *earlier)
        out.append(lax.all_gather(part, "tensor", axis=0, tiled=True))
    return out


def line_scatter(parts, *earlier):
    out = []
    for part in parts:
        if earlier:
            part = after(part, *earlier)
        out.append(
            lax.psum_scatter(part, "tensor", scatter_dimension=0, tiled=True).astype(F32)
        )
    return out


def line_sends(parts, *earlier):
    size = lax.axis_size("tensor")
    me = lax.axis_index("tensor")
    count = parts[0].shape[0] // size
    pieces = []
    for k in range(size):
        index = lax.rem(me + k, size) * count
        piece = [lax.dynamic_slice_in_dim(part, index, count, 0) for part in parts]
        piece = jnp.concatenate(piece, axis=0)
        if k:
            if earlier:
                piece = after(piece, *earlier)
            piece = send_z(piece, k)
        pieces.append(piece)
    return pieces


def place_kernel(place_ref, in_ref, out_ref):
    out_ref[...] = in_ref[...]


def z_place(rows, moved):
    size = lax.axis_size("tensor")
    me = lax.axis_index("tensor")
    count, width = rows.shape
    out = pl.pallas_call(
        place_kernel,
        grid_spec=pltpu.PrefetchScalarGridSpec(
            num_scalar_prefetch=1,
            grid=(1,),
            in_specs=[pl.BlockSpec((count, width), lambda i, place_ref: (0, 0))],
            out_specs=pl.BlockSpec((count, width), lambda i, place_ref: (place_ref[0], 0)),
        ),
        out_shape=jax.ShapeDtypeStruct((size * count, width), rows.dtype),
        cost_estimate=pl.CostEstimate(
            flops=0, bytes_accessed=4 * rows.size, transcendentals=0
        ),
        name="place",
    )(me.astype(jnp.int32).reshape(1), rows)
    for d in range(1, size):
        piece = moved[d - 1][0] + moved[size - d - 1][1]
        at = lax.rem(me - d + size, size) * count
        out = lax.dynamic_update_slice_in_dim(out, piece, at, 0)
    return out


def block_of(total, index, size):
    if isinstance(total, list):
        return jnp.concatenate([block_of(t, index, size) for t in total], axis=0)
    count = total.shape[0] // size
    return lax.dynamic_slice_in_dim(total, index * count, count, 0)


def z_rotated(rows, moved):
    size = lax.axis_size("tensor")
    pieces = [moved[d - 1][0] + moved[size - d - 1][1] for d in range(1, size)]
    return jnp.concatenate([rows] + pieces, axis=0)


def z_scatter_first(parts):
    size = lax.axis_size("tensor")
    count = parts[0].shape[0] // size
    right = lax.ppermute(parts[0][count : 2 * count], "tensor", [(0, 1)])
    left = lax.ppermute(parts[0][(size - 1) * count :], "tensor", [(size - 1, size - 2)])
    return [right, left]


def z_scatter_parts(parts, hooks=None, first=None, rotated=False):
    size = lax.axis_size("tensor")
    me = lax.axis_index("tensor")
    hooks = hooks or {}
    sums, moved = [], [[] for _ in parts]
    for h, total in enumerate(parts):

        def part(offset, total=total):
            if rotated:
                count = total.shape[0] // size
                at = (-offset) % size * count
                return total[at : at + count]
            return block_of(total, jnp.clip(me + offset, 0, size - 1), size)

        right = left = None
        for s in range(size - 1):
            if s == 0 and h == 0 and first is not None:
                right, left = first
                moved[h].append(first)
                continue
            d = size - 1 - s
            to_right, to_left = part(d), part(-d)
            if s:
                to_right = (to_right.astype(F32) + right.astype(F32)).astype(BF16)
                to_left = (to_left.astype(F32) + left.astype(F32)).astype(BF16)
            earlier = list(hooks.get((h, s), []))
            if h:
                earlier += moved[h - 1][s]
            to_right, to_left = ordered((to_right, to_left), *earlier)
            right = lax.ppermute(to_right, "tensor", [(i, i + 1) for i in range(s + 1)])
            left = lax.ppermute(to_left, "tensor", [(i, i - 1) for i in range(size - 1 - s, size)])
            moved[h].append([right, left])
        sums.append(part(0).astype(F32) + right.astype(F32) + left.astype(F32))
    return sums, moved


def z_sends(value):
    size = lax.axis_size("tensor")
    return [value] + [send_z(value, k) for k in range(1, size)]


def z_sum(value):
    return sum(z_sends(value))


def tile_of(width):
    return max(t for t in range(LANES, 513, LANES) if width % t == 0)


def norm_project_kernel(members, x_ref, gain_ref, w_ref, *refs):
    normed_ref, out_ref = refs[-2:]
    block, rows = x_ref.shape[1] // members, w_ref.shape[0] // members

    @pl.when(pl.program_id(0) == 0)
    def _():
        x = x_ref[...].astype(F32)
        mean = jnp.sum(x * x, axis=1, keepdims=True) * (1.0 / x.shape[1])
        normed_ref[...] = (x * lax.rsqrt(mean + NORM_EPS) * gain_ref[...]).astype(BF16)

    out = None
    for j in range(members):
        part = dot(
            normed_ref[:, j * block : (j + 1) * block], w_ref[j * rows : j * rows + block, :]
        )
        out = part if out is None else out + part
    out_ref[...] = out


def norm_project(x, gain, weights, held, index, parts, members):
    rows, model = x.shape
    total, width = rows * parts, weights.shape[1]
    tile = tile_of(width)
    return pl.pallas_call(
        partial(norm_project_kernel, members),
        grid=(width // tile,),
        in_specs=[
            pl.BlockSpec((rows, model), lambda j: (0, 0)),
            pl.BlockSpec((1, model), lambda j: (0, 0)),
            pl.BlockSpec((weights.shape[0], tile), lambda j: (0, j)),
        ]
        + [pl.BlockSpec(memory_space=pl.ANY)] * len(held),
        out_specs=[
            pl.BlockSpec((rows, model), lambda j: (index, 0)),
            pl.BlockSpec((rows, tile), lambda j: (index, j)),
        ],
        out_shape=[
            jax.ShapeDtypeStruct((total, model), BF16),
            jax.ShapeDtypeStruct((total, width), F32),
        ],
        input_output_aliases={3: 0, 4: 1} if held else {},
        compiler_params=pltpu.CompilerParams(vmem_limit_bytes=VMEM_LIMIT),
        cost_estimate=pl.CostEstimate(
            flops=2 * rows * model * width,
            bytes_accessed=2 * (rows + width) * model + 4 * rows * width,
            transcendentals=0,
        ),
        name="norm_project",
    )(x, gain, weights, *held)


def gradient_kernel(parts, uses, ranges, *refs):
    out_ref, done_ref = refs[-2:]
    done_ref[...] = jnp.zeros_like(done_ref)
    lefts, rights = refs[: sum(parts)], refs[sum(parts) : sum(parts) + len(uses)]
    turned, at = [], 0
    for number in parts:
        turned.append([left[...].T for left in lefts[at : at + number]])
        at += number
    at = 0
    for use, right, (first, stop) in zip(uses, rights, ranges):
        width = stop - first
        rows = right.shape[0] // parts[use]
        total = None
        for h, left in enumerate(turned[use]):
            part = dot(left, right[h * rows : (h + 1) * rows, first:stop])
            total = part if total is None else total + part
        out_ref[:, at : at + width] = total.astype(BF16)
        at += width


def gradient(lefts, rights, uses, held, piece, pieces, ranges=None):
    model = lefts[0][0].shape[1]
    ranges = ranges or [(0, right.shape[1]) for right in rights]
    width = sum(stop - first for first, stop in ranges)
    tile = min(256, model // pieces)
    steps = model // pieces // tile
    parts = [len(left) for left in lefts]
    flat = [part for left in lefts for part in left]
    held = [] if held is None else [held]
    return pl.pallas_call(
        partial(gradient_kernel, parts, uses, ranges),
        grid=(steps,),
        in_specs=[
            pl.BlockSpec((part.shape[0], tile), lambda j: (0, piece * steps + j)) for part in flat
        ]
        + [pl.BlockSpec(right.shape, lambda j: (0, 0)) for right in rights]
        + [pl.BlockSpec(memory_space=pl.ANY)] * len(held),
        out_specs=[
            pl.BlockSpec((tile, width), lambda j: (piece * steps + j, 0)),
            pl.BlockSpec((8, LANES), lambda j: (0, 0)),
        ],
        out_shape=[
            jax.ShapeDtypeStruct((model, width), BF16),
            jax.ShapeDtypeStruct((8, LANES), F32),
        ],
        input_output_aliases={len(flat) + len(rights): 0} if held else {},
        compiler_params=pltpu.CompilerParams(vmem_limit_bytes=VMEM_LIMIT),
        cost_estimate=pl.CostEstimate(
            flops=2 * rights[0].shape[0] * (model // pieces) * width,
            bytes_accessed=2 * (rights[0].shape[0] * (model + width) + model * width) // pieces,
            transcendentals=0,
        ),
        name="gradient",
    )(*flat, *rights, *held)


def feed_forward_kernel(parts, *refs):
    xs, ds = refs[:parts], refs[parts : 2 * parts]
    gate_ref, up_ref, down_ref, act_ref, d_gate_ref, d_up_ref = refs[2 * parts :]
    for h in range(parts):
        rows = xs[h].shape[0]
        here = slice(h * rows, (h + 1) * rows)
        gate = dot(xs[h][...], gate_ref[...])
        up = dot(xs[h][...], up_ref[...])
        sig_gate = sigmoid(gate)
        silu_gate = gate * sig_gate
        act_ref[here, :] = (silu_gate * up).astype(BF16)
        d_act = dot(ds[h][...], down_ref[...])
        d_gate = d_act * up * (sig_gate * (1.0 + gate * (1.0 - sig_gate)))
        d_gate_ref[here, :] = d_gate.astype(BF16)
        d_up_ref[here, :] = (d_act * silu_gate).astype(BF16)


def feed_forward(normed, d_out, weights, hidden_units):
    parts, (rows, model) = len(normed), normed[0].shape
    tile = min(256, hidden_units)
    steps = hidden_units // tile

    def columns(first):
        return pl.BlockSpec((model, tile), lambda j: (0, first * steps + j))

    whole = pl.BlockSpec((rows, model), lambda j: (0, 0))
    out = jax.ShapeDtypeStruct((rows * parts, hidden_units), BF16)
    return pl.pallas_call(
        partial(feed_forward_kernel, parts),
        grid=(steps,),
        in_specs=[whole] * (2 * parts) + [columns(0), columns(1), columns(2)],
        out_specs=[pl.BlockSpec((rows * parts, tile), lambda j: (0, j))] * 3,
        out_shape=[out] * 3,
        compiler_params=pltpu.CompilerParams(vmem_limit_bytes=VMEM_LIMIT),
        cost_estimate=pl.CostEstimate(
            flops=6 * rows * parts * model * hidden_units,
            bytes_accessed=2 * (2 * rows * parts + 3 * hidden_units) * model,
            transcendentals=rows * parts * hidden_units,
        ),
        name="feed_forward",
    )(*normed, *d_out, weights, weights, weights)


def branch_back_kernel(parts, *refs):
    w_ref, gm_ref, out_ref, inner_ref = refs[parts:]
    first = pl.program_id(0) == 0

    @pl.when(first)
    def _():
        inner_ref[...] = jnp.zeros_like(inner_ref)

    for h in range(parts):
        rows = refs[h].shape[0]
        here = slice(h * rows, (h + 1) * rows)
        out = dot(refs[h][...], w_ref[...])
        out_ref[here, :] = out
        inner = jnp.sum(out * gm_ref[here, :].astype(F32), axis=1, keepdims=True)
        inner_ref[here, :] += jnp.where(first, 0.0, inner)


def branch_back(d_branch, weights, gm):
    parts, (rows, model) = len(d_branch), d_branch[0].shape
    tile = weights.shape[1] - gm.shape[1]
    steps = weights.shape[1] // tile
    total = rows * parts
    return pl.pallas_call(
        partial(branch_back_kernel, parts),
        grid=(steps,),
        in_specs=[pl.BlockSpec((rows, model), lambda j: (0, 0))] * parts
        + [
            pl.BlockSpec((model, tile), lambda j: (0, j)),
            pl.BlockSpec((total, tile), lambda j: (0, jnp.maximum(j - 1, 0))),
        ],
        out_specs=[
            pl.BlockSpec((total, tile), lambda j: (0, j)),
            pl.BlockSpec((total, LANES), lambda j: (0, 0)),
        ],
        out_shape=[
            jax.ShapeDtypeStruct((total, weights.shape[1]), F32),
            jax.ShapeDtypeStruct((total, LANES), F32),
        ],
        compiler_params=pltpu.CompilerParams(vmem_limit_bytes=VMEM_LIMIT),
        cost_estimate=pl.CostEstimate(
            flops=2 * total * model * weights.shape[1],
            bytes_accessed=2 * (total + weights.shape[1]) * model,
            transcendentals=0,
        ),
        name="branch_back",
    )(*d_branch, weights, gm)


def put_parts(out, refs):
    rows = out.shape[0] // len(refs)
    for h, ref in enumerate(refs):
        ref[...] = out[h * rows : (h + 1) * rows]


def transposed_kernel(count, *refs):
    out = None
    for left, right in zip(refs[:count], refs[count : 2 * count]):
        part = dot(left[...], right[...], NT)
        out = part if out is None else out + part
    put_parts(out.astype(BF16), refs[2 * count :])


def transposed_product(lefts, weights, first, parts):
    rows, width = lefts[0].shape
    model = weights.shape[0]
    tile = min(512, model)
    count = len(lefts)

    def columns(k):
        return pl.BlockSpec((tile, width), lambda j: (j, first + k))

    return pl.pallas_call(
        partial(transposed_kernel, count),
        grid=(model // tile,),
        in_specs=[pl.BlockSpec((rows, width), lambda j: (0, 0))] * count
        + [columns(k) for k in range(count)],
        out_specs=[pl.BlockSpec((rows // parts, tile), lambda j: (0, j))] * parts,
        out_shape=[jax.ShapeDtypeStruct((rows // parts, model), BF16)] * parts,
        compiler_params=pltpu.CompilerParams(vmem_limit_bytes=VMEM_LIMIT),
        cost_estimate=pl.CostEstimate(
            flops=2 * rows * model * width * count,
            bytes_accessed=2 * ((rows + model) * width * count + rows * model),
            transcendentals=0,
        ),
        name="transposed_product",
    )(*lefts, *([weights] * count))


def branch_kernel(att_ref, gm_ref, rstd_ref, w_ref, *out_refs):
    split = att_ref.shape[1]
    out = dot(att_ref[...], w_ref[:, :split], NT)
    out = out + rstd_ref[...] * dot(gm_ref[...], w_ref[:, split:], NT)
    put_parts(out.astype(BF16), out_refs)


def branch_product(attended, gm, rstd, weights, parts):
    rows = attended.shape[0]
    model, width = weights.shape
    tile = min(512, model)

    def whole(array):
        return pl.BlockSpec(array.shape, lambda j: (0, 0))

    return pl.pallas_call(
        branch_kernel,
        grid=(model // tile,),
        in_specs=[
            whole(attended),
            whole(gm),
            whole(rstd),
            pl.BlockSpec((tile, width), lambda j: (j, 0)),
        ],
        out_specs=[pl.BlockSpec((rows // parts, tile), lambda j: (0, j))] * parts,
        out_shape=[jax.ShapeDtypeStruct((rows // parts, model), BF16)] * parts,
        compiler_params=pltpu.CompilerParams(vmem_limit_bytes=VMEM_LIMIT),
        cost_estimate=pl.CostEstimate(
            flops=2 * rows * model * width,
            bytes_accessed=2 * ((rows + model) * width + rows * model),
            transcendentals=0,
        ),
        name="branch",
    )(attended, gm, rstd, weights)


def back_kernel(block, d_ref, w_ref, out_ref):
    count = out_ref.shape[1] // block
    rows = w_ref.shape[0] // count
    for k in range(count):
        out = dot(d_ref[...], w_ref[k * rows : k * rows + block, :], NT)
        out_ref[:, k * block : (k + 1) * block] = out.astype(BF16)


def back_product(d_all, weights, index, parts, members, model):
    rows, block = d_all.shape[0] // parts, model // members
    each = 2
    return pl.pallas_call(
        partial(back_kernel, block),
        grid=(members // each,),
        in_specs=[
            pl.BlockSpec((rows, d_all.shape[1]), lambda j: (index, 0)),
            pl.BlockSpec((each * weights.shape[0] // members, weights.shape[1]), lambda j: (j, 0)),
        ],
        out_specs=pl.BlockSpec((rows, each * block), lambda j: (0, j)),
        out_shape=jax.ShapeDtypeStruct((rows, model), BF16),
        compiler_params=pltpu.CompilerParams(vmem_limit_bytes=VMEM_LIMIT),
        cost_estimate=pl.CostEstimate(
            flops=2 * rows * model * d_all.shape[1],
            bytes_accessed=2 * (rows * d_all.shape[1] + weights.size + rows * model),
            transcendentals=0,
        ),
        name="back_product",
    )(d_all, weights)


def rotary_rows(length):
    half = HEAD_SIZE // 2
    freqs = np.float32(ROPE_BASE) ** (
        -np.arange(half).astype(np.float32) * np.float32(2.0) / np.float32(HEAD_SIZE)
    )
    angles = np.arange(length).astype(np.float32)[:, None] * freqs.astype(np.float32)[None, :]
    cosine, sine = np.cos(angles), np.sin(angles)
    return (
        np.concatenate([cosine, cosine], axis=1).astype(np.float32),
        np.concatenate([-sine, sine], axis=1).astype(np.float32),
    )


def rotate(value, cosine, sine):
    return value * cosine + pltpu.roll(value, HEAD_SIZE // 2, 1) * sine


def chunk_place(index, parts, members):
    return lax.rem(index, parts) * members + lax.div(index, parts)


def in_sequence(ref, places, rows, columns=slice(None)):
    return jnp.concatenate([ref[p * rows : (p + 1) * rows, columns] for p in places], axis=0)


def attention_probs(q_ref, keys, cos_ref, sin_ref, allowed, start, stop, places, rows):
    here = places[start // rows : stop // rows]
    query = in_sequence(q_ref, here, rows)
    query = rotate(query, cos_ref[start:stop, :], sin_ref[start:stop, :]).astype(BF16)
    scores = dot(query, keys, NT) * (HEAD_SIZE**-0.5)
    scores = jnp.where(allowed, scores, MASK_FILL)
    raised = jnp.exp(scores - jnp.max(scores, axis=1, keepdims=True))
    return query, raised * (1.0 / jnp.sum(raised, axis=1, keepdims=True))


def attention_mask(aux_ref, segr_ref, start, stop):
    rows = start + lax.broadcasted_iota(jnp.int32, (stop - start, stop), 0)
    cols = lax.broadcasted_iota(jnp.int32, (stop - start, stop), 1)
    return (aux_ref[start:stop, 0:1] == segr_ref[0:1, :stop]) & (rows >= cols)


def attention_forward_kernel(heads, block, places, *refs):
    q_refs = refs[:heads]
    k_ref, v_ref, cos_ref, sin_ref, aux_ref, segr_ref, out_ref = refs[heads:]
    length = k_ref.shape[0]
    rows = length // len(places)
    keys = rotate(in_sequence(k_ref, places, rows), cos_ref[...], sin_ref[...]).astype(BF16)
    vals = in_sequence(v_ref, places, rows).astype(BF16)
    for start in range(0, length, block):
        stop = start + block
        allowed = attention_mask(aux_ref, segr_ref, start, stop)
        for h in range(heads):
            _, probs = attention_probs(
                q_refs[h], keys[:stop], cos_ref, sin_ref, allowed, start, stop, places, rows
            )
            out = dot(probs.astype(BF16), vals[:stop]).astype(BF16)
            columns = slice(h * HEAD_SIZE, (h + 1) * HEAD_SIZE)
            for c in range(block // rows):
                p = places[start // rows + c]
                out_ref[p * rows : (p + 1) * rows, columns] = out[c * rows : (c + 1) * rows]


def attention_backward_kernel(heads, block, places, *refs):
    q_refs = refs[:heads]
    k_ref, v_ref, cos_ref, sin_ref, aux_ref, segr_ref, do_ref, out_ref, dk, dv = refs[heads:]
    length = k_ref.shape[0]
    rows = length // len(places)
    scale = HEAD_SIZE**-0.5
    keys = rotate(in_sequence(k_ref, places, rows), cos_ref[...], sin_ref[...]).astype(BF16)
    vals = in_sequence(v_ref, places, rows).astype(BF16)
    dk[...] = jnp.zeros_like(dk)
    dv[...] = jnp.zeros_like(dv)
    for start in range(0, length, block):
        stop = start + block
        allowed = attention_mask(aux_ref, segr_ref, start, stop)
        here = places[start // rows : stop // rows]
        for h in range(heads):
            columns = slice(h * HEAD_SIZE, (h + 1) * HEAD_SIZE)
            query, probs = attention_probs(
                q_refs[h], keys[:stop], cos_ref, sin_ref, allowed, start, stop, places, rows
            )
            given = in_sequence(do_ref, here, rows, columns).astype(BF16)
            d_probs = dot(given, vals[:stop], NT)
            delta = jnp.sum(probs * d_probs, axis=1, keepdims=True)
            d_scores = (probs * (d_probs - delta)).astype(BF16)
            d_query = dot(d_scores, keys[:stop]) * scale
            d_query = rotate(d_query, cos_ref[start:stop, :], -sin_ref[start:stop, :]).astype(BF16)
            for c, p in enumerate(here):
                out_ref[p * rows : (p + 1) * rows, columns] = d_query[c * rows : (c + 1) * rows]
            dk[:stop, :] += dot(d_scores, query, TN)
            dv[:stop, :] += dot(probs.astype(BF16), given, TN)
    d_keys = rotate(dk[...] * scale, cos_ref[...], -sin_ref[...]).astype(BF16)
    d_vals = dv[...].astype(BF16)
    for c, p in enumerate(places):
        there = slice(p * rows, (p + 1) * rows)
        out_ref[there, heads * HEAD_SIZE : (heads + 1) * HEAD_SIZE] = d_keys[
            c * rows : (c + 1) * rows
        ]
        out_ref[there, (heads + 1) * HEAD_SIZE :] = d_vals[c * rows : (c + 1) * rows]


def attention_call(
    kernel, name, panel, first, heads, tables, aux, segr, extra, width, scratch, places
):
    length = panel.shape[0]

    def column(index):
        return pl.BlockSpec((length, HEAD_SIZE), lambda i: (0, index))

    def whole(array):
        return pl.BlockSpec(array.shape, lambda i: (0, 0))

    specs = [column(first // HEAD_SIZE + h) for h in range(heads + 2)]
    operands = [*tables, aux, segr]
    specs += [whole(a) for a in operands]
    if extra is not None:
        specs.append(pl.BlockSpec((length, heads * HEAD_SIZE), lambda i: (0, 0)))
        operands.append(extra)
    return pl.pallas_call(
        partial(kernel, heads, min(256, length), places),
        grid=(1,),
        in_specs=specs,
        out_specs=pl.BlockSpec((length, width), lambda i: (0, 0)),
        out_shape=jax.ShapeDtypeStruct((length, width), BF16),
        scratch_shapes=scratch,
        compiler_params=pltpu.CompilerParams(vmem_limit_bytes=VMEM_LIMIT),
        cost_estimate=pl.CostEstimate(
            flops=(5000 if extra is not None else 3300) * heads * length * length,
            bytes_accessed=4 * length * 12 * HEAD_SIZE,
            transcendentals=heads * length * length,
        ),
        name=name,
    )(*([panel] * (heads + 2)), *operands)


def split_pair(value):
    high = value.astype(BF16)
    return high, (value - high.astype(F32)).astype(BF16)


def widen(value, expand_ref):
    high, rest = split_pair(value)
    return dot(jnp.concatenate([high, rest], axis=1), expand_ref[...])


def by_head(value, reduce_ref):
    high, rest = split_pair(value)
    return dot(high, reduce_ref[...]) + dot(rest, reduce_ref[...])


def conv_rows(current, halo, pad, taps_ref, aux):
    rows = current.shape[0]
    pad[0:8, :] = halo
    pad[8 : 8 + rows, :] = current
    out = taps_ref[3:4, :] * current
    for k in range(1, 4):
        out = out + taps_ref[3 - k : 4 - k, :] * (pad[8 - k : 8 - k + rows, :] * aux[:, k : k + 1])
    return out


def head_scalars(dt_raw, par_ref, lower):
    biased = dt_raw + par_ref[1:2, :]
    step = jnp.maximum(biased, 0.0) + jnp.log1p(jnp.exp(-jnp.abs(biased)))
    log_decay = -step * jnp.exp(par_ref[0:1, :])
    cumulative = sums_of(lower, log_decay)
    return biased, step, log_decay, cumulative


def triangle(rows, flip):
    i = lax.broadcasted_iota(jnp.int32, (rows, rows), 0)
    j = lax.broadcasted_iota(jnp.int32, (rows, rows), 1)
    return (i <= j) if flip else (i >= j)


def mamba_forward_kernel(
    cols,
    p_ref,
    halo_ref,
    aux_ref,
    segr_ref,
    cx_ref,
    cbc_ref,
    par_ref,
    dskip_ref,
    mgain_ref,
    expand_ref,
    gm_ref,
    sq_ref,
    y_ref,
    st_ref,
    state,
    pad_x,
    pad_bc,
):
    width, states = cols["width"], cols["states"]
    rows = p_ref.shape[0]
    r_ref, halo_r_ref = p_ref.at[:, 2 * width :], halo_ref.at[:, 2 * width :]
    x0, bc0, dt0 = cols["x"], cols["bc"], cols["dt"]

    @pl.when(pl.program_id(0) == 0)
    def _():
        state[...] = jnp.zeros_like(state)

    aux = aux_ref[...]
    u_x = conv_rows(
        p_ref[:, x0 : x0 + width], halo_ref[:, x0 : x0 + width], pad_x, cx_ref, aux
    )
    x_conv = u_x * sigmoid(u_x)
    u_bc = conv_rows(
        r_ref[:, bc0 : bc0 + 2 * states], halo_r_ref[:, bc0 : bc0 + 2 * states], pad_bc, cbc_ref, aux
    )
    bc = (u_bc * sigmoid(u_bc)).astype(BF16)
    keys, query = bc[:, :states], bc[:, states:]
    lower = triangle(rows, False)
    _, step, _, cum = head_scalars(
        r_ref[:, dt0 : dt0 + LANES], par_ref, lower.astype(F32).astype(BF16)
    )
    cum_t = cum.T
    last = cum[rows - 1 : rows, :]
    entering = jnp.exp(cum) * aux[:, 7:8]
    leaving = jnp.exp(last - cum) * aux[:, 8:9]
    wide = widen(jnp.concatenate([step, entering, leaving], axis=0), expand_ref)
    step_w, enter_w, leave_w = wide[:rows], wide[rows : 2 * rows], wide[2 * rows :]
    xs = x_conv * step_w
    xs_low = xs.astype(BF16)
    mask = lower & (aux[:, 0:1] == segr_ref[0:1, :])
    c_dot_b = dot(query, keys, NT)
    held = state[...]
    held_low = held.astype(BF16)
    st_ref[0] = held_low
    carried = dot(query, held_low) * enter_w
    lane = lax.broadcasted_iota(jnp.int32, (rows, LANES), 1)
    parts = []
    for pair in range(width // LANES):
        pair_x = xs_low[:, pair * LANES : (pair + 1) * LANES]
        both = []
        for h in (2 * pair, 2 * pair + 1):
            gap = cum[:, h : h + 1] - cum_t[h : h + 1, :]
            decay = jnp.exp(jnp.where(mask, gap, MASK_FILL))
            both.append((decay * c_dot_b).astype(BF16))
        both = dot(jnp.concatenate(both, axis=0), pair_x)
        parts.append(jnp.where(lane < P_SIZE, both[:rows], both[rows:]))
    y = jnp.concatenate(parts, axis=1) + carried + dskip_ref[0:1, :] * x_conv
    state[...] = held * enter_w[rows - 1 : rows, :] + dot(
        keys, (leave_w * xs).astype(BF16), TN
    )
    z = p_ref[:, :width]
    gated = y * (z * sigmoid(z))
    y_ref[...] = y
    gm_ref[...] = (gated * mgain_ref[0:1, :]).astype(BF16)
    sq_ref[...] = jnp.broadcast_to(jnp.sum(gated * gated, axis=1, keepdims=True), sq_ref.shape)


def mamba_backward_kernel(
    cols,
    p_ref,
    halo_ref,
    aux_ref,
    segr_ref,
    cx_ref,
    cbc_ref,
    par_ref,
    dskip_ref,
    mgain_ref,
    expand_ref,
    reduce_ref,
    y_ref,
    st_ref,
    db_ref,
    aux2_ref,
    dqkv_ref,
    da_ref,
    gw_ref,
    gcx_ref,
    gcbc_ref,
    gh_ref,
    d_state,
    pad_x,
    pad_bc,
    fut_x,
    fut_bc,
):
    width, states = cols["width"], cols["states"]
    rows = p_ref.shape[0]
    r_ref, halo_r_ref = p_ref.at[:, 2 * width :], halo_ref.at[:, 2 * width :]
    x0, q0, bc0, dt0 = cols["x"], cols["q"], cols["bc"], cols["dt"]
    dp_ref = da_ref.at[:, : 2 * width]
    dr_ref = da_ref.at[:, 2 * width :]
    first_step = pl.program_id(0) == 0

    @pl.when(first_step)
    def _():
        d_state[...] = jnp.zeros_like(d_state)
        gw_ref[...] = jnp.zeros_like(gw_ref)
        gcx_ref[...] = jnp.zeros_like(gcx_ref)
        gcbc_ref[...] = jnp.zeros_like(gcbc_ref)
        gh_ref[...] = jnp.zeros_like(gh_ref)
        fut_x[...] = jnp.zeros_like(fut_x)
        fut_bc[...] = jnp.zeros_like(fut_bc)

    aux = aux_ref[...]
    u_x = conv_rows(
        p_ref[:, x0 : x0 + width], halo_ref[:, x0 : x0 + width], pad_x, cx_ref, aux
    )
    sig_x = sigmoid(u_x)
    x_conv = u_x * sig_x
    u_bc = conv_rows(
        r_ref[:, bc0 : bc0 + 2 * states], halo_r_ref[:, bc0 : bc0 + 2 * states], pad_bc, cbc_ref, aux
    )
    sig_bc = sigmoid(u_bc)
    bc = (u_bc * sig_bc).astype(BF16)
    keys, query = bc[:, :states], bc[:, states:]
    lower = triangle(rows, False).astype(F32).astype(BF16)
    biased, step, log_decay, cum = head_scalars(r_ref[:, dt0 : dt0 + LANES], par_ref, lower)
    cum_t = cum.T
    last = cum[rows - 1 : rows, :]
    entering = jnp.exp(cum) * aux[:, 7:8]
    leaving = jnp.exp(last - cum) * aux[:, 8:9]
    wide = widen(jnp.concatenate([step, entering, leaving], axis=0), expand_ref)
    step_w, enter_w, leave_w = wide[:rows], wide[rows : 2 * rows], wide[2 * rows :]
    xs = x_conv * step_w
    xs_low = xs.astype(BF16)

    y = y_ref[...]
    z = p_ref[:, :width]
    sig_z = sigmoid(z)
    silu_z = z * sig_z
    gated = y * silu_z
    rstd = aux2_ref[:, 0:1]
    inner = aux2_ref[:, 1:2]
    d_mixed = db_ref[:, db_ref.shape[1] - width :]
    g_mgain = jnp.sum(d_mixed * (gated * rstd), axis=0, keepdims=True)
    d_gated = rstd * (d_mixed * mgain_ref[0:1, :]) - gated * inner
    d_y = d_gated * silu_z
    dp_ref[:, :width] = (d_gated * y * (sig_z * (1.0 + z * (1.0 - sig_z)))).astype(BF16)
    gw_ref[0:1, :] += g_mgain
    gw_ref[1:2, :] += jnp.sum(d_y * x_conv, axis=0, keepdims=True)

    dy_low = d_y.astype(BF16)
    held_low = st_ref[0]
    d_next = d_state[...]
    d_next_low = d_next.astype(BF16)
    entered_dy = (enter_w * d_y).astype(BF16)
    left_xs = (leave_w * xs).astype(BF16)
    from_next = leave_w * dot(keys, d_next_low)
    mask_t = triangle(rows, True) & (aux[:, 0:1] == segr_ref[0:1, :])
    b_dot_c = dot(keys, query, NT)
    lane = lax.broadcasted_iota(jnp.int32, (rows, LANES), 1)
    d_gram = jnp.zeros((rows, rows), F32)
    parts = []
    for pair in range(width // LANES):
        pair_dy = dy_low[:, pair * LANES : (pair + 1) * LANES]
        pair_x = xs_low[:, pair * LANES : (pair + 1) * LANES]
        none = jnp.zeros_like(pair_x)
        only = [jnp.where(lane < P_SIZE, pair_x, none), jnp.where(lane < P_SIZE, none, pair_x)]
        products = dot(jnp.concatenate(only, axis=0), pair_dy, NT)
        both = []
        for e, h in enumerate((2 * pair, 2 * pair + 1)):
            gap = cum_t[h : h + 1, :] - cum[:, h : h + 1]
            decay = jnp.exp(jnp.where(mask_t, gap, MASK_FILL))
            both.append((decay * b_dot_c).astype(BF16))
            d_gram = d_gram + decay * products[e * rows : (e + 1) * rows]
        both = dot(jnp.concatenate(both, axis=0), pair_dy)
        parts.append(jnp.where(lane < P_SIZE, both[:rows], both[rows:]))
    d_xs_inner = jnp.concatenate(parts, axis=1)
    d_xs = d_xs_inner + from_next
    d_gram = d_gram.astype(BF16)
    d_keys = dot(d_gram, query) + dot(left_xs, d_next_low, NT)
    d_query = dot(d_gram, keys, TN) + dot(entered_dy, held_low, NT)
    keep_w = enter_w[rows - 1 : rows, :]
    d_state[...] = dot(query, entered_dy, TN) + keep_w * d_next

    y_scan = y - dskip_ref[0:1, :] * x_conv
    pairs = dy_low.astype(F32) * y_scan - xs_low.astype(F32) * d_xs_inner
    d_cum = by_head(pairs - xs * from_next, reduce_ref)
    at_last = jnp.sum(xs * from_next, axis=0, keepdims=True) + keep_w * jnp.sum(
        held_low.astype(F32) * d_next, axis=0, keepdims=True
    )
    at_last = by_head(jnp.broadcast_to(at_last, (8, width)), reduce_ref)[0:1, :]
    d_log = sums_of(triangle(rows, True).astype(F32).astype(BF16), d_cum) + at_last
    d_step = by_head(x_conv * d_xs, reduce_ref) - d_log * jnp.exp(par_ref[0:1, :])
    d_dt = d_step * sigmoid(biased)
    dr_ref[:, dt0 : dt0 + LANES] = d_dt.astype(BF16)
    gh_ref[0:1, :] += jnp.sum(d_log * log_decay, axis=0, keepdims=True)
    gh_ref[1:2, :] += jnp.sum(d_dt, axis=0, keepdims=True)

    d_ux = (dskip_ref[0:1, :] * d_y + step_w * d_xs) * (sig_x * (1.0 + u_x * (1.0 - sig_x)))
    d_conv = jnp.concatenate([d_keys, d_query], axis=1)
    d_ubc = d_conv * (sig_bc * (1.0 + u_bc * (1.0 - sig_bc)))
    for grad, pad, fut, taps_ref, g_ref, d_ref, c0 in (
        (d_ux, pad_x, fut_x, cx_ref, gcx_ref, dp_ref, x0),
        (d_ubc, pad_bc, fut_bc, cbc_ref, gcbc_ref, dr_ref, bc0),
    ):
        size = grad.shape[1]
        g_ref[3:4, :] += jnp.sum(grad * pad[8 : 8 + rows, :], axis=0, keepdims=True)
        for k in range(1, 4):
            shifted = pad[8 - k : 8 - k + rows, :] * aux[:, k : k + 1]
            g_ref[3 - k : 4 - k, :] += jnp.sum(grad * shifted, axis=0, keepdims=True)
        fut[0:rows, :] = grad
        d_in = taps_ref[3:4, :] * grad
        for k in range(1, 4):
            d_in = d_in + taps_ref[3 - k : 4 - k, :] * (
                fut[k : k + rows, :] * aux[:, 3 + k : 4 + k]
            )
        fut[rows : rows + 8, :] = grad[0:8, :]
        d_ref[:, c0 : c0 + size] = d_in.astype(BF16)
    dr_ref[:, q0 : q0 + dqkv_ref.shape[1]] = dqkv_ref[...]


def head_maps(width):
    expand = (np.arange(width)[None, :] // P_SIZE == np.arange(LANES)[:, None]).astype(np.float32)
    return (
        jnp.asarray(np.concatenate([expand, expand], axis=0), BF16),
        jnp.asarray(expand.T, BF16),
    )


def mamba_specs(chunk, chunk_of, parts, members):
    def place(i):
        return chunk_place(chunk_of(i), parts, members)

    def rows(array):
        return pl.BlockSpec((chunk, array.shape[1]), lambda i: (place(i), 0))

    def fixed(array):
        return pl.BlockSpec(array.shape, lambda i: (0, 0))

    def before(i):
        earlier = chunk_place(jnp.maximum(chunk_of(i) - 1, 0), parts, members)
        return ((earlier + 1) * (chunk // 8) - 1, 0)

    def halo(array):
        return pl.BlockSpec((8, array.shape[1]), before)

    aux = pl.BlockSpec((chunk, LANES), lambda i: (chunk_of(i), 0))
    seg = pl.BlockSpec((8, chunk), lambda i: (0, chunk_of(i)))
    return rows, fixed, halo, aux, seg


def mamba_forward(cols, panel, aux, segr, cx, cbc, par, dskip, mgain, chunk, parts, members):
    length = panel.shape[0]
    width, states = cols["width"], cols["states"]
    chunks = length // chunk
    expand, _ = head_maps(width)
    rows, fixed, halo, by_aux, seg = mamba_specs(chunk, lambda i: i, parts, members)
    small = [cx, cbc, par, dskip, mgain, expand]
    shapes = [
        jax.ShapeDtypeStruct((length, width), BF16),
        jax.ShapeDtypeStruct((length, LANES), F32),
        jax.ShapeDtypeStruct((length, width), F32),
        jax.ShapeDtypeStruct((chunks, states, width), BF16),
    ]
    return pl.pallas_call(
        partial(mamba_forward_kernel, cols),
        grid=(chunks,),
        in_specs=[rows(panel), halo(panel), by_aux, seg] + [fixed(a) for a in small],
        out_specs=[
            rows(shapes[0]),
            rows(shapes[1]),
            rows(shapes[2]),
            pl.BlockSpec((1, states, width), lambda i: (i, 0, 0)),
        ],
        out_shape=shapes,
        scratch_shapes=[
            pltpu.VMEM((states, width), F32),
            pltpu.VMEM((chunk + 8, width), F32),
            pltpu.VMEM((chunk + 8, 2 * states), F32),
        ],
        compiler_params=pltpu.CompilerParams(vmem_limit_bytes=VMEM_LIMIT),
        cost_estimate=pl.CostEstimate(
            flops=20000 * length * width,
            bytes_accessed=4 * (panel.size + 3 * length * width),
            transcendentals=length * width * 4,
        ),
        name="mamba_forward",
    )(panel, panel, aux, segr, *small)


def mamba_backward(
    cols,
    panel,
    aux,
    segr,
    cx,
    cbc,
    par,
    dskip,
    mgain,
    y,
    held,
    d_branch_in,
    aux2,
    d_qkv,
    chunk,
    parts,
    members,
):
    length = panel.shape[0]
    width, states = cols["width"], cols["states"]
    chunks = length // chunk
    expand, reduce = head_maps(width)
    rows, fixed, halo, by_aux, seg = mamba_specs(
        chunk, lambda i: chunks - 1 - i, parts, members
    )
    small = [cx, cbc, par, dskip, mgain, expand, reduce]
    sums = [(8, width), (8, width), (8, 2 * states), (8, LANES)]
    whole = jax.ShapeDtypeStruct(panel.shape, BF16)
    return pl.pallas_call(
        partial(mamba_backward_kernel, cols),
        grid=(chunks,),
        in_specs=[rows(panel), halo(panel), by_aux, seg]
        + [fixed(a) for a in small]
        + [
            rows(y),
            pl.BlockSpec((1, states, width), lambda i: (chunks - 1 - i, 0, 0)),
            rows(d_branch_in),
            rows(aux2),
            rows(d_qkv),
        ],
        out_specs=[rows(whole)] + [pl.BlockSpec(s, lambda i: (0, 0)) for s in sums],
        out_shape=[whole]
        + [jax.ShapeDtypeStruct(s, F32) for s in sums],
        scratch_shapes=[
            pltpu.VMEM((states, width), F32),
            pltpu.VMEM((chunk + 8, width), F32),
            pltpu.VMEM((chunk + 8, 2 * states), F32),
            pltpu.VMEM((chunk + 8, width), F32),
            pltpu.VMEM((chunk + 8, 2 * states), F32),
        ],
        compiler_params=pltpu.CompilerParams(vmem_limit_bytes=VMEM_LIMIT),
        cost_estimate=pl.CostEstimate(
            flops=47000 * length * width,
            bytes_accessed=4 * (panel.size + 3 * length * width),
            transcendentals=length * width * 4,
        ),
        name="mamba_backward",
    )(panel, panel, aux, segr, *small, y, held, d_branch_in, aux2, d_qkv)


def pad_rows(value, rows):
    return jnp.pad(value, ((0, rows - value.shape[0]), (0, 0)))


def segment_tables(segment, chunk):
    length = segment.shape[0]
    seg = segment.astype(F32)
    columns = [seg]
    for k in range(1, 4):
        before = jnp.concatenate([jnp.full((k,), -1.0, F32), seg[:-k]])
        columns.append((before == seg).astype(F32))
    for k in range(1, 4):
        after = jnp.concatenate([seg[k:], jnp.full((k,), -1.0, F32)])
        columns.append((after == seg).astype(F32))
    blocks = seg.reshape(-1, chunk)
    ends = blocks[:, -1:]
    prior = jnp.concatenate([jnp.full((1, 1), -1.0, F32), ends[:-1]], axis=0)
    columns.append((blocks == prior).astype(F32).reshape(-1))
    columns.append((blocks == ends).astype(F32).reshape(-1))
    stacked = jnp.stack(columns + [jnp.zeros_like(seg)] * (16 - len(columns)), axis=0)
    return jnp.pad(stacked.T, ((0, 0), (0, LANES - 16))), jnp.broadcast_to(seg, (8, length))


def rms_factor(hidden):
    return lax.rsqrt(jnp.mean(hidden * hidden, axis=-1, keepdims=True) + NORM_EPS)


def norm_backward(hidden, gain, d_normed, grad_h):
    factor = rms_factor(hidden)
    weighted = gain * d_normed
    inner_mean = jnp.mean(weighted * hidden, axis=-1, keepdims=True)
    return grad_h + factor * weighted - hidden * factor**3 * inner_mean, factor


def after(value, *earlier):
    return lax.optimization_barrier((value, *earlier))[0]


def local(
    inputs,
    cotangent,
    seg_ids,
    norm_gains,
    w_q,
    key_value_weight,
    w_zx,
    w_bc,
    w_dt,
    a_log,
    dt_bias,
    d_skip,
    conv_x,
    conv_bc,
    m_gain,
    w_ao,
    w_mo,
    w_gu,
    w_down,
):
    members = lax.axis_size("dp")
    size_z = lax.axis_size("tensor")
    me_z = lax.axis_index("tensor")
    length = seg_ids.shape[1]
    count, model = inputs.shape[1:]
    block = model // members
    owned = key_value_weight.shape[1]
    heads = w_q.shape[2] // HEAD_SIZE
    kv_head = me_z * heads // (QUERY_HEADS // KEY_VALUE_HEADS)
    width = w_zx.shape[3]
    m_heads = w_dt.shape[2]
    states2 = w_bc.shape[2]
    hidden_units = w_gu.shape[3]
    taps = conv_bc.shape[2]
    gains_own = norm_gains.shape[2]
    cols = {"width": width, "states": states2 // 2, "x": width, "q": 0}
    cols["k"] = cols["q"] + heads * HEAD_SIZE
    cols["v"] = cols["k"] + HEAD_SIZE
    cols["bc"] = cols["v"] + HEAD_SIZE
    cols["dt"] = cols["bc"] + states2
    att_width = heads * HEAD_SIZE
    parts = 2 if count % 256 == 0 else 1
    sub = count // parts
    chunk = sub
    chunks = length // chunk
    late = parts - 1
    places = [(c % parts) * size_z + c // parts for c in range(chunks)]

    def split(value):
        return [value[h * sub : (h + 1) * sub] for h in range(parts)]

    def by_part(value):
        rows = size_z * sub
        return [value[h * rows : (h + 1) * rows] for h in range(parts)]

    lane_rows = 2 * KEY_VALUE_HEADS * HEAD_SIZE + states2
    shared = jnp.concatenate(
        [
            jnp.pad(norm_gains[0], ((0, 0), (0, lane_rows - gains_own))),
            jnp.pad(conv_bc[0], ((0, 10), (0, lane_rows - taps))),
            jnp.concatenate([key_value_weight[0], w_bc[0]], axis=1),
        ],
        axis=0,
    )
    def scatter_dp(value):
        return lax.psum_scatter(value, "dp", scatter_dimension=0, tiled=True)

    def gather_dp(value, *earlier):
        if earlier:
            value = after(value, *earlier)
        return lax.all_gather(value, "dp", axis=0, tiled=True)

    x_parts = split(inputs[0])
    shared = z_gather_direct(shared).reshape(size_z, 16 + owned, lane_rows)
    tiny = shared[:, :16]
    shared = shared[:, 16:].reshape(block, lane_rows)
    kv_cols = [
        lax.dynamic_slice_in_dim(shared, (base + kv_head) * HEAD_SIZE, HEAD_SIZE, 1)
        for base in (0, KEY_VALUE_HEADS)
    ]
    panel_rest = jnp.concatenate(
        [w_q[0]]
        + kv_cols
        + [
            shared[:, 2 * KEY_VALUE_HEADS * HEAD_SIZE :],
            jnp.pad(w_dt[0], ((0, 0), (0, LANES - m_heads))),
        ],
        axis=1,
    )
    rest_width = panel_rest.shape[1]
    tiny = jnp.concatenate(
        [
            jnp.swapaxes(tiny[:, :2, :gains_own], 0, 1).reshape(2, block),
            jnp.pad(
                jnp.swapaxes(tiny[:, 2:6, :taps], 0, 1).reshape(4, size_z * taps),
                ((0, 10), (0, block - size_z * taps)),
            ),
        ],
        axis=0,
    )
    panel_rows = jnp.concatenate([w_zx[0].reshape(block, 2 * width), panel_rest], axis=1)
    all_width = panel_rows.shape[1]
    tiny = jnp.pad(tiny, ((0, 0), (0, all_width - block)))
    panel_rows = jnp.concatenate([panel_rows, tiny], axis=0)
    w_all = gather_dp(panel_rows)
    x_moved = z_gather_parts(x_parts, in_turn=True)
    tiny = w_all.reshape(members, block + 16, all_width)[:, block:, :block].astype(F32)
    gains = jnp.swapaxes(tiny[:, :2], 0, 1).reshape(2, model)
    convbc_all = jnp.swapaxes(tiny[:, 2:6, : size_z * taps], 0, 1).reshape(4, states2)
    gain1, gain2 = gains[0:1], gains[1:2]
    w_b = gather_dp(jnp.concatenate([w_ao[0], w_mo[0]], axis=0).T, panel_rows)
    w_cd = jnp.concatenate([w_gu[0].reshape(block, 2 * hidden_units), w_down[0].T], axis=1)
    w_cd = gather_dp(w_cd, panel_rows)

    seg_own, a_own, dtb_own, dskip_own, cx_own, mgain_own = ordered(
        [seg_ids[0], a_log[0], dt_bias[0], d_skip[0], conv_x[0], m_gain[0]], panel_rows
    )
    aux, segr = segment_tables(seg_own, chunk)
    tables = [jnp.asarray(t) for t in rotary_rows(length)]
    cx = pad_rows(cx_own, 8)
    cbc = pad_rows(convbc_all, 8)
    par = jnp.pad(jnp.stack([a_own, dtb_own]), ((0, 6), (0, LANES - m_heads)))
    dskip = jnp.broadcast_to(jnp.repeat(dskip_own, P_SIZE)[None, :], (8, width))
    mgain = jnp.broadcast_to(mgain_own[None, :], (8, width))
    setup = (aux, segr, cx, cbc, par, dskip, mgain)

    held = ()
    d_moved = None
    for h in range(parts):
        pieces = x_moved[h]
        if h:
            pieces = pieces[:-1] + [ordered(pieces[-1], held[0])]
        x_all = z_place(x_parts[h], pieces)
        held = norm_project(x_all, gain1, w_all, held, h, parts, members)
        if d_moved is None:
            d_moved = z_gather_parts([after(cotangent[0], held[0])])[0]
    normed1, panel = held
    gm, squares, y_out, held = mamba_forward(cols, panel, *setup, chunk, parts, size_z)
    squares = z_sends(squares[:, 0].reshape(-1, LANES))
    attended = attention_call(
        attention_forward_kernel,
        "attention_forward",
        after(panel, y_out, *d_moved[0]),
        2 * width + cols["q"],
        heads,
        tables,
        aux,
        segr,
        None,
        att_width,
        [],
        places,
    )
    squares = sum(ordered(squares, attended)).reshape(length, 1)
    rstd = lax.rsqrt(squares / (HM * P_SIZE) + NORM_EPS)
    branch = branch_product(attended, gm, rstd, w_b, parts)
    sums, moved = z_scatter_parts(
        branch, {(0, 1): d_moved[min(1, size_z - 2)], (late, size_z - 2): d_moved[-1]}
    )
    x_own = after(inputs[0], *branch).astype(F32)
    h_mid, normed2_own = [], []
    for h, x in enumerate(split(x_own)):
        total = sums[h]
        if h:
            total = after(total, normed2_own[h - 1])
        h_mid.append(x + total)
        normed2_own.append((h_mid[h] * rms_factor(h_mid[h]) * gain2).astype(BF16))
    moved = z_gather_parts(normed2_own)
    d_out = [
        z_rotated(own, [[split(right)[h], split(left)[h]] for right, left in d_moved])
        for h, own in enumerate(split(cotangent[0]))
    ]
    normed2 = [z_rotated(own, m) for own, m in zip(normed2_own, moved)]
    act, d_gate, d_up = feed_forward(normed2, d_out, w_cd, hidden_units)
    d_norm2 = transposed_product([d_gate, d_up], w_cd, 0, parts)
    first = z_scatter_first(d_norm2)
    hooks = {(0, 1): [], (late, 1): []}
    given, g_cd, pieces = list(d_norm2), None, 2
    places_of = [(0, 1), (late, 1)]
    for piece in range(pieces):
        left, right = ordered((normed2, d_out), *given)
        g_cd, token = gradient(
            [left, right], [d_gate, d_up, act], [0, 0, 1], g_cd, piece, pieces
        )
        given = [*first, token]
        hooks[places_of[piece]].append(token)
    sums, moved = z_scatter_parts(d_norm2, hooks, first, True)
    g_cd = scatter_dp(g_cd)
    grad_mid, grad_low = [], []
    for h, part in enumerate(split(cotangent[0])):
        total = sums[h]
        if h:
            total = after(total, grad_low[h - 1])
        grad, _ = norm_backward(h_mid[h], gain2, total, part.astype(F32))
        grad_mid.append(grad)
        grad_low.append(grad.astype(BF16))
    h_mid_all = jnp.concatenate(h_mid, axis=0)
    moved = z_gather_parts(grad_low)
    ffn = transposed_product([after(act, *moved[0][0])], w_cd, 2, parts)
    ffn = [
        lax.dynamic_slice_in_dim(part, lax.rem(me_z - b + size_z, size_z) * sub, sub, 0)
        for b in range(size_z)
        for part in ffn
    ]
    ffn = jnp.concatenate(ffn, axis=0)
    d_branch = [z_place(own, m) for own, m in zip(grad_low, moved)]
    ffn = line_scatter([ffn], *moved[late][-1])[0]
    g_c, g_d = g_cd[:, : 2 * hidden_units], g_cd[:, 2 * hidden_units :]

    d_b, inner = branch_back(d_branch, w_b, gm)
    inner = z_sends(inner[:, 0].reshape(-1, LANES))
    d_qkv = attention_call(
        attention_backward_kernel,
        "attention_backward",
        after(panel, g_cd),
        2 * width + cols["q"],
        heads,
        tables,
        aux,
        segr,
        d_b,
        att_width + 2 * HEAD_SIZE,
        [pltpu.VMEM((length, HEAD_SIZE), F32), pltpu.VMEM((length, HEAD_SIZE), F32)],
        places,
    )
    inner = sum(ordered(inner, d_qkv)).reshape(length, 1)
    aux2 = jnp.pad(
        jnp.concatenate([rstd, rstd**3 * inner / (HM * P_SIZE)], axis=1),
        ((0, 0), (0, LANES - 2)),
    )
    d_all, g_wide, g_cx, g_cbc, g_heads = mamba_backward(
        cols, panel, *setup, y_out, held, d_b, aux2, d_qkv, chunk, parts, size_z
    )
    mixed = (after(gm, aux2).astype(F32) * rstd).astype(BF16)
    mixed = jnp.concatenate([attended, mixed], axis=1)
    g_all, _ = gradient([[normed1], d_branch], [d_all, mixed], [0, 1], None, 0, 1)
    d_norm1, low = [], g_all
    for h in range(parts):
        low = back_product(after(d_all, low), w_all, h, parts, members, model)
        d_norm1.append(low)
    g_all = scatter_dp(g_all)
    g_zx = g_all[:, : 2 * width].astype(F32)
    g_rest = g_all[:, 2 * width : all_width]
    g_b = g_all[:, all_width:].astype(F32)

    by_dp = [
        g_cbc[:4].reshape(-1, LANES),
        g_heads[0:2],
        jnp.pad(g_wide[1].reshape(m_heads, P_SIZE).sum(axis=1), (0, LANES - m_heads))[None],
        g_cx[:4].reshape(-1, LANES),
        g_wide[0].reshape(-1, LANES),
    ]
    ends = np.cumsum([v.shape[0] for v in by_dp])
    by_dp = jnp.concatenate(by_dp, axis=0)
    by_dp = pad_rows(by_dp, -(-by_dp.shape[0] // 8) * 8)
    by_dp = dp_sum(after(by_dp, *d_norm1))
    dp_taps = size_z * taps
    g_convbc = lax.dynamic_slice_in_dim(
        by_dp[: ends[0]].reshape(4, states2), lax.axis_index("dp") * dp_taps, dp_taps, 1
    )
    g_convbc = jnp.pad(
        g_convbc.T.reshape(size_z, taps, 4), ((0, 0), (0, owned - taps), (0, 0))
    ).reshape(block, 4)
    g_alog = by_dp[ends[0] : ends[0] + 1, :m_heads]
    g_dtbias = by_dp[ends[0] + 1 : ends[1], :m_heads]
    g_dskip = by_dp[ends[1] : ends[2], :m_heads]
    g_convx = by_dp[ends[2] : ends[3]].reshape(1, 4, width)
    g_mgain = by_dp[ends[3] : ends[4]].reshape(1, width)

    g_rest = g_rest.astype(F32)
    first = cols["q"]
    gain1_own = jnp.sum(panel_rest.astype(F32) * g_rest, axis=1) + jnp.sum(
        w_zx[0].reshape(block, 2 * width).astype(F32) * g_zx, axis=1
    )
    gain2_own = jnp.sum(
        w_gu[0].reshape(block, 2 * hidden_units).astype(F32) * g_c.astype(F32),
        axis=1,
    )
    mine = lax.axis_index("dp") * block
    gain1_own = gain1_own / lax.dynamic_slice_in_dim(gain1[0], mine, block, 0)
    gain2_own = gain2_own / lax.dynamic_slice_in_dim(gain2[0], mine, block, 0)
    small = jnp.concatenate([gain1_own[:, None], gain2_own[:, None], g_convbc], axis=1)
    g_q = g_rest[:, : cols["k"] - first]
    g_dt = g_rest[:, cols["dt"] - first : cols["dt"] - first + m_heads]
    kv_part = jnp.zeros((block, 2 * KEY_VALUE_HEADS * HEAD_SIZE), F32)
    for base, name in ((0, "k"), (KEY_VALUE_HEADS, "v")):
        at = cols[name] - first
        kv_part = lax.dynamic_update_slice_in_dim(
            kv_part, g_rest[:, at : at + HEAD_SIZE], (base + kv_head) * HEAD_SIZE, 1
        )
    kv_total = 2 * KEY_VALUE_HEADS * HEAD_SIZE
    shared_grad = jnp.concatenate(
        [
            kv_part,
            g_rest[:, cols["bc"] - first : cols["dt"] - first],
            jnp.pad(small, ((0, 0), (0, LANES - small.shape[1]))),
        ],
        axis=1,
    )
    hidden_out = (h_mid_all + ffn).astype(BF16)
    shared_grad = z_scatter_direct(shared_grad.astype(BF16))
    small = shared_grad[:, kv_total + states2 :]
    shared_grad = shared_grad[:, : kv_total + states2]
    g_gains = small[:, :2].T[None]
    g_convbc = small[:taps, 2:6].T[None]
    sums, moved = z_scatter_parts(d_norm1)
    norm_sum = jnp.concatenate(sums, axis=0)
    grad_in, _ = norm_backward(x_own, gain1, norm_sum, jnp.concatenate(grad_mid, axis=0))
    input_grad = grad_in

    return (
        hidden_out[None],
        input_grad[None],
        g_gains,
        g_q[None],
        shared_grad[None, :, :kv_total],
        g_zx.reshape(1, block, 2, width),
        shared_grad[None, :, kv_total:],
        g_dt[None],
        g_alog,
        g_dtbias,
        g_dskip,
        g_convx,
        g_convbc,
        g_mgain,
        g_b[:, :att_width].T[None],
        g_b[:, att_width:].T[None],
        g_c.astype(F32).reshape(1, block, 2, hidden_units),
        g_d.astype(F32).T[None],
    )


def solution(mesh):
    return jax.shard_map(
        local,
        mesh=mesh,
        in_specs=(
            P("dp", "tensor", None),
            P("dp", "tensor", None),
            P("dp", None),
            P(None, None, ("dp", "tensor")),
            P(None, "dp", "tensor"),
            P(None, ("dp", "tensor"), None),
            P(None, "dp", None, "tensor"),
            P(None, ("dp", "tensor"), None),
            P(None, "dp", "tensor"),
            P(None, "tensor"),
            P(None, "tensor"),
            P(None, "tensor"),
            P(None, None, "tensor"),
            P(None, None, ("dp", "tensor")),
            P(None, "tensor"),
            P(None, "tensor", "dp"),
            P(None, "tensor", "dp"),
            P(None, "dp", None, "tensor"),
            P(None, "tensor", "dp"),
        ),
        out_specs=(
            P("dp", "tensor", None),
            P("dp", "tensor", None),
            P(None, None, ("dp", "tensor")),
            P(None, "dp", "tensor"),
            P(None, ("dp", "tensor"), None),
            P(None, "dp", None, "tensor"),
            P(None, ("dp", "tensor"), None),
            P(None, "dp", "tensor"),
            P(None, "tensor"),
            P(None, "tensor"),
            P(None, "tensor"),
            P(None, None, "tensor"),
            P(None, None, ("dp", "tensor")),
            P(None, "tensor"),
            P(None, "tensor", "dp"),
            P(None, "tensor", "dp"),
            P(None, "dp", None, "tensor"),
            P(None, "tensor", "dp"),
        ),
        check_vma=False,
    )
```

```python
from functools import partial

import jax
import jax.numpy as jnp
import numpy as np
from jax import lax
from jax.experimental import pallas as pl
from jax.experimental.pallas import tpu as pltpu
from jax.sharding import PartitionSpec as P

QUERY_HEADS = 8
KEY_VALUE_HEADS = 2
HEAD_SIZE = 128
HM = 48
P_SIZE = 64
LANES = 128
NORM_EPS = 1e-05
ROPE_BASE = 100000000000.0
MASK_FILL = -1e30
F32 = jnp.float32
BF16 = jnp.bfloat16
NN = (((1,), (0,)), ((), ()))
NT = (((1,), (1,)), ((), ()))
TN = (((0,), (0,)), ((), ()))
VMEM_LIMIT = 48 * 1024 * 1024


def dot(left, right, dims=NN):
    return lax.dot_general(left, right, dims, preferred_element_type=F32)


def sums_of(zero_one, value):
    high = value.astype(BF16)
    value = value - high.astype(F32)
    middle = value.astype(BF16)
    low = (value - middle.astype(F32)).astype(BF16)
    width = value.shape[1]
    out = dot(zero_one, jnp.concatenate([high, middle, low], axis=1))
    return out[:, :width] + out[:, width : 2 * width] + out[:, 2 * width :]


def sigmoid(v):
    return 0.5 * jnp.tanh(0.5 * v) + 0.5


def send_dp(value, mask):
    size = lax.axis_size("dp")
    return lax.ppermute(value, "dp", [(i, i ^ mask) for i in range(size)])


def chip_gather(rows, *earlier):
    chips = lax.axis_size("dp") // 2
    if earlier:
        rows = after(rows, *earlier)
    return [rows] + [send_dp(rows, 2 * k) for k in range(1, chips)]


def core_gather(pieces, *earlier):
    if earlier:
        pieces = ordered(pieces, *earlier)
    chips = len(pieces)
    me = lax.axis_index("dp")
    chip, core = lax.div(me, 2), lax.rem(me, 2)
    rows, width = pieces[0].shape
    mine = jnp.zeros((chips, rows, width), pieces[0].dtype)
    for k, piece in enumerate(pieces):
        mine = lax.dynamic_update_slice(mine, piece[None], (chip ^ k, 0, 0))
    other = send_dp(mine, 1)
    out = jnp.zeros((chips, 2, rows, width), mine.dtype)
    out = lax.dynamic_update_slice(out, mine[:, None], (0, core, 0, 0))
    out = lax.dynamic_update_slice(out, other[:, None], (0, 1 - core, 0, 0))
    return out.reshape(2 * chips * rows, width)


def core_scatter(grad, *earlier):
    chips = lax.axis_size("dp") // 2
    core = lax.rem(lax.axis_index("dp"), 2)
    blocks = grad.reshape(chips, 2, -1, grad.shape[1])
    other = send_dp(lax.dynamic_index_in_dim(blocks, 1 - core, 1, keepdims=False), 1)
    if earlier:
        other = after(other, *earlier)
    mine = lax.dynamic_index_in_dim(blocks, core, 1, keepdims=False)
    return (mine.astype(F32) + other.astype(F32)).astype(grad.dtype)


def chip_scatter(pair):
    chips = pair.shape[0]
    chip = lax.div(lax.axis_index("dp"), 2)
    pieces = [lax.dynamic_index_in_dim(pair, chip, 0, keepdims=False)]
    for k in range(1, chips):
        piece = lax.dynamic_index_in_dim(pair, chip ^ k, 0, keepdims=False)
        pieces.append(send_dp(piece, 2 * k))
    return pieces


def add_up(pieces, *earlier):
    if earlier:
        pieces = ordered(pieces, *earlier)
    total = pieces[0].astype(F32)
    for piece in pieces[1:]:
        total = total + piece.astype(F32)
    return total


def dp_sum(value):
    chips = lax.axis_size("dp") // 2
    value = value + send_dp(value, 1)
    total = value
    for k in range(1, chips):
        total = total + send_dp(value, 2 * k)
    return total


def send_z(value, shift):
    size = lax.axis_size("tensor")
    return lax.ppermute(value, "tensor", [(i, (i + shift) % size) for i in range(size)])


def z_gather_direct(rows):
    size = lax.axis_size("tensor")
    me = lax.axis_index("tensor")
    count = rows.shape[0]
    out = jnp.zeros((size * count,) + rows.shape[1:], rows.dtype)
    pieces = [rows] + [send_z(rows, k) for k in range(1, size)]
    for k, piece in enumerate(pieces):
        out = lax.dynamic_update_slice_in_dim(out, piece, lax.rem(me - k + size, size) * count, 0)
    return out


def z_scatter_direct(total):
    size = lax.axis_size("tensor")
    me = lax.axis_index("tensor")
    count = total.shape[0] // size
    mine = lax.dynamic_slice_in_dim(total, me * count, count, 0).astype(F32)
    for k in range(1, size):
        piece = lax.dynamic_slice_in_dim(total, lax.rem(me + k, size) * count, count, 0)
        mine = mine + send_z(piece, k).astype(F32)
    return mine


def ordered(values, *earlier):
    return lax.optimization_barrier((tuple(values), earlier))[0]


def z_gather_first(rows):
    size = lax.axis_size("tensor")
    right = lax.ppermute(rows, "tensor", [(i, i + 1) for i in range(size - 1)])
    left = lax.ppermute(rows, "tensor", [(i, i - 1) for i in range(1, size)])
    return [right, left]


def z_gather_parts(parts, hooks=None, first=None, in_turn=False):
    size = lax.axis_size("tensor")
    hooks = hooks or {}
    moved = [[] for _ in parts]
    for h, rows in enumerate(parts):
        right = left = rows
        for s in range(size - 1):
            if s == 0 and h == 0 and first is not None:
                right, left = first
                moved[h].append(first)
                continue
            earlier = list(hooks.get((h, s), []))
            if h and in_turn:
                earlier += moved[h - 1][s]
            if s or earlier:
                right, left = ordered((right, left), *earlier)
            right = lax.ppermute(right, "tensor", [(i, i + 1) for i in range(s, size - 1)])
            left = lax.ppermute(left, "tensor", [(i, i - 1) for i in range(1, size - s)])
            moved[h].append([right, left])
    return moved


def line_gather(parts, *earlier):
    out = []
    for part in parts:
        if earlier:
            part = after(part, *earlier)
        out.append(lax.all_gather(part, "tensor", axis=0, tiled=True))
    return out


def line_scatter(parts, *earlier):
    out = []
    for part in parts:
        if earlier:
            part = after(part, *earlier)
        out.append(
            lax.psum_scatter(part, "tensor", scatter_dimension=0, tiled=True).astype(F32)
        )
    return out


def line_sends(parts, *earlier):
    size = lax.axis_size("tensor")
    me = lax.axis_index("tensor")
    count = parts[0].shape[0] // size
    pieces = []
    for k in range(size):
        index = lax.rem(me + k, size) * count
        piece = [lax.dynamic_slice_in_dim(part, index, count, 0) for part in parts]
        piece = jnp.concatenate(piece, axis=0)
        if k:
            if earlier:
                piece = after(piece, *earlier)
            piece = send_z(piece, k)
        pieces.append(piece)
    return pieces


def place_kernel(place_ref, in_ref, out_ref):
    out_ref[...] = in_ref[...]


def z_place(rows, moved):
    size = lax.axis_size("tensor")
    me = lax.axis_index("tensor")
    count, width = rows.shape
    out = pl.pallas_call(
        place_kernel,
        grid_spec=pltpu.PrefetchScalarGridSpec(
            num_scalar_prefetch=1,
            grid=(1,),
            in_specs=[pl.BlockSpec((count, width), lambda i, place_ref: (0, 0))],
            out_specs=pl.BlockSpec((count, width), lambda i, place_ref: (place_ref[0], 0)),
        ),
        out_shape=jax.ShapeDtypeStruct((size * count, width), rows.dtype),
        cost_estimate=pl.CostEstimate(
            flops=0, bytes_accessed=4 * rows.size, transcendentals=0
        ),
        name="place",
    )(me.astype(jnp.int32).reshape(1), rows)
    for d in range(1, size):
        piece = moved[d - 1][0] + moved[size - d - 1][1]
        at = lax.rem(me - d + size, size) * count
        out = lax.dynamic_update_slice_in_dim(out, piece, at, 0)
    return out


def block_of(total, index, size):
    if isinstance(total, list):
        return jnp.concatenate([block_of(t, index, size) for t in total], axis=0)
    count = total.shape[0] // size
    return lax.dynamic_slice_in_dim(total, index * count, count, 0)


def z_rotated(rows, moved):
    size = lax.axis_size("tensor")
    pieces = [moved[d - 1][0] + moved[size - d - 1][1] for d in range(1, size)]
    return jnp.concatenate([rows] + pieces, axis=0)


def z_scatter_first(parts):
    size = lax.axis_size("tensor")
    count = parts[0].shape[0] // size
    right = lax.ppermute(parts[0][count : 2 * count], "tensor", [(0, 1)])
    left = lax.ppermute(parts[0][(size - 1) * count :], "tensor", [(size - 1, size - 2)])
    return [right, left]


def z_scatter_parts(parts, hooks=None, first=None, rotated=False):
    size = lax.axis_size("tensor")
    me = lax.axis_index("tensor")
    hooks = hooks or {}
    sums, moved = [], [[] for _ in parts]
    for h, total in enumerate(parts):

        def part(offset, total=total):
            if rotated:
                count = total.shape[0] // size
                at = (-offset) % size * count
                return total[at : at + count]
            return block_of(total, jnp.clip(me + offset, 0, size - 1), size)

        right = left = None
        for s in range(size - 1):
            if s == 0 and h == 0 and first is not None:
                right, left = first
                moved[h].append(first)
                continue
            d = size - 1 - s
            to_right, to_left = part(d), part(-d)
            if s:
                to_right = (to_right.astype(F32) + right.astype(F32)).astype(BF16)
                to_left = (to_left.astype(F32) + left.astype(F32)).astype(BF16)
            earlier = list(hooks.get((h, s), []))
            if h:
                earlier += moved[h - 1][s]
            to_right, to_left = ordered((to_right, to_left), *earlier)
            right = lax.ppermute(to_right, "tensor", [(i, i + 1) for i in range(s + 1)])
            left = lax.ppermute(to_left, "tensor", [(i, i - 1) for i in range(size - 1 - s, size)])
            moved[h].append([right, left])
        sums.append(part(0).astype(F32) + right.astype(F32) + left.astype(F32))
    return sums, moved


def z_sends(value):
    size = lax.axis_size("tensor")
    return [value] + [send_z(value, k) for k in range(1, size)]


def z_sum(value):
    return sum(z_sends(value))


def tile_of(width):
    return max(t for t in range(LANES, 513, LANES) if width % t == 0)


def norm_project_kernel(members, x_ref, gain_ref, w_ref, *refs):
    normed_ref, out_ref = refs[-2:]
    block, rows = x_ref.shape[1] // members, w_ref.shape[0] // members

    @pl.when(pl.program_id(0) == 0)
    def _():
        x = x_ref[...].astype(F32)
        mean = jnp.sum(x * x, axis=1, keepdims=True) * (1.0 / x.shape[1])
        normed_ref[...] = (x * lax.rsqrt(mean + NORM_EPS) * gain_ref[...]).astype(BF16)

    out = None
    for j in range(members):
        part = dot(
            normed_ref[:, j * block : (j + 1) * block], w_ref[j * rows : j * rows + block, :]
        )
        out = part if out is None else out + part
    out_ref[...] = out


def norm_project(x, gain, weights, held, index, parts, members):
    rows, model = x.shape
    total, width = rows * parts, weights.shape[1]
    tile = tile_of(width)
    return pl.pallas_call(
        partial(norm_project_kernel, members),
        grid=(width // tile,),
        in_specs=[
            pl.BlockSpec((rows, model), lambda j: (0, 0)),
            pl.BlockSpec((1, model), lambda j: (0, 0)),
            pl.BlockSpec((weights.shape[0], tile), lambda j: (0, j)),
        ]
        + [pl.BlockSpec(memory_space=pl.ANY)] * len(held),
        out_specs=[
            pl.BlockSpec((rows, model), lambda j: (index, 0)),
            pl.BlockSpec((rows, tile), lambda j: (index, j)),
        ],
        out_shape=[
            jax.ShapeDtypeStruct((total, model), BF16),
            jax.ShapeDtypeStruct((total, width), F32),
        ],
        input_output_aliases={3: 0, 4: 1} if held else {},
        compiler_params=pltpu.CompilerParams(vmem_limit_bytes=VMEM_LIMIT),
        cost_estimate=pl.CostEstimate(
            flops=2 * rows * model * width,
            bytes_accessed=2 * (rows + width) * model + 4 * rows * width,
            transcendentals=0,
        ),
        name="norm_project",
    )(x, gain, weights, *held)


def gradient_kernel(parts, uses, ranges, *refs):
    out_ref, done_ref = refs[-2:]
    done_ref[...] = jnp.zeros_like(done_ref)
    lefts, rights = refs[: sum(parts)], refs[sum(parts) : sum(parts) + len(uses)]
    turned, at = [], 0
    for number in parts:
        turned.append([left[...].T for left in lefts[at : at + number]])
        at += number
    at = 0
    for use, right, (first, stop) in zip(uses, rights, ranges):
        width = stop - first
        rows = right.shape[0] // parts[use]
        total = None
        for h, left in enumerate(turned[use]):
            part = dot(left, right[h * rows : (h + 1) * rows, first:stop])
            total = part if total is None else total + part
        out_ref[:, at : at + width] = total.astype(BF16)
        at += width


def gradient(lefts, rights, uses, held, piece, pieces, ranges=None):
    model = lefts[0][0].shape[1]
    ranges = ranges or [(0, right.shape[1]) for right in rights]
    width = sum(stop - first for first, stop in ranges)
    tile = min(512, model // pieces)
    steps = model // pieces // tile
    parts = [len(left) for left in lefts]
    flat = [part for left in lefts for part in left]
    held = [] if held is None else [held]
    return pl.pallas_call(
        partial(gradient_kernel, parts, uses, ranges),
        grid=(steps,),
        in_specs=[
            pl.BlockSpec((part.shape[0], tile), lambda j: (0, piece * steps + j)) for part in flat
        ]
        + [pl.BlockSpec(right.shape, lambda j: (0, 0)) for right in rights]
        + [pl.BlockSpec(memory_space=pl.ANY)] * len(held),
        out_specs=[
            pl.BlockSpec((tile, width), lambda j: (piece * steps + j, 0)),
            pl.BlockSpec((8, LANES), lambda j: (0, 0)),
        ],
        out_shape=[
            jax.ShapeDtypeStruct((model, width), BF16),
            jax.ShapeDtypeStruct((8, LANES), F32),
        ],
        input_output_aliases={len(flat) + len(rights): 0} if held else {},
        compiler_params=pltpu.CompilerParams(vmem_limit_bytes=VMEM_LIMIT),
        cost_estimate=pl.CostEstimate(
            flops=2 * rights[0].shape[0] * (model // pieces) * width,
            bytes_accessed=2 * (rights[0].shape[0] * (model + width) + model * width) // pieces,
            transcendentals=0,
        ),
        name="gradient",
    )(*flat, *rights, *held)


def feed_forward_kernel(parts, *refs):
    xs, ds = refs[:parts], refs[parts : 2 * parts]
    gate_ref, up_ref, down_ref, act_ref, d_gate_ref, d_up_ref = refs[2 * parts :]
    for h in range(parts):
        rows = xs[h].shape[0]
        here = slice(h * rows, (h + 1) * rows)
        gate = dot(xs[h][...], gate_ref[...])
        up = dot(xs[h][...], up_ref[...])
        sig_gate = sigmoid(gate)
        silu_gate = gate * sig_gate
        act_ref[here, :] = (silu_gate * up).astype(BF16)
        d_act = dot(ds[h][...], down_ref[...])
        d_gate = d_act * up * (sig_gate * (1.0 + gate * (1.0 - sig_gate)))
        d_gate_ref[here, :] = d_gate.astype(BF16)
        d_up_ref[here, :] = (d_act * silu_gate).astype(BF16)


def feed_forward(normed, d_out, weights, hidden_units):
    parts, (rows, model) = len(normed), normed[0].shape
    tile = min(256, hidden_units)
    steps = hidden_units // tile

    def columns(first):
        return pl.BlockSpec((model, tile), lambda j: (0, first * steps + j))

    whole = pl.BlockSpec((rows, model), lambda j: (0, 0))
    out = jax.ShapeDtypeStruct((rows * parts, hidden_units), BF16)
    return pl.pallas_call(
        partial(feed_forward_kernel, parts),
        grid=(steps,),
        in_specs=[whole] * (2 * parts) + [columns(0), columns(1), columns(2)],
        out_specs=[pl.BlockSpec((rows * parts, tile), lambda j: (0, j))] * 3,
        out_shape=[out] * 3,
        compiler_params=pltpu.CompilerParams(vmem_limit_bytes=VMEM_LIMIT),
        cost_estimate=pl.CostEstimate(
            flops=6 * rows * parts * model * hidden_units,
            bytes_accessed=2 * (2 * rows * parts + 3 * hidden_units) * model,
            transcendentals=rows * parts * hidden_units,
        ),
        name="feed_forward",
    )(*normed, *d_out, weights, weights, weights)


def branch_back_kernel(parts, *refs):
    w_ref, gm_ref, out_ref, inner_ref = refs[parts:]
    first = pl.program_id(0) == 0

    @pl.when(first)
    def _():
        inner_ref[...] = jnp.zeros_like(inner_ref)

    for h in range(parts):
        rows = refs[h].shape[0]
        here = slice(h * rows, (h + 1) * rows)
        out = dot(refs[h][...], w_ref[...])
        out_ref[here, :] = out
        inner = jnp.sum(out * gm_ref[here, :].astype(F32), axis=1, keepdims=True)
        inner_ref[here, :] += jnp.where(first, 0.0, inner)


def branch_back(d_branch, weights, gm):
    parts, (rows, model) = len(d_branch), d_branch[0].shape
    tile = weights.shape[1] - gm.shape[1]
    steps = weights.shape[1] // tile
    total = rows * parts
    return pl.pallas_call(
        partial(branch_back_kernel, parts),
        grid=(steps,),
        in_specs=[pl.BlockSpec((rows, model), lambda j: (0, 0))] * parts
        + [
            pl.BlockSpec((model, tile), lambda j: (0, j)),
            pl.BlockSpec((total, tile), lambda j: (0, jnp.maximum(j - 1, 0))),
        ],
        out_specs=[
            pl.BlockSpec((total, tile), lambda j: (0, j)),
            pl.BlockSpec((total, LANES), lambda j: (0, 0)),
        ],
        out_shape=[
            jax.ShapeDtypeStruct((total, weights.shape[1]), F32),
            jax.ShapeDtypeStruct((total, LANES), F32),
        ],
        compiler_params=pltpu.CompilerParams(vmem_limit_bytes=VMEM_LIMIT),
        cost_estimate=pl.CostEstimate(
            flops=2 * total * model * weights.shape[1],
            bytes_accessed=2 * (total + weights.shape[1]) * model,
            transcendentals=0,
        ),
        name="branch_back",
    )(*d_branch, weights, gm)


def put_parts(out, refs):
    rows = out.shape[0] // len(refs)
    for h, ref in enumerate(refs):
        ref[...] = out[h * rows : (h + 1) * rows]


def transposed_kernel(count, *refs):
    out = None
    for left, right in zip(refs[:count], refs[count : 2 * count]):
        part = dot(left[...], right[...], NT)
        out = part if out is None else out + part
    put_parts(out.astype(BF16), refs[2 * count :])


def transposed_product(lefts, weights, first, parts):
    rows, width = lefts[0].shape
    model = weights.shape[0]
    tile = min(512, model)
    count = len(lefts)

    def columns(k):
        return pl.BlockSpec((tile, width), lambda j: (j, first + k))

    return pl.pallas_call(
        partial(transposed_kernel, count),
        grid=(model // tile,),
        in_specs=[pl.BlockSpec((rows, width), lambda j: (0, 0))] * count
        + [columns(k) for k in range(count)],
        out_specs=[pl.BlockSpec((rows // parts, tile), lambda j: (0, j))] * parts,
        out_shape=[jax.ShapeDtypeStruct((rows // parts, model), BF16)] * parts,
        compiler_params=pltpu.CompilerParams(vmem_limit_bytes=VMEM_LIMIT),
        cost_estimate=pl.CostEstimate(
            flops=2 * rows * model * width * count,
            bytes_accessed=2 * ((rows + model) * width * count + rows * model),
            transcendentals=0,
        ),
        name="transposed_product",
    )(*lefts, *([weights] * count))


def branch_kernel(att_ref, gm_ref, rstd_ref, w_ref, *out_refs):
    split = att_ref.shape[1]
    out = dot(att_ref[...], w_ref[:, :split], NT)
    out = out + rstd_ref[...] * dot(gm_ref[...], w_ref[:, split:], NT)
    put_parts(out.astype(BF16), out_refs)


def branch_product(attended, gm, rstd, weights, parts):
    rows = attended.shape[0]
    model, width = weights.shape
    tile = min(512, model)

    def whole(array):
        return pl.BlockSpec(array.shape, lambda j: (0, 0))

    return pl.pallas_call(
        branch_kernel,
        grid=(model // tile,),
        in_specs=[
            whole(attended),
            whole(gm),
            whole(rstd),
            pl.BlockSpec((tile, width), lambda j: (j, 0)),
        ],
        out_specs=[pl.BlockSpec((rows // parts, tile), lambda j: (0, j))] * parts,
        out_shape=[jax.ShapeDtypeStruct((rows // parts, model), BF16)] * parts,
        compiler_params=pltpu.CompilerParams(vmem_limit_bytes=VMEM_LIMIT),
        cost_estimate=pl.CostEstimate(
            flops=2 * rows * model * width,
            bytes_accessed=2 * ((rows + model) * width + rows * model),
            transcendentals=0,
        ),
        name="branch",
    )(attended, gm, rstd, weights)


def back_kernel(block, d_ref, w_ref, out_ref):
    count = out_ref.shape[1] // block
    rows = w_ref.shape[0] // count
    for k in range(count):
        out = dot(d_ref[...], w_ref[k * rows : k * rows + block, :], NT)
        out_ref[:, k * block : (k + 1) * block] = out.astype(BF16)


def back_product(d_all, weights, index, parts, members, model):
    rows, block = d_all.shape[0] // parts, model // members
    each = 2
    return pl.pallas_call(
        partial(back_kernel, block),
        grid=(members // each,),
        in_specs=[
            pl.BlockSpec((rows, d_all.shape[1]), lambda j: (index, 0)),
            pl.BlockSpec((each * weights.shape[0] // members, weights.shape[1]), lambda j: (j, 0)),
        ],
        out_specs=pl.BlockSpec((rows, each * block), lambda j: (0, j)),
        out_shape=jax.ShapeDtypeStruct((rows, model), BF16),
        compiler_params=pltpu.CompilerParams(vmem_limit_bytes=VMEM_LIMIT),
        cost_estimate=pl.CostEstimate(
            flops=2 * rows * model * d_all.shape[1],
            bytes_accessed=2 * (rows * d_all.shape[1] + weights.size + rows * model),
            transcendentals=0,
        ),
        name="back_product",
    )(d_all, weights)


def rotary_rows(length):
    half = HEAD_SIZE // 2
    freqs = np.float32(ROPE_BASE) ** (
        -np.arange(half).astype(np.float32) * np.float32(2.0) / np.float32(HEAD_SIZE)
    )
    angles = np.arange(length).astype(np.float32)[:, None] * freqs.astype(np.float32)[None, :]
    cosine, sine = np.cos(angles), np.sin(angles)
    return (
        np.concatenate([cosine, cosine], axis=1).astype(np.float32),
        np.concatenate([-sine, sine], axis=1).astype(np.float32),
    )


def rotate(value, cosine, sine):
    return value * cosine + pltpu.roll(value, HEAD_SIZE // 2, 1) * sine


def chunk_place(index, parts, members):
    return lax.rem(index, parts) * members + lax.div(index, parts)


def in_sequence(ref, places, rows, columns=slice(None)):
    return jnp.concatenate([ref[p * rows : (p + 1) * rows, columns] for p in places], axis=0)


def attention_probs(q_ref, keys, cos_ref, sin_ref, allowed, start, stop, places, rows):
    here = places[start // rows : stop // rows]
    query = in_sequence(q_ref, here, rows)
    query = rotate(query, cos_ref[start:stop, :], sin_ref[start:stop, :]).astype(BF16)
    scores = dot(query, keys, NT) * (HEAD_SIZE**-0.5)
    scores = jnp.where(allowed, scores, MASK_FILL)
    raised = jnp.exp(scores - jnp.max(scores, axis=1, keepdims=True))
    return query, raised * (1.0 / jnp.sum(raised, axis=1, keepdims=True))


def attention_mask(aux_ref, segr_ref, start, stop):
    rows = start + lax.broadcasted_iota(jnp.int32, (stop - start, stop), 0)
    cols = lax.broadcasted_iota(jnp.int32, (stop - start, stop), 1)
    return (aux_ref[start:stop, 0:1] == segr_ref[0:1, :stop]) & (rows >= cols)


def attention_forward_kernel(heads, block, places, *refs):
    q_refs = refs[:heads]
    k_ref, v_ref, cos_ref, sin_ref, aux_ref, segr_ref, out_ref = refs[heads:]
    length = k_ref.shape[0]
    rows = length // len(places)
    keys = rotate(in_sequence(k_ref, places, rows), cos_ref[...], sin_ref[...]).astype(BF16)
    vals = in_sequence(v_ref, places, rows).astype(BF16)
    for start in range(0, length, block):
        stop = start + block
        allowed = attention_mask(aux_ref, segr_ref, start, stop)
        for h in range(heads):
            _, probs = attention_probs(
                q_refs[h], keys[:stop], cos_ref, sin_ref, allowed, start, stop, places, rows
            )
            out = dot(probs.astype(BF16), vals[:stop]).astype(BF16)
            columns = slice(h * HEAD_SIZE, (h + 1) * HEAD_SIZE)
            for c in range(block // rows):
                p = places[start // rows + c]
                out_ref[p * rows : (p + 1) * rows, columns] = out[c * rows : (c + 1) * rows]


def attention_backward_kernel(heads, block, places, *refs):
    q_refs = refs[:heads]
    k_ref, v_ref, cos_ref, sin_ref, aux_ref, segr_ref, do_ref, out_ref, dk, dv = refs[heads:]
    length = k_ref.shape[0]
    rows = length // len(places)
    scale = HEAD_SIZE**-0.5
    keys = rotate(in_sequence(k_ref, places, rows), cos_ref[...], sin_ref[...]).astype(BF16)
    vals = in_sequence(v_ref, places, rows).astype(BF16)
    dk[...] = jnp.zeros_like(dk)
    dv[...] = jnp.zeros_like(dv)
    for start in range(0, length, block):
        stop = start + block
        allowed = attention_mask(aux_ref, segr_ref, start, stop)
        here = places[start // rows : stop // rows]
        for h in range(heads):
            columns = slice(h * HEAD_SIZE, (h + 1) * HEAD_SIZE)
            query, probs = attention_probs(
                q_refs[h], keys[:stop], cos_ref, sin_ref, allowed, start, stop, places, rows
            )
            given = in_sequence(do_ref, here, rows, columns).astype(BF16)
            d_probs = dot(given, vals[:stop], NT)
            delta = jnp.sum(probs * d_probs, axis=1, keepdims=True)
            d_scores = (probs * (d_probs - delta)).astype(BF16)
            d_query = dot(d_scores, keys[:stop]) * scale
            d_query = rotate(d_query, cos_ref[start:stop, :], -sin_ref[start:stop, :]).astype(BF16)
            for c, p in enumerate(here):
                out_ref[p * rows : (p + 1) * rows, columns] = d_query[c * rows : (c + 1) * rows]
            dk[:stop, :] += dot(d_scores, query, TN)
            dv[:stop, :] += dot(probs.astype(BF16), given, TN)
    d_keys = rotate(dk[...] * scale, cos_ref[...], -sin_ref[...]).astype(BF16)
    d_vals = dv[...].astype(BF16)
    for c, p in enumerate(places):
        there = slice(p * rows, (p + 1) * rows)
        out_ref[there, heads * HEAD_SIZE : (heads + 1) * HEAD_SIZE] = d_keys[
            c * rows : (c + 1) * rows
        ]
        out_ref[there, (heads + 1) * HEAD_SIZE :] = d_vals[c * rows : (c + 1) * rows]


def attention_call(
    kernel, name, panel, first, heads, tables, aux, segr, extra, width, scratch, places
):
    length = panel.shape[0]

    def column(index):
        return pl.BlockSpec((length, HEAD_SIZE), lambda i: (0, index))

    def whole(array):
        return pl.BlockSpec(array.shape, lambda i: (0, 0))

    specs = [column(first // HEAD_SIZE + h) for h in range(heads + 2)]
    operands = [*tables, aux, segr]
    specs += [whole(a) for a in operands]
    if extra is not None:
        specs.append(pl.BlockSpec((length, heads * HEAD_SIZE), lambda i: (0, 0)))
        operands.append(extra)
    return pl.pallas_call(
        partial(kernel, heads, min(256, length), places),
        grid=(1,),
        in_specs=specs,
        out_specs=pl.BlockSpec((length, width), lambda i: (0, 0)),
        out_shape=jax.ShapeDtypeStruct((length, width), BF16),
        scratch_shapes=scratch,
        compiler_params=pltpu.CompilerParams(vmem_limit_bytes=VMEM_LIMIT),
        cost_estimate=pl.CostEstimate(
            flops=(5000 if extra is not None else 3300) * heads * length * length,
            bytes_accessed=4 * length * 12 * HEAD_SIZE,
            transcendentals=heads * length * length,
        ),
        name=name,
    )(*([panel] * (heads + 2)), *operands)


def split_pair(value):
    high = value.astype(BF16)
    return high, (value - high.astype(F32)).astype(BF16)


def widen(value, expand_ref):
    high, rest = split_pair(value)
    return dot(jnp.concatenate([high, rest], axis=1), expand_ref[...])


def by_head(value, reduce_ref):
    high, rest = split_pair(value)
    return dot(high, reduce_ref[...]) + dot(rest, reduce_ref[...])


def conv_rows(current, halo, pad, taps_ref, aux):
    rows = current.shape[0]
    pad[0:8, :] = halo
    pad[8 : 8 + rows, :] = current
    out = taps_ref[3:4, :] * current
    for k in range(1, 4):
        out = out + taps_ref[3 - k : 4 - k, :] * (pad[8 - k : 8 - k + rows, :] * aux[:, k : k + 1])
    return out


def head_scalars(dt_raw, par_ref, lower):
    biased = dt_raw + par_ref[1:2, :]
    step = jnp.maximum(biased, 0.0) + jnp.log1p(jnp.exp(-jnp.abs(biased)))
    log_decay = -step * jnp.exp(par_ref[0:1, :])
    cumulative = sums_of(lower, log_decay)
    return biased, step, log_decay, cumulative


def triangle(rows, flip):
    i = lax.broadcasted_iota(jnp.int32, (rows, rows), 0)
    j = lax.broadcasted_iota(jnp.int32, (rows, rows), 1)
    return (i <= j) if flip else (i >= j)


def mamba_forward_kernel(
    cols,
    p_ref,
    halo_ref,
    aux_ref,
    segr_ref,
    cx_ref,
    cbc_ref,
    par_ref,
    dskip_ref,
    mgain_ref,
    expand_ref,
    gm_ref,
    sq_ref,
    y_ref,
    st_ref,
    state,
    pad_x,
    pad_bc,
):
    width, states = cols["width"], cols["states"]
    rows = p_ref.shape[0]
    r_ref, halo_r_ref = p_ref.at[:, 2 * width :], halo_ref.at[:, 2 * width :]
    x0, bc0, dt0 = cols["x"], cols["bc"], cols["dt"]

    @pl.when(pl.program_id(0) == 0)
    def _():
        state[...] = jnp.zeros_like(state)

    aux = aux_ref[...]
    u_x = conv_rows(
        p_ref[:, x0 : x0 + width], halo_ref[:, x0 : x0 + width], pad_x, cx_ref, aux
    )
    x_conv = u_x * sigmoid(u_x)
    u_bc = conv_rows(
        r_ref[:, bc0 : bc0 + 2 * states], halo_r_ref[:, bc0 : bc0 + 2 * states], pad_bc, cbc_ref, aux
    )
    bc = (u_bc * sigmoid(u_bc)).astype(BF16)
    keys, query = bc[:, :states], bc[:, states:]
    lower = triangle(rows, False)
    _, step, _, cum = head_scalars(
        r_ref[:, dt0 : dt0 + LANES], par_ref, lower.astype(F32).astype(BF16)
    )
    cum_t = cum.T
    last = cum[rows - 1 : rows, :]
    entering = jnp.exp(cum) * aux[:, 7:8]
    leaving = jnp.exp(last - cum) * aux[:, 8:9]
    wide = widen(jnp.concatenate([step, entering, leaving], axis=0), expand_ref)
    step_w, enter_w, leave_w = wide[:rows], wide[rows : 2 * rows], wide[2 * rows :]
    xs = x_conv * step_w
    xs_low = xs.astype(BF16)
    mask = lower & (aux[:, 0:1] == segr_ref[0:1, :])
    c_dot_b = dot(query, keys, NT)
    held = state[...]
    held_low = held.astype(BF16)
    st_ref[0] = held_low
    carried = dot(query, held_low) * enter_w
    lane = lax.broadcasted_iota(jnp.int32, (rows, LANES), 1)
    parts = []
    for pair in range(width // LANES):
        pair_x = xs_low[:, pair * LANES : (pair + 1) * LANES]
        both = []
        for h in (2 * pair, 2 * pair + 1):
            gap = cum[:, h : h + 1] - cum_t[h : h + 1, :]
            decay = jnp.exp(jnp.where(mask, gap, MASK_FILL))
            both.append((decay * c_dot_b).astype(BF16))
        both = dot(jnp.concatenate(both, axis=0), pair_x)
        parts.append(jnp.where(lane < P_SIZE, both[:rows], both[rows:]))
    y = jnp.concatenate(parts, axis=1) + carried + dskip_ref[0:1, :] * x_conv
    state[...] = held * enter_w[rows - 1 : rows, :] + dot(
        keys, (leave_w * xs).astype(BF16), TN
    )
    z = p_ref[:, :width]
    gated = y * (z * sigmoid(z))
    y_ref[...] = y
    gm_ref[...] = (gated * mgain_ref[0:1, :]).astype(BF16)
    sq_ref[...] = jnp.broadcast_to(jnp.sum(gated * gated, axis=1, keepdims=True), sq_ref.shape)


def mamba_backward_kernel(
    cols,
    p_ref,
    halo_ref,
    aux_ref,
    segr_ref,
    cx_ref,
    cbc_ref,
    par_ref,
    dskip_ref,
    mgain_ref,
    expand_ref,
    reduce_ref,
    y_ref,
    st_ref,
    db_ref,
    aux2_ref,
    dqkv_ref,
    da_ref,
    gw_ref,
    gcx_ref,
    gcbc_ref,
    gh_ref,
    d_state,
    pad_x,
    pad_bc,
    fut_x,
    fut_bc,
):
    width, states = cols["width"], cols["states"]
    rows = p_ref.shape[0]
    r_ref, halo_r_ref = p_ref.at[:, 2 * width :], halo_ref.at[:, 2 * width :]
    x0, q0, bc0, dt0 = cols["x"], cols["q"], cols["bc"], cols["dt"]
    dp_ref = da_ref.at[:, : 2 * width]
    dr_ref = da_ref.at[:, 2 * width :]
    first_step = pl.program_id(0) == 0

    @pl.when(first_step)
    def _():
        d_state[...] = jnp.zeros_like(d_state)
        gw_ref[...] = jnp.zeros_like(gw_ref)
        gcx_ref[...] = jnp.zeros_like(gcx_ref)
        gcbc_ref[...] = jnp.zeros_like(gcbc_ref)
        gh_ref[...] = jnp.zeros_like(gh_ref)
        fut_x[...] = jnp.zeros_like(fut_x)
        fut_bc[...] = jnp.zeros_like(fut_bc)

    aux = aux_ref[...]
    u_x = conv_rows(
        p_ref[:, x0 : x0 + width], halo_ref[:, x0 : x0 + width], pad_x, cx_ref, aux
    )
    sig_x = sigmoid(u_x)
    x_conv = u_x * sig_x
    u_bc = conv_rows(
        r_ref[:, bc0 : bc0 + 2 * states], halo_r_ref[:, bc0 : bc0 + 2 * states], pad_bc, cbc_ref, aux
    )
    sig_bc = sigmoid(u_bc)
    bc = (u_bc * sig_bc).astype(BF16)
    keys, query = bc[:, :states], bc[:, states:]
    lower = triangle(rows, False).astype(F32).astype(BF16)
    biased, step, log_decay, cum = head_scalars(r_ref[:, dt0 : dt0 + LANES], par_ref, lower)
    cum_t = cum.T
    last = cum[rows - 1 : rows, :]
    entering = jnp.exp(cum) * aux[:, 7:8]
    leaving = jnp.exp(last - cum) * aux[:, 8:9]
    wide = widen(jnp.concatenate([step, entering, leaving], axis=0), expand_ref)
    step_w, enter_w, leave_w = wide[:rows], wide[rows : 2 * rows], wide[2 * rows :]
    xs = x_conv * step_w
    xs_low = xs.astype(BF16)

    y = y_ref[...]
    z = p_ref[:, :width]
    sig_z = sigmoid(z)
    silu_z = z * sig_z
    gated = y * silu_z
    rstd = aux2_ref[:, 0:1]
    inner = aux2_ref[:, 1:2]
    d_mixed = db_ref[:, db_ref.shape[1] - width :]
    g_mgain = jnp.sum(d_mixed * (gated * rstd), axis=0, keepdims=True)
    d_gated = rstd * (d_mixed * mgain_ref[0:1, :]) - gated * inner
    d_y = d_gated * silu_z
    dp_ref[:, :width] = (d_gated * y * (sig_z * (1.0 + z * (1.0 - sig_z)))).astype(BF16)
    gw_ref[0:1, :] += g_mgain
    gw_ref[1:2, :] += jnp.sum(d_y * x_conv, axis=0, keepdims=True)

    dy_low = d_y.astype(BF16)
    held_low = st_ref[0]
    d_next = d_state[...]
    d_next_low = d_next.astype(BF16)
    entered_dy = (enter_w * d_y).astype(BF16)
    left_xs = (leave_w * xs).astype(BF16)
    from_next = leave_w * dot(keys, d_next_low)
    mask_t = triangle(rows, True) & (aux[:, 0:1] == segr_ref[0:1, :])
    b_dot_c = dot(keys, query, NT)
    lane = lax.broadcasted_iota(jnp.int32, (rows, LANES), 1)
    d_gram = jnp.zeros((rows, rows), F32)
    parts = []
    for pair in range(width // LANES):
        pair_dy = dy_low[:, pair * LANES : (pair + 1) * LANES]
        pair_x = xs_low[:, pair * LANES : (pair + 1) * LANES]
        none = jnp.zeros_like(pair_x)
        only = [jnp.where(lane < P_SIZE, pair_x, none), jnp.where(lane < P_SIZE, none, pair_x)]
        products = dot(jnp.concatenate(only, axis=0), pair_dy, NT)
        both = []
        for e, h in enumerate((2 * pair, 2 * pair + 1)):
            gap = cum_t[h : h + 1, :] - cum[:, h : h + 1]
            decay = jnp.exp(jnp.where(mask_t, gap, MASK_FILL))
            both.append((decay * b_dot_c).astype(BF16))
            d_gram = d_gram + decay * products[e * rows : (e + 1) * rows]
        both = dot(jnp.concatenate(both, axis=0), pair_dy)
        parts.append(jnp.where(lane < P_SIZE, both[:rows], both[rows:]))
    d_xs_inner = jnp.concatenate(parts, axis=1)
    d_xs = d_xs_inner + from_next
    d_gram = d_gram.astype(BF16)
    d_keys = dot(d_gram, query) + dot(left_xs, d_next_low, NT)
    d_query = dot(d_gram, keys, TN) + dot(entered_dy, held_low, NT)
    keep_w = enter_w[rows - 1 : rows, :]
    d_state[...] = dot(query, entered_dy, TN) + keep_w * d_next

    y_scan = y - dskip_ref[0:1, :] * x_conv
    pairs = dy_low.astype(F32) * y_scan - xs_low.astype(F32) * d_xs_inner
    d_cum = by_head(pairs - xs * from_next, reduce_ref)
    at_last = jnp.sum(xs * from_next, axis=0, keepdims=True) + keep_w * jnp.sum(
        held_low.astype(F32) * d_next, axis=0, keepdims=True
    )
    at_last = by_head(jnp.broadcast_to(at_last, (8, width)), reduce_ref)[0:1, :]
    d_log = sums_of(triangle(rows, True).astype(F32).astype(BF16), d_cum) + at_last
    d_step = by_head(x_conv * d_xs, reduce_ref) - d_log * jnp.exp(par_ref[0:1, :])
    d_dt = d_step * sigmoid(biased)
    dr_ref[:, dt0 : dt0 + LANES] = d_dt.astype(BF16)
    gh_ref[0:1, :] += jnp.sum(d_log * log_decay, axis=0, keepdims=True)
    gh_ref[1:2, :] += jnp.sum(d_dt, axis=0, keepdims=True)

    d_ux = (dskip_ref[0:1, :] * d_y + step_w * d_xs) * (sig_x * (1.0 + u_x * (1.0 - sig_x)))
    d_conv = jnp.concatenate([d_keys, d_query], axis=1)
    d_ubc = d_conv * (sig_bc * (1.0 + u_bc * (1.0 - sig_bc)))
    for grad, pad, fut, taps_ref, g_ref, d_ref, c0 in (
        (d_ux, pad_x, fut_x, cx_ref, gcx_ref, dp_ref, x0),
        (d_ubc, pad_bc, fut_bc, cbc_ref, gcbc_ref, dr_ref, bc0),
    ):
        size = grad.shape[1]
        g_ref[3:4, :] += jnp.sum(grad * pad[8 : 8 + rows, :], axis=0, keepdims=True)
        for k in range(1, 4):
            shifted = pad[8 - k : 8 - k + rows, :] * aux[:, k : k + 1]
            g_ref[3 - k : 4 - k, :] += jnp.sum(grad * shifted, axis=0, keepdims=True)
        fut[0:rows, :] = grad
        d_in = taps_ref[3:4, :] * grad
        for k in range(1, 4):
            d_in = d_in + taps_ref[3 - k : 4 - k, :] * (
                fut[k : k + rows, :] * aux[:, 3 + k : 4 + k]
            )
        fut[rows : rows + 8, :] = grad[0:8, :]
        d_ref[:, c0 : c0 + size] = d_in.astype(BF16)
    dr_ref[:, q0 : q0 + dqkv_ref.shape[1]] = dqkv_ref[...]


def head_maps(width):
    expand = (np.arange(width)[None, :] // P_SIZE == np.arange(LANES)[:, None]).astype(np.float32)
    return (
        jnp.asarray(np.concatenate([expand, expand], axis=0), BF16),
        jnp.asarray(expand.T, BF16),
    )


def mamba_specs(chunk, chunk_of, parts, members):
    def place(i):
        return chunk_place(chunk_of(i), parts, members)

    def rows(array):
        return pl.BlockSpec((chunk, array.shape[1]), lambda i: (place(i), 0))

    def fixed(array):
        return pl.BlockSpec(array.shape, lambda i: (0, 0))

    def before(i):
        earlier = chunk_place(jnp.maximum(chunk_of(i) - 1, 0), parts, members)
        return ((earlier + 1) * (chunk // 8) - 1, 0)

    def halo(array):
        return pl.BlockSpec((8, array.shape[1]), before)

    aux = pl.BlockSpec((chunk, LANES), lambda i: (chunk_of(i), 0))
    seg = pl.BlockSpec((8, chunk), lambda i: (0, chunk_of(i)))
    return rows, fixed, halo, aux, seg


def mamba_forward(cols, panel, aux, segr, cx, cbc, par, dskip, mgain, chunk, parts, members):
    length = panel.shape[0]
    width, states = cols["width"], cols["states"]
    chunks = length // chunk
    expand, _ = head_maps(width)
    rows, fixed, halo, by_aux, seg = mamba_specs(chunk, lambda i: i, parts, members)
    small = [cx, cbc, par, dskip, mgain, expand]
    shapes = [
        jax.ShapeDtypeStruct((length, width), BF16),
        jax.ShapeDtypeStruct((length, LANES), F32),
        jax.ShapeDtypeStruct((length, width), F32),
        jax.ShapeDtypeStruct((chunks, states, width), BF16),
    ]
    return pl.pallas_call(
        partial(mamba_forward_kernel, cols),
        grid=(chunks,),
        in_specs=[rows(panel), halo(panel), by_aux, seg] + [fixed(a) for a in small],
        out_specs=[
            rows(shapes[0]),
            rows(shapes[1]),
            rows(shapes[2]),
            pl.BlockSpec((1, states, width), lambda i: (i, 0, 0)),
        ],
        out_shape=shapes,
        scratch_shapes=[
            pltpu.VMEM((states, width), F32),
            pltpu.VMEM((chunk + 8, width), F32),
            pltpu.VMEM((chunk + 8, 2 * states), F32),
        ],
        compiler_params=pltpu.CompilerParams(vmem_limit_bytes=VMEM_LIMIT),
        cost_estimate=pl.CostEstimate(
            flops=20000 * length * width,
            bytes_accessed=4 * (panel.size + 3 * length * width),
            transcendentals=length * width * 4,
        ),
        name="mamba_forward",
    )(panel, panel, aux, segr, *small)


def mamba_backward(
    cols,
    panel,
    aux,
    segr,
    cx,
    cbc,
    par,
    dskip,
    mgain,
    y,
    held,
    d_branch_in,
    aux2,
    d_qkv,
    chunk,
    parts,
    members,
):
    length = panel.shape[0]
    width, states = cols["width"], cols["states"]
    chunks = length // chunk
    expand, reduce = head_maps(width)
    rows, fixed, halo, by_aux, seg = mamba_specs(
        chunk, lambda i: chunks - 1 - i, parts, members
    )
    small = [cx, cbc, par, dskip, mgain, expand, reduce]
    sums = [(8, width), (8, width), (8, 2 * states), (8, LANES)]
    whole = jax.ShapeDtypeStruct(panel.shape, BF16)
    return pl.pallas_call(
        partial(mamba_backward_kernel, cols),
        grid=(chunks,),
        in_specs=[rows(panel), halo(panel), by_aux, seg]
        + [fixed(a) for a in small]
        + [
            rows(y),
            pl.BlockSpec((1, states, width), lambda i: (chunks - 1 - i, 0, 0)),
            rows(d_branch_in),
            rows(aux2),
            rows(d_qkv),
        ],
        out_specs=[rows(whole)] + [pl.BlockSpec(s, lambda i: (0, 0)) for s in sums],
        out_shape=[whole]
        + [jax.ShapeDtypeStruct(s, F32) for s in sums],
        scratch_shapes=[
            pltpu.VMEM((states, width), F32),
            pltpu.VMEM((chunk + 8, width), F32),
            pltpu.VMEM((chunk + 8, 2 * states), F32),
            pltpu.VMEM((chunk + 8, width), F32),
            pltpu.VMEM((chunk + 8, 2 * states), F32),
        ],
        compiler_params=pltpu.CompilerParams(vmem_limit_bytes=VMEM_LIMIT),
        cost_estimate=pl.CostEstimate(
            flops=47000 * length * width,
            bytes_accessed=4 * (panel.size + 3 * length * width),
            transcendentals=length * width * 4,
        ),
        name="mamba_backward",
    )(panel, panel, aux, segr, *small, y, held, d_branch_in, aux2, d_qkv)


def pad_rows(value, rows):
    return jnp.pad(value, ((0, rows - value.shape[0]), (0, 0)))


def segment_tables(segment, chunk):
    length = segment.shape[0]
    seg = segment.astype(F32)
    columns = [seg]
    for k in range(1, 4):
        before = jnp.concatenate([jnp.full((k,), -1.0, F32), seg[:-k]])
        columns.append((before == seg).astype(F32))
    for k in range(1, 4):
        after = jnp.concatenate([seg[k:], jnp.full((k,), -1.0, F32)])
        columns.append((after == seg).astype(F32))
    blocks = seg.reshape(-1, chunk)
    ends = blocks[:, -1:]
    prior = jnp.concatenate([jnp.full((1, 1), -1.0, F32), ends[:-1]], axis=0)
    columns.append((blocks == prior).astype(F32).reshape(-1))
    columns.append((blocks == ends).astype(F32).reshape(-1))
    stacked = jnp.stack(columns + [jnp.zeros_like(seg)] * (16 - len(columns)), axis=0)
    return jnp.pad(stacked.T, ((0, 0), (0, LANES - 16))), jnp.broadcast_to(seg, (8, length))


def rms_factor(hidden):
    return lax.rsqrt(jnp.mean(hidden * hidden, axis=-1, keepdims=True) + NORM_EPS)


def norm_backward(hidden, gain, d_normed, grad_h):
    factor = rms_factor(hidden)
    weighted = gain * d_normed
    inner_mean = jnp.mean(weighted * hidden, axis=-1, keepdims=True)
    return grad_h + factor * weighted - hidden * factor**3 * inner_mean, factor


def after(value, *earlier):
    return lax.optimization_barrier((value, *earlier))[0]


def local(
    inputs,
    cotangent,
    seg_ids,
    norm_gains,
    w_q,
    key_value_weight,
    w_zx,
    w_bc,
    w_dt,
    a_log,
    dt_bias,
    d_skip,
    conv_x,
    conv_bc,
    m_gain,
    w_ao,
    w_mo,
    w_gu,
    w_down,
):
    members = lax.axis_size("dp")
    size_z = lax.axis_size("tensor")
    me_z = lax.axis_index("tensor")
    length = seg_ids.shape[1]
    count, model = inputs.shape[1:]
    block = model // members
    owned = key_value_weight.shape[1]
    heads = w_q.shape[2] // HEAD_SIZE
    kv_head = me_z * heads // (QUERY_HEADS // KEY_VALUE_HEADS)
    width = w_zx.shape[3]
    m_heads = w_dt.shape[2]
    states2 = w_bc.shape[2]
    hidden_units = w_gu.shape[3]
    taps = conv_bc.shape[2]
    gains_own = norm_gains.shape[2]
    cols = {"width": width, "states": states2 // 2, "x": width, "q": 0}
    cols["k"] = cols["q"] + heads * HEAD_SIZE
    cols["v"] = cols["k"] + HEAD_SIZE
    cols["bc"] = cols["v"] + HEAD_SIZE
    cols["dt"] = cols["bc"] + states2
    att_width = heads * HEAD_SIZE
    parts = 2 if count % 256 == 0 else 1
    sub = count // parts
    chunk = sub
    chunks = length // chunk
    late = parts - 1
    places = [(c % parts) * size_z + c // parts for c in range(chunks)]

    def split(value):
        return [value[h * sub : (h + 1) * sub] for h in range(parts)]

    def by_part(value):
        rows = size_z * sub
        return [value[h * rows : (h + 1) * rows] for h in range(parts)]

    lane_rows = 2 * KEY_VALUE_HEADS * HEAD_SIZE + states2
    shared = jnp.concatenate(
        [
            jnp.pad(norm_gains[0], ((0, 0), (0, lane_rows - gains_own))),
            jnp.pad(conv_bc[0], ((0, 10), (0, lane_rows - taps))),
            jnp.concatenate([key_value_weight[0], w_bc[0]], axis=1),
        ],
        axis=0,
    )
    def scatter_dp(value):
        return lax.psum_scatter(value, "dp", scatter_dimension=0, tiled=True)

    def gather_dp(value, *earlier):
        if earlier:
            value = after(value, *earlier)
        return lax.all_gather(value, "dp", axis=0, tiled=True)

    x_parts = split(inputs[0])
    shared = z_gather_direct(shared).reshape(size_z, 16 + owned, lane_rows)
    tiny = shared[:, :16]
    shared = shared[:, 16:].reshape(block, lane_rows)
    kv_cols = [
        lax.dynamic_slice_in_dim(shared, (base + kv_head) * HEAD_SIZE, HEAD_SIZE, 1)
        for base in (0, KEY_VALUE_HEADS)
    ]
    panel_rest = jnp.concatenate(
        [w_q[0]]
        + kv_cols
        + [
            shared[:, 2 * KEY_VALUE_HEADS * HEAD_SIZE :],
            jnp.pad(w_dt[0], ((0, 0), (0, LANES - m_heads))),
        ],
        axis=1,
    )
    rest_width = panel_rest.shape[1]
    tiny = jnp.concatenate(
        [
            jnp.swapaxes(tiny[:, :2, :gains_own], 0, 1).reshape(2, block),
            jnp.pad(
                jnp.swapaxes(tiny[:, 2:6, :taps], 0, 1).reshape(4, size_z * taps),
                ((0, 10), (0, block - size_z * taps)),
            ),
        ],
        axis=0,
    )
    panel_rows = jnp.concatenate([w_zx[0].reshape(block, 2 * width), panel_rest], axis=1)
    all_width = panel_rows.shape[1]
    tiny = jnp.pad(tiny, ((0, 0), (0, all_width - block)))
    panel_rows = jnp.concatenate([panel_rows, tiny], axis=0)
    w_all = gather_dp(panel_rows)
    x_moved = z_gather_parts(x_parts, in_turn=True)
    tiny = w_all.reshape(members, block + 16, all_width)[:, block:, :block].astype(F32)
    gains = jnp.swapaxes(tiny[:, :2], 0, 1).reshape(2, model)
    convbc_all = jnp.swapaxes(tiny[:, 2:6, : size_z * taps], 0, 1).reshape(4, states2)
    gain1, gain2 = gains[0:1], gains[1:2]
    w_b = gather_dp(jnp.concatenate([w_ao[0], w_mo[0]], axis=0).T, panel_rows)
    w_cd = jnp.concatenate([w_gu[0].reshape(block, 2 * hidden_units), w_down[0].T], axis=1)
    w_cd = gather_dp(w_cd, panel_rows)

    seg_own, a_own, dtb_own, dskip_own, cx_own, mgain_own = ordered(
        [seg_ids[0], a_log[0], dt_bias[0], d_skip[0], conv_x[0], m_gain[0]], panel_rows
    )
    aux, segr = segment_tables(seg_own, chunk)
    tables = [jnp.asarray(t) for t in rotary_rows(length)]
    cx = pad_rows(cx_own, 8)
    cbc = pad_rows(convbc_all, 8)
    par = jnp.pad(jnp.stack([a_own, dtb_own]), ((0, 6), (0, LANES - m_heads)))
    dskip = jnp.broadcast_to(jnp.repeat(dskip_own, P_SIZE)[None, :], (8, width))
    mgain = jnp.broadcast_to(mgain_own[None, :], (8, width))
    setup = (aux, segr, cx, cbc, par, dskip, mgain)

    held = ()
    d_moved = None
    for h in range(parts):
        pieces = x_moved[h]
        if h:
            pieces = pieces[:-1] + [ordered(pieces[-1], held[0])]
        x_all = z_place(x_parts[h], pieces)
        held = norm_project(x_all, gain1, w_all, held, h, parts, members)
        if d_moved is None:
            d_moved = z_gather_parts([after(cotangent[0], held[0])])[0]
    normed1, panel = held
    gm, squares, y_out, held = mamba_forward(cols, panel, *setup, chunk, parts, size_z)
    squares = z_sends(squares[:, 0].reshape(-1, LANES))
    attended = attention_call(
        attention_forward_kernel,
        "attention_forward",
        after(panel, y_out, *d_moved[0]),
        2 * width + cols["q"],
        heads,
        tables,
        aux,
        segr,
        None,
        att_width,
        [],
        places,
    )
    squares = sum(ordered(squares, attended)).reshape(length, 1)
    rstd = lax.rsqrt(squares / (HM * P_SIZE) + NORM_EPS)
    branch = branch_product(attended, gm, rstd, w_b, parts)
    sums, moved = z_scatter_parts(
        branch, {(0, 1): d_moved[min(1, size_z - 2)], (late, size_z - 2): d_moved[-1]}
    )
    x_own = after(inputs[0], *branch).astype(F32)
    h_mid, normed2_own = [], []
    for h, x in enumerate(split(x_own)):
        total = sums[h]
        if h:
            total = after(total, normed2_own[h - 1])
        h_mid.append(x + total)
        normed2_own.append((h_mid[h] * rms_factor(h_mid[h]) * gain2).astype(BF16))
    moved = z_gather_parts(normed2_own)
    d_out = [
        z_rotated(own, [[split(right)[h], split(left)[h]] for right, left in d_moved])
        for h, own in enumerate(split(cotangent[0]))
    ]
    normed2 = [z_rotated(own, m) for own, m in zip(normed2_own, moved)]
    act, d_gate, d_up = feed_forward(normed2, d_out, w_cd, hidden_units)
    d_norm2 = transposed_product([d_gate, d_up], w_cd, 0, parts)
    first = z_scatter_first(d_norm2)
    hooks = {(0, 1): [], (late, 1): []}
    given, g_cd, pieces = list(d_norm2), None, 2
    places_of = [(0, 1), (late, 1)]
    for piece in range(pieces):
        left, right = ordered((normed2, d_out), *given)
        g_cd, token = gradient(
            [left, right], [d_gate, d_up, act], [0, 0, 1], g_cd, piece, pieces
        )
        given = [*first, token]
        hooks[places_of[piece]].append(token)
    sums, moved = z_scatter_parts(d_norm2, hooks, first, True)
    g_cd = scatter_dp(g_cd)
    grad_mid, grad_low = [], []
    for h, part in enumerate(split(cotangent[0])):
        total = sums[h]
        if h:
            total = after(total, grad_low[h - 1])
        grad, _ = norm_backward(h_mid[h], gain2, total, part.astype(F32))
        grad_mid.append(grad)
        grad_low.append(grad.astype(BF16))
    h_mid_all = jnp.concatenate(h_mid, axis=0)
    moved = z_gather_parts(grad_low)
    ffn = transposed_product([after(act, *moved[0][0])], w_cd, 2, parts)
    ffn = [
        lax.dynamic_slice_in_dim(part, lax.rem(me_z - b + size_z, size_z) * sub, sub, 0)
        for b in range(size_z)
        for part in ffn
    ]
    ffn = jnp.concatenate(ffn, axis=0)
    d_branch = [z_place(own, m) for own, m in zip(grad_low, moved)]
    ffn = line_scatter([ffn], *moved[late][-1])[0]
    g_c, g_d = g_cd[:, : 2 * hidden_units], g_cd[:, 2 * hidden_units :]

    d_b, inner = branch_back(d_branch, w_b, gm)
    inner = z_sends(inner[:, 0].reshape(-1, LANES))
    d_qkv = attention_call(
        attention_backward_kernel,
        "attention_backward",
        after(panel, g_cd),
        2 * width + cols["q"],
        heads,
        tables,
        aux,
        segr,
        d_b,
        att_width + 2 * HEAD_SIZE,
        [pltpu.VMEM((length, HEAD_SIZE), F32), pltpu.VMEM((length, HEAD_SIZE), F32)],
        places,
    )
    inner = sum(ordered(inner, d_qkv)).reshape(length, 1)
    aux2 = jnp.pad(
        jnp.concatenate([rstd, rstd**3 * inner / (HM * P_SIZE)], axis=1),
        ((0, 0), (0, LANES - 2)),
    )
    d_all, g_wide, g_cx, g_cbc, g_heads = mamba_backward(
        cols, panel, *setup, y_out, held, d_b, aux2, d_qkv, chunk, parts, size_z
    )
    mixed = (after(gm, aux2).astype(F32) * rstd).astype(BF16)
    mixed = jnp.concatenate([attended, mixed], axis=1)
    g_all, _ = gradient([[normed1], d_branch], [d_all, mixed], [0, 1], None, 0, 1)
    d_norm1, low = [], g_all
    for h in range(parts):
        low = back_product(after(d_all, low), w_all, h, parts, members, model)
        d_norm1.append(low)
    g_all = scatter_dp(g_all)
    g_zx = g_all[:, : 2 * width].astype(F32)
    g_rest = g_all[:, 2 * width : all_width]
    g_b = g_all[:, all_width:].astype(F32)

    by_dp = [
        g_cbc[:4].reshape(-1, LANES),
        g_heads[0:2],
        jnp.pad(g_wide[1].reshape(m_heads, P_SIZE).sum(axis=1), (0, LANES - m_heads))[None],
        g_cx[:4].reshape(-1, LANES),
        g_wide[0].reshape(-1, LANES),
    ]
    ends = np.cumsum([v.shape[0] for v in by_dp])
    by_dp = jnp.concatenate(by_dp, axis=0)
    by_dp = pad_rows(by_dp, -(-by_dp.shape[0] // 8) * 8)
    by_dp = dp_sum(after(by_dp, *d_norm1))
    dp_taps = size_z * taps
    g_convbc = lax.dynamic_slice_in_dim(
        by_dp[: ends[0]].reshape(4, states2), lax.axis_index("dp") * dp_taps, dp_taps, 1
    )
    g_convbc = jnp.pad(
        g_convbc.T.reshape(size_z, taps, 4), ((0, 0), (0, owned - taps), (0, 0))
    ).reshape(block, 4)
    g_alog = by_dp[ends[0] : ends[0] + 1, :m_heads]
    g_dtbias = by_dp[ends[0] + 1 : ends[1], :m_heads]
    g_dskip = by_dp[ends[1] : ends[2], :m_heads]
    g_convx = by_dp[ends[2] : ends[3]].reshape(1, 4, width)
    g_mgain = by_dp[ends[3] : ends[4]].reshape(1, width)

    g_rest = g_rest.astype(F32)
    first = cols["q"]
    gain1_own = jnp.sum(panel_rest.astype(F32) * g_rest, axis=1) + jnp.sum(
        w_zx[0].reshape(block, 2 * width).astype(F32) * g_zx, axis=1
    )
    gain2_own = jnp.sum(
        w_gu[0].reshape(block, 2 * hidden_units).astype(F32) * g_c.astype(F32),
        axis=1,
    )
    mine = lax.axis_index("dp") * block
    gain1_own = gain1_own / lax.dynamic_slice_in_dim(gain1[0], mine, block, 0)
    gain2_own = gain2_own / lax.dynamic_slice_in_dim(gain2[0], mine, block, 0)
    small = jnp.concatenate([gain1_own[:, None], gain2_own[:, None], g_convbc], axis=1)
    g_q = g_rest[:, : cols["k"] - first]
    g_dt = g_rest[:, cols["dt"] - first : cols["dt"] - first + m_heads]
    kv_part = jnp.zeros((block, 2 * KEY_VALUE_HEADS * HEAD_SIZE), F32)
    for base, name in ((0, "k"), (KEY_VALUE_HEADS, "v")):
        at = cols[name] - first
        kv_part = lax.dynamic_update_slice_in_dim(
            kv_part, g_rest[:, at : at + HEAD_SIZE], (base + kv_head) * HEAD_SIZE, 1
        )
    kv_total = 2 * KEY_VALUE_HEADS * HEAD_SIZE
    shared_grad = jnp.concatenate(
        [
            kv_part,
            g_rest[:, cols["bc"] - first : cols["dt"] - first],
            jnp.pad(small, ((0, 0), (0, LANES - small.shape[1]))),
        ],
        axis=1,
    )
    hidden_out = (h_mid_all + ffn).astype(BF16)
    shared_grad = z_scatter_direct(shared_grad.astype(BF16))
    small = shared_grad[:, kv_total + states2 :]
    shared_grad = shared_grad[:, : kv_total + states2]
    g_gains = small[:, :2].T[None]
    g_convbc = small[:taps, 2:6].T[None]
    sums, moved = z_scatter_parts(d_norm1)
    norm_sum = jnp.concatenate(sums, axis=0)
    grad_in, _ = norm_backward(x_own, gain1, norm_sum, jnp.concatenate(grad_mid, axis=0))
    input_grad = grad_in

    return (
        hidden_out[None],
        input_grad[None],
        g_gains,
        g_q[None],
        shared_grad[None, :, :kv_total],
        g_zx.reshape(1, block, 2, width),
        shared_grad[None, :, kv_total:],
        g_dt[None],
        g_alog,
        g_dtbias,
        g_dskip,
        g_convx,
        g_convbc,
        g_mgain,
        g_b[:, :att_width].T[None],
        g_b[:, att_width:].T[None],
        g_c.astype(F32).reshape(1, block, 2, hidden_units),
        g_d.astype(F32).T[None],
    )


def solution(mesh):
    return jax.shard_map(
        local,
        mesh=mesh,
        in_specs=(
            P("dp", "tensor", None),
            P("dp", "tensor", None),
            P("dp", None),
            P(None, None, ("dp", "tensor")),
            P(None, "dp", "tensor"),
            P(None, ("dp", "tensor"), None),
            P(None, "dp", None, "tensor"),
            P(None, ("dp", "tensor"), None),
            P(None, "dp", "tensor"),
            P(None, "tensor"),
            P(None, "tensor"),
            P(None, "tensor"),
            P(None, None, "tensor"),
            P(None, None, ("dp", "tensor")),
            P(None, "tensor"),
            P(None, "tensor", "dp"),
            P(None, "tensor", "dp"),
            P(None, "dp", None, "tensor"),
            P(None, "tensor", "dp"),
        ),
        out_specs=(
            P("dp", "tensor", None),
            P("dp", "tensor", None),
            P(None, None, ("dp", "tensor")),
            P(None, "dp", "tensor"),
            P(None, ("dp", "tensor"), None),
            P(None, "dp", None, "tensor"),
            P(None, ("dp", "tensor"), None),
            P(None, "dp", "tensor"),
            P(None, "tensor"),
            P(None, "tensor"),
            P(None, "tensor"),
            P(None, None, "tensor"),
            P(None, None, ("dp", "tensor")),
            P(None, "tensor"),
            P(None, "tensor", "dp"),
            P(None, "tensor", "dp"),
            P(None, "dp", None, "tensor"),
            P(None, "tensor", "dp"),
        ),
        check_vma=False,
    )
```
